32 devices in a mesh: gx: 2 (over x), gy: 4 (over z), gz: 4 (over y, core).
Axes of the slice: x: 2, y: 2, z: 4, core: 2. Of those that a mesh axis runs over, the one named last changes fastest.
Arguments:
- field: float32 [16, 512, 1024], P('gz', 'gx', 'gy'), may hold values from -6 to 6
Outputs:
- coefficients: float32 [16, 512, 1024], P('gz', 'gx', 'gy')
- coarse_values: float32 [8, 256, 512], P('gz', 'gx', 'gy')
The draws below stay inside these ranges and needn't reach their ends.
All inputs are finite; a program needn't handle non-finite values.
Results may differ from the reference program's by a relative error of at most 0.00022.
Values sent between devices are 32-bit elements; how exact they have to be, the bound alone decides.
No kernel may reach another device: no remote copies, remote signals or barrier semaphores. Data moves between devices by JAX's collectives and lax.ppermute only.
A program may use at most 64 MiB of HBM per device.

```python
import jax
import jax.numpy as jnp
from jax import lax

NZ = 16
NX = 512
NY = 1024


def block_levels(key, dims, shards, low, high):
    gain, own = 1.0, jax.random.fold_in(key, 6)
    for axis_at, parts in shards:
        draws = jnp.exp(jax.random.uniform(jax.random.fold_in(own, axis_at), (parts,), jnp.float32, low / len(shards), high / len(shards)))
        gain = gain * jnp.repeat(draws, dims[axis_at] // parts).reshape([-1 if axis == axis_at else 1 for axis in range(len(dims))])
    return gain


def noise(own_key, extent, width, most, pieces=(), held_as=jnp.bfloat16):
    level = block_levels(own_key, extent, pieces, -0.22, 0.18) if pieces else 1.0
    drawn = jax.random.normal(own_key, extent, jnp.float32) * width * level
    return jnp.minimum(jnp.maximum(drawn, -most), most).astype(held_as)


def setup_inputs(seed: int = 0) -> dict:
    arg_keys = jax.random.split(jax.random.key(seed), 2)
    return {
        "field": noise(arg_keys[0], (NZ, NX, NY), 1.0, 6.0, ((0, 4), (1, 2), (2, 4)), jnp.float32),
    }


def lift(values, along):
    rotated = jnp.moveaxis(values, along, 0)
    length = rotated.shape[0]
    padded = jnp.pad(rotated, ((1, 1), (0, 0), (0, 0)))
    average = 0.5 * (padded[:-2] + padded[2:])
    is_odd = (jnp.arange(length) % 2 == 1)[:, None, None]
    return jnp.moveaxis(jnp.where(is_odd, average, rotated), 0, along)

def restrict(values, along):
    rotated = jnp.moveaxis(values, along, 0)
    length = rotated.shape[0]
    padded = jnp.pad(rotated, ((1, 1), (0, 0), (0, 0)))
    weighted = (padded[:-2] + 4.0 * padded[1:-1] + padded[2:]) / 6.0
    shifted = jnp.concatenate([jnp.zeros_like(weighted[:1]), weighted], axis=0)
    restricted = weighted[0::2] + 0.5 * (shifted[0:length:2] + weighted[1::2])
    return jnp.moveaxis(restricted, 0, along)

def solve_lines(loads, along):
    rotated = jnp.moveaxis(loads, along, 1)
    length = rotated.shape[1]
    position = jnp.arange(length)
    one_third = jnp.ones((length,), rotated.dtype) / 3.0
    below_diag = jnp.broadcast_to(jnp.where(position == 0, 0.0, one_third).astype(rotated.dtype), rotated.shape[:-1])
    above_diag = jnp.broadcast_to(jnp.where(position == length - 1, 0.0, one_third).astype(rotated.dtype), rotated.shape[:-1])
    middle = jnp.broadcast_to(4.0 * one_third, rotated.shape[:-1])
    solved = lax.linalg.tridiagonal_solve(below_diag, middle, above_diag, rotated)
    return jnp.moveaxis(solved, 1, along)

def reference(field):
    interpolant = lift(lift(lift(field, 1), 2), 0)
    coefficients = field - interpolant
    loads = restrict(restrict(restrict(coefficients, 1), 2), 0)
    correction = solve_lines(solve_lines(solve_lines(loads, 1), 2), 0)
    coarse_values = field[::2, ::2, ::2] + correction
    return (coefficients, coarse_values)
```

```python
import functools

import jax
import jax.numpy as jnp
import numpy as np
from jax import lax
from jax.experimental import pallas as pl
from jax.experimental.pallas import tpu as pltpu
from jax.sharding import PartitionSpec as P

RATIO = 2.0 - np.sqrt(3.0)
VMEM_LIMIT = 48 * 1024 * 1024


def inverse_mass(i, j, n):
    low, high = np.minimum(i, j), np.maximum(i, j)
    sign = np.where((high - low) % 2 == 0, 1.0, -1.0)
    value = RATIO ** (high - low + 1.0) * (1.0 - RATIO ** (2.0 * (low + 1))) * (1.0 - RATIO ** (2.0 * (n - high)))
    return 3.0 * sign * value / ((1.0 - RATIO**2) * (1.0 - RATIO ** (2.0 * (n + 1))))


def line_operator(i, k, n):
    a = k // 2
    odd = k % 2 == 1

    def at(j):
        inside = (j >= 0) & (j < n)
        return np.where(inside, inverse_mass(i, np.clip(j, 0, n - 1), n), 0.0)

    even_part = np.where(a == 0, 9.0, 10.0) * at(a) + at(a - 1) + at(a + 1)
    odd_part = 6.0 * at(a) + 6.0 * at(a + 1)
    return np.where(odd, odd_part, even_part) / 12.0


def line_tables(parts, m):
    n = parts * m
    node, fine = np.arange(m), np.arange(2 * m)
    block = np.zeros((parts, m, 2 * m))
    to_right, to_left = np.zeros((parts, 2 * m)), np.zeros((parts, 2 * m))
    from_left, from_right = np.zeros((parts, m)), np.zeros((parts, m))
    weight_left, weight_right = np.zeros((parts, parts)), np.zeros((parts, parts))
    first = np.zeros((parts, m))
    first_right = np.zeros((parts,))
    for p in range(parts):
        k = p * 2 * m + fine
        block[p] = line_operator((p * m + node)[:, None], k[None, :], n)
        if p + 1 < parts:
            to_right[p] = line_operator(np.full_like(k, (p + 1) * m), k, n)
        if p > 0:
            to_left[p] = line_operator(np.full_like(k, p * m - 1), k, n)
        from_left[p] = (-RATIO) ** node * (1 - RATIO ** (2.0 * (n - p * m - node))) / (1 - RATIO ** (2.0 * (n - p * m)))
        from_right[p] = (
            (-RATIO) ** (m - 1 - node) * (1 - RATIO ** (2.0 * (p * m + node + 1))) / (1 - RATIO ** (2.0 * (p + 1) * m))
        )
        for q in range(parts):
            if q < p:
                weight_left[p, q] = (
                    (-RATIO) ** ((p - q - 1) * m)
                    * (1 - RATIO ** (2.0 * (n - p * m)))
                    / (1 - RATIO ** (2.0 * (n - (q + 1) * m)))
                )
            if q > p:
                weight_right[p, q] = (
                    (-RATIO) ** ((q - p - 1) * m) * (1 - RATIO ** (2.0 * (p + 1) * m)) / (1 - RATIO ** (2.0 * q * m))
                )
    first[0] = inverse_mass(node, np.zeros_like(node), n) / 3.0
    if parts > 1:
        first_right[0] = -inverse_mass(np.array(m), np.array(0), n) / 3.0
    return {
        "block": block,
        "to_right": to_right,
        "to_left": to_left,
        "from_left": from_left,
        "from_right": from_right,
        "weight_left": weight_left,
        "weight_right": weight_right,
        "first": first,
        "first_right": first_right,
    }


def even_selector(m):
    pick = np.zeros((2 * m, m))
    pick[2 * np.arange(m), np.arange(m)] = 1.0
    return pick


def lift_matrix(m):
    up = np.zeros((2 * m, m + 1))
    up[2 * np.arange(m), np.arange(m)] = 1.0
    up[2 * np.arange(m) + 1, np.arange(m)] = 0.5
    up[2 * np.arange(m) + 1, np.arange(m) + 1] = 0.5
    return up


def f32(values):
    return np.asarray(values, np.float32)


def combine_tables(sizes, tx, ty, tz, mz):
    gx, gy, gz = sizes
    count = gx * gy * gz
    sender = np.arange(count)
    qx, qy, qz = sender // (gy * gz), (sender // gz) % gy, sender % gz
    rows = 32
    wx, wy, wz = (np.zeros((parts, rows, count, 4)) for parts in sizes)

    def side(t, p, q, which):
        if which == 0:
            return (q == p) * 1.0
        return (t["weight_left"] if which == 1 else t["weight_right"])[p][q]

    for sx in range(3):
        for sy in range(3):
            if sx == 0 and sy == 0:
                continue
            for z in range(mz):
                row = (sx * 3 + sy) * mz + z
                for p in range(gx):
                    wx[p, row] = side(tx, p, qx, sx)[:, None]
                for p in range(gy):
                    wy[p, row] = side(ty, p, qy, sy)[:, None]
                for p in range(gz):
                    wz[p, row, :, z] += qz == p
                    wz[p, row, :, 0] += tz["weight_left"][p][qz] * tz["from_left"][p, z]
                    wz[p, row, :, 0] += tz["weight_right"][p][qz] * tz["from_right"][p, z]
    for case, (ox, oy) in enumerate(((1, 0), (0, 1), (1, 1))):
        for layer in range(mz + 1):
            row = 9 * mz + case * (mz + 1) + layer
            for p in range(gx):
                wx[p, row] = (qx == p + ox)[:, None]
            for p in range(gy):
                wy[p, row] = (qy == p + oy)[:, None]
            for p in range(gz):
                if layer < mz:
                    wz[p, row, :, mz + layer] = qz == p
                else:
                    wz[p, row, :, mz] = qz == p + 1
    return tuple(f32(w.reshape(w.shape[0], rows, count * 4)) for w in (wx, wy, wz))


def dot(a, b, contract=((1,), (0,))):
    return lax.dot_general(
        a, b, (contract, ((), ())), precision=lax.Precision.HIGHEST, preferred_element_type=jnp.float32
    )


def start_all(copies):
    for copy in copies:
        copy.start()


def edges_kernel(
    sizes, scalars, field, row_x, row_y, right_y, right_x, send, f, ax, ay, ry, rx, kinds, sem
):
    gx, gy, gz = sizes
    px, py, pz = lax.axis_index("gx"), lax.axis_index("gy"), lax.axis_index("gz")
    depth = f.shape[0]
    planes = [pltpu.make_async_copy(field.at[z], f.at[z], sem.at[z]) for z in range(depth)]
    others = [
        pltpu.make_async_copy(row_x.at[px], ax, sem.at[depth]),
        pltpu.make_async_copy(row_y.at[py], ay, sem.at[depth + 1]),
        pltpu.make_async_copy(right_y.at[py], ry, sem.at[depth + 2]),
        pltpu.make_async_copy(right_x.at[px], rx, sem.at[depth + 3]),
    ]
    start_all(others[:2] + planes + others[2:])
    others[0].wait()
    others[1].wait()
    along_y, along_x = [], []
    for z in range(depth):
        planes[z].wait()
        along_y.append(dot(ax[0:8, :], f[z]))
        along_x.append(dot(ay[0:8, :], f[z], ((1,), (1,))))
    others[2].wait()
    others[3].wait()
    my, mx = ry.shape[1] // 4, rx.shape[1] // 2
    by_y = dot(jnp.concatenate(along_y, axis=0), ry[...])
    by_x = dot(jnp.concatenate(along_x, axis=0), rx[...])
    first_y, first_x = ay[8:9, :my], ax[8:9, :mx]
    kappa_x, kappa_y = scalars[gz, px], scalars[gz + 1, py]

    kinds[...] = jnp.zeros_like(kinds)
    mz = depth // 2
    for out in range(mz + 2):
        tile_y = sum(scalars[pz, out * depth + z] * by_y[8 * z : 8 * z + 8] for z in range(depth))
        tile_x = sum(scalars[pz, out * depth + z] * by_x[8 * z : 8 * z + 8] for z in range(depth))
        base = (mz + 2) * depth + out * mz
        first_row = sum(scalars[pz, base + j] * by_y[16 * j + 2 : 16 * j + 3, my : 2 * my] for j in range(mz))
        first_col = sum(scalars[pz, base + j] * by_x[16 * j + 2 : 16 * j + 3, mx:] for j in range(mz))
        corner = first_row[:, 0:1]
        lane = lax.broadcasted_iota(jnp.int32, (1, my), 1)
        chunks = {
            (1, 0): tile_y[0:1, :my] - kappa_x * (first_row - first_y * corner),
            (2, 0): tile_y[1:2, :my],
            (0, 1): tile_x[0:1, :mx] - kappa_y * (first_col - first_x * corner),
            (0, 2): tile_x[1:2, :mx],
            (1, 1): tile_y[0:1, 2 * my : 3 * my] - jnp.where(lane == 0, kappa_x * kappa_y * corner, 0.0),
            (1, 2): tile_y[0:1, 3 * my :],
            (2, 1): tile_y[1:2, 2 * my : 3 * my],
            (2, 2): tile_y[1:2, 3 * my :],
        }
        for (sx, sy), row in chunks.items():
            kind = (sx * 3 + sy) * 3
            if out < mz:
                kinds[kind, out : out + 1, :] = row
            else:
                kinds[kind + out - mz + 1, 0:1, :] = row
    for j in range(mz):
        row = by_y[16 * j + 2 : 16 * j + 3, my : 2 * my]
        col = by_x[16 * j + 2 : 16 * j + 3, mx:]
        for sx in range(3):
            for sy in range(3):
                for sz in range(3):
                    kinds[(sx * 3 + sy) * 3 + sz, mz + j : mz + j + 1, :] = col if sx == 0 else row

    def side(there, here):
        return jnp.where(there == here, 0, jnp.where(there > here, 1, 2))

    def scatter(tx, ty, tz, at):
        send[pl.ds(at, 1)] = kinds[pl.ds((side(tx, px) * 3 + side(ty, py)) * 3 + side(tz, pz), 1)]

    if gx * gy * gz <= 32:
        for at in range(gx * gy * gz):
            scatter(at // (gy * gz), (at // gz) % gy, at % gz, at)
    else:

        @pl.loop(0, gx * gy * gz)
        def _(at):
            scatter(at // (gy * gz), (at // gz) % gy, at % gz, at)


def bulk_kernel(sizes, hops, scalars, field, sx_all, sy_all, pick, row_x, row_y, own, even, *rest):
    gz = sizes[2]
    pays, (f, sx, sy, sel, ax, ay, picked, sem) = rest[: len(hops)], rest[len(hops) :]
    px, py, pz = lax.axis_index("gx"), lax.axis_index("gy"), lax.axis_index("gz")
    depth = f.shape[0]
    mz, mx, my = own.shape
    planes = [pltpu.make_async_copy(field.at[z], f.at[z], sem.at[z]) for z in range(depth)]
    others = [
        pltpu.make_async_copy(sx_all.at[px], sx, sem.at[depth]),
        pltpu.make_async_copy(sy_all.at[py], sy, sem.at[depth + 1]),
        pltpu.make_async_copy(pick, sel, sem.at[depth + 2]),
        pltpu.make_async_copy(row_x.at[px], ax, sem.at[depth + 3]),
        pltpu.make_async_copy(row_y.at[py], ay, sem.at[depth + 4]),
    ]
    start_all(others[:1] + planes + others[1:])
    others[0].wait()
    solved, evens = [], []
    for copy in others[1:]:
        copy.wait()
    for z in range(depth):
        planes[z].wait()
        solved.append(dot(dot(sx[...], f[z]), sy[...]))
        if z % 2 == 0:
            picked[z // 2] = dot(f[z], sel[...])
            evens.append(picked[z // 2, pl.ds(0, mx, stride=2), :])
    for j in range(mz):
        even[j] = evens[j]
    first_y = ay[8:9, :my]
    first_x = jnp.transpose(jnp.broadcast_to(ax[8:9, :mx], (8, mx)))[:, 0:1]
    outs = []
    for out in range(mz + 2):
        value = sum(scalars[pz, out * depth + z] * solved[z] for z in range(depth))
        base = (mz + 2) * depth + out * mz
        part = sum(scalars[pz, base + j] * evens[j] for j in range(mz))
        part = part - first_x * part[0:1, :]
        part = part - part[:, 0:1] * first_y
        outs.append(value - part)
    for j in range(mz):
        own[j] = evens[j] + outs[j]
    for pay, hop in zip(pays, hops, strict=True):
        right = (pz ^ hop) > pz
        pay[0] = jnp.where(right, outs[mz], outs[mz + 1])
        if pay.shape[0] > 1:
            pay[1] = evens[0]


def inner_kernel(hops, scalars, field, even, own, up_x, up_y, *rest):
    gets, (coefficients, coarse) = rest[: len(hops)], rest[len(hops) :]
    gz = lax.axis_size("gz")
    pz = lax.axis_index("gz")
    depth = field.shape[0]
    mz = even.shape[0]
    base = (mz + 2) * (depth + mz)
    ahead = jnp.zeros(even.shape[1:], jnp.float32)
    left, right = ahead, ahead
    for get, hop in zip(gets, hops, strict=True):
        q = pz ^ hop
        left = left + scalars[pz, base + q] * get[0]
        right = right + scalars[pz, base + gz + q] * get[0]
        if get.shape[0] > 1:
            ahead = ahead + jnp.where(q == pz + 1, 1.0, 0.0) * get[1]
    base = base + 2 * gz
    for j in range(mz):
        coarse[j] = own[j] + scalars[pz, base + j] * left + scalars[pz, base + mz + j] * right
    lifted = []
    for j in range(mz + 1):
        layer = even[j] if j < mz else ahead
        lifted.append(dot(dot(up_x[...], layer), up_y[...]))
    for j in range(mz):
        coefficients[2 * j] = field[2 * j] - lifted[j]
        coefficients[2 * j + 1] = field[2 * j + 1] - 0.5 * (lifted[j] + lifted[j + 1])


def finish_kernel(
    sizes, received, wx, wy, wz, row_x, row_y, up_y, up_x, inner, before, coefficients, coarse, w, ax, ay, c, sem
):
    px, py, pz = lax.axis_index("gx"), lax.axis_index("gy"), lax.axis_index("gz")
    mz, mx, my = coarse.shape
    depth = c.shape[0]
    copies = [
        pltpu.make_async_copy(wx.at[px], w.at[0], sem.at[0]),
        pltpu.make_async_copy(wy.at[py], w.at[1], sem.at[1]),
        pltpu.make_async_copy(wz.at[pz], w.at[2], sem.at[2]),
        pltpu.make_async_copy(row_x.at[px], ax, sem.at[3]),
        pltpu.make_async_copy(row_y.at[py], ay, sem.at[4]),
    ]
    fetch = pltpu.make_async_copy(inner, c, sem.at[5])
    start_all(copies + [fetch])
    for copy in copies:
        copy.wait()
    got = dot(w[0] * w[1] * w[2], received[...])
    ux, vx, uy, vy = ax[9:10, :mx], ax[10:11, :mx], ay[9:10, :my], ay[10:11, :my]

    def part(sx, sy, z):
        at = (sx * 3 + sy) * mz + z
        return got[at : at + 1]

    for z in range(mz):
        a, b = [], []
        for sy, end in ((1, uy), (2, vy)):
            a.append(part(0, sy, z) + ux * part(1, sy, z)[:, 0:1] + vx * part(2, sy, z)[:, 0:1])
            b.append(end)
        for sx, end in ((1, ux), (2, vx)):
            a.append(end)
            b.append(part(sx, 0, z))
        zero = jnp.zeros((4, mx), jnp.float32)
        coarse[z] = before[z] + dot(
            jnp.concatenate(a + [zero], axis=0), jnp.concatenate(b + [zero], axis=0), ((0,), (0,))
        )

    base = 9 * mz
    halo_x = got[base : base + mz + 1]
    halo_y = got[base + mz + 1 : base + 2 * (mz + 1)]
    halo_xy = got[base + 2 * (mz + 1) : base + 3 * (mz + 1)]
    lane = lax.broadcasted_iota(jnp.int32, (1, 2 * my), 1)
    last = jnp.where(lane == 2 * my - 1, 1.0, 0.0)
    pad = jnp.zeros((8 - mz - 1, halo_x.shape[1]), jnp.float32)
    row = dot(jnp.concatenate([halo_x, pad], axis=0), up_y[...])
    col = dot(jnp.concatenate([halo_y, pad], axis=0), up_x[...])
    fetch.wait()
    for z in range(depth):
        j = z // 2
        if z % 2 == 0:
            r, s, k = row[j : j + 1], col[j : j + 1], halo_xy[j : j + 1, 0:1]
        else:
            r = 0.5 * (row[j : j + 1] + row[j + 1 : j + 2])
            s = 0.5 * (col[j : j + 1] + col[j + 1 : j + 2])
            k = 0.5 * (halo_xy[j : j + 1, 0:1] + halo_xy[j + 1 : j + 2, 0:1])
        r = 0.5 * r + 0.25 * last * k
        s = jnp.concatenate([0.5 * s, jnp.zeros((7, 2 * mx), jnp.float32)], axis=0)
        e = jnp.concatenate([last, jnp.zeros((7, 2 * my), jnp.float32)], axis=0)
        c[z, :, my:] = c[z, :, my:] - dot(s, e[:, my:], ((0,), (0,)))
        c[z, 2 * mx - 1 : 2 * mx, :] = c[z, 2 * mx - 1 : 2 * mx, :] - r
    store = pltpu.make_async_copy(c, coefficients, sem.at[6])
    store.start()
    store.wait()


def params():
    return pltpu.CompilerParams(vmem_limit_bytes=VMEM_LIMIT)


ANY = pl.BlockSpec(memory_space=pl.ANY)
SMEM = pl.BlockSpec(memory_space=pltpu.SMEM)
VMEM = pl.BlockSpec(memory_space=pltpu.VMEM)


def on_device(sizes, field):
    gx, gy, gz = sizes
    depth, height, breadth = field.shape
    mz, mx, my = depth // 2, height // 2, breadth // 2
    count = gx * gy * gz
    axes = ("gx", "gy", "gz")
    tx, ty, tz = line_tables(gx, mx), line_tables(gy, my), line_tables(gz, mz)

    def rows(t, parts, m):
        table = np.zeros((parts, 16, 2 * m))
        table[:, 0], table[:, 1], table[:, 2, 0] = t["to_right"], t["to_left"], 1.0
        table[:, 8, :m], table[:, 9, :m], table[:, 10, :m] = t["first"], t["from_left"], t["from_right"]
        return f32(table)

    row_x, row_y = rows(tx, gx, mx), rows(ty, gy, my)
    right_y = np.zeros((gy, 2 * my, 4 * my))
    right_y[:, :, :my] = t_block = ty["block"].transpose(0, 2, 1)
    right_y[:, :, my : 2 * my] = even_selector(my)
    right_y[:, :, 2 * my], right_y[:, :, 3 * my] = ty["to_right"], ty["to_left"]
    right_x = np.zeros((gx, 2 * mx, 2 * mx))
    right_x[:, :, :mx] = tx["block"].transpose(0, 2, 1)
    right_x[:, :, mx:] = even_selector(mx)

    width = max((mz + 2) * (depth + mz) + 2 * gz + 2 * mz, gx, gy)
    scalars = np.zeros((gz + 2, width))
    for p in range(gz):
        full = np.concatenate([tz["block"][p], tz["to_right"][p : p + 1], tz["to_left"][p : p + 1]], axis=0)
        nodes = np.zeros((mz + 2, mz))
        nodes[:mz] = np.eye(mz)
        nodes[:mz, 0] -= tz["first"][p]
        nodes[mz, 0] = tz["first_right"][p]
        line = np.concatenate(
            [
                full.reshape(-1),
                nodes.reshape(-1),
                tz["weight_left"][p],
                tz["weight_right"][p],
                tz["from_left"][p],
                tz["from_right"][p],
            ]
        )
        scalars[p, : line.size] = line
    scalars[gz, :gx], scalars[gz + 1, :gy] = tx["first_right"], ty["first_right"]
    scalars = f32(scalars)

    vmem = pltpu.VMEM
    send = pl.pallas_call(
        functools.partial(edges_kernel, sizes),
        out_shape=jax.ShapeDtypeStruct((count, 4, my), jnp.float32),
        in_specs=[SMEM] + [ANY] * 5,
        out_specs=VMEM,
        scratch_shapes=[
            vmem(field.shape, jnp.float32),
            vmem((16, 2 * mx), jnp.float32),
            vmem((16, 2 * my), jnp.float32),
            vmem((2 * my, 4 * my), jnp.float32),
            vmem((2 * mx, 2 * mx), jnp.float32),
            vmem((27, 4, my), jnp.float32),
            pltpu.SemaphoreType.DMA((depth + 4,)),
        ],
        compiler_params=params(),
        name="edges",
    )(scalars, field, row_x, row_y, f32(right_y), f32(right_x))
    received = lax.all_to_all(send, axes, 0, 0, tiled=True).reshape(count * 4, my)

    hops = tuple(range(1, gz))
    plane = (mx, my)
    pay_shapes = [jax.ShapeDtypeStruct((2 if hop & (hop + 1) == 0 else 1, *plane), jnp.float32) for hop in hops]
    own, even, *pays = pl.pallas_call(
        functools.partial(bulk_kernel, sizes, hops),
        out_shape=[jax.ShapeDtypeStruct((mz, *plane), jnp.float32)] * 2 + pay_shapes,
        in_specs=[SMEM] + [ANY] * 6,
        out_specs=[VMEM] * (2 + len(hops)),
        scratch_shapes=[
            vmem(field.shape, jnp.float32),
            vmem((mx, 2 * mx), jnp.float32),
            vmem((2 * my, my), jnp.float32),
            vmem((2 * my, my), jnp.float32),
            vmem((16, 2 * mx), jnp.float32),
            vmem((16, 2 * my), jnp.float32),
            vmem((mz, 2 * mx, my), jnp.float32),
            pltpu.SemaphoreType.DMA((depth + 5,)),
        ],
        compiler_params=params(),
        name="bulk",
    )(scalars, field, f32(tx["block"]), f32(t_block), f32(even_selector(my)), row_x, row_y)
    gets = [lax.ppermute(pay, "gz", [(i, i ^ hop) for i in range(gz)]) for pay, hop in zip(pays, hops, strict=True)]

    up_x, up_y = lift_matrix(mx)[:, :mx], lift_matrix(my)[:, :my].T
    inner, before = pl.pallas_call(
        functools.partial(inner_kernel, hops),
        out_shape=[jax.ShapeDtypeStruct(field.shape, jnp.float32), jax.ShapeDtypeStruct(own.shape, jnp.float32)],
        in_specs=[SMEM] + [VMEM] * (5 + len(hops)),
        out_specs=[VMEM] * 2,
        compiler_params=params(),
        name="inner",
    )(scalars, field, even, own, f32(up_x), f32(up_y), *gets)

    wx, wy, wz = combine_tables(sizes, tx, ty, tz, mz)
    return pl.pallas_call(
        functools.partial(finish_kernel, sizes),
        out_shape=[jax.ShapeDtypeStruct(field.shape, jnp.float32), jax.ShapeDtypeStruct(own.shape, jnp.float32)],
        in_specs=[VMEM] + [ANY] * 5 + [VMEM, VMEM, ANY, VMEM],
        out_specs=[ANY, VMEM],
        scratch_shapes=[
            vmem((3, wx.shape[1], count * 4), jnp.float32),
            vmem((16, 2 * mx), jnp.float32),
            vmem((16, 2 * my), jnp.float32),
            vmem(field.shape, jnp.float32),
            pltpu.SemaphoreType.DMA((7,)),
        ],
        compiler_params=params(),
        name="finish",
    )(received, wx, wy, wz, row_x, row_y, f32(up_y), f32(up_x.T), inner, before)


def solution(mesh):
    sizes = tuple(mesh.shape[axis] for axis in ("gx", "gy", "gz"))
    return jax.shard_map(
        functools.partial(on_device, sizes),
        mesh=mesh,
        in_specs=(P("gz", "gx", "gy"),),
        out_specs=(P("gz", "gx", "gy"), P("gz", "gx", "gy")),
        check_vma=False,
    )
```

```python
import functools

import jax
import jax.numpy as jnp
import numpy as np
from jax import lax
from jax.experimental import pallas as pl
from jax.experimental.pallas import tpu as pltpu
from jax.sharding import PartitionSpec as P

RATIO = 2.0 - np.sqrt(3.0)
VMEM_LIMIT = 48 * 1024 * 1024


def inverse_mass(i, j, n):
    low, high = np.minimum(i, j), np.maximum(i, j)
    sign = np.where((high - low) % 2 == 0, 1.0, -1.0)
    value = RATIO ** (high - low + 1.0) * (1.0 - RATIO ** (2.0 * (low + 1))) * (1.0 - RATIO ** (2.0 * (n - high)))
    return 3.0 * sign * value / ((1.0 - RATIO**2) * (1.0 - RATIO ** (2.0 * (n + 1))))


def line_operator(i, k, n):
    a = k // 2
    odd = k % 2 == 1

    def at(j):
        inside = (j >= 0) & (j < n)
        return np.where(inside, inverse_mass(i, np.clip(j, 0, n - 1), n), 0.0)

    even_part = np.where(a == 0, 9.0, 10.0) * at(a) + at(a - 1) + at(a + 1)
    odd_part = 6.0 * at(a) + 6.0 * at(a + 1)
    return np.where(odd, odd_part, even_part) / 12.0


def line_tables(parts, m):
    n = parts * m
    node, fine = np.arange(m), np.arange(2 * m)
    block = np.zeros((parts, m, 2 * m))
    to_right, to_left = np.zeros((parts, 2 * m)), np.zeros((parts, 2 * m))
    from_left, from_right = np.zeros((parts, m)), np.zeros((parts, m))
    weight_left, weight_right = np.zeros((parts, parts)), np.zeros((parts, parts))
    first = np.zeros((parts, m))
    first_right = np.zeros((parts,))
    for p in range(parts):
        k = p * 2 * m + fine
        block[p] = line_operator((p * m + node)[:, None], k[None, :], n)
        if p + 1 < parts:
            to_right[p] = line_operator(np.full_like(k, (p + 1) * m), k, n)
        if p > 0:
            to_left[p] = line_operator(np.full_like(k, p * m - 1), k, n)
        from_left[p] = (-RATIO) ** node * (1 - RATIO ** (2.0 * (n - p * m - node))) / (1 - RATIO ** (2.0 * (n - p * m)))
        from_right[p] = (
            (-RATIO) ** (m - 1 - node) * (1 - RATIO ** (2.0 * (p * m + node + 1))) / (1 - RATIO ** (2.0 * (p + 1) * m))
        )
        for q in range(parts):
            if q < p:
                weight_left[p, q] = (
                    (-RATIO) ** ((p - q - 1) * m)
                    * (1 - RATIO ** (2.0 * (n - p * m)))
                    / (1 - RATIO ** (2.0 * (n - (q + 1) * m)))
                )
            if q > p:
                weight_right[p, q] = (
                    (-RATIO) ** ((q - p - 1) * m) * (1 - RATIO ** (2.0 * (p + 1) * m)) / (1 - RATIO ** (2.0 * q * m))
                )
    first[0] = inverse_mass(node, np.zeros_like(node), n) / 3.0
    if parts > 1:
        first_right[0] = -inverse_mass(np.array(m), np.array(0), n) / 3.0
    return {
        "block": block,
        "to_right": to_right,
        "to_left": to_left,
        "from_left": from_left,
        "from_right": from_right,
        "weight_left": weight_left,
        "weight_right": weight_right,
        "first": first,
        "first_right": first_right,
    }


def even_selector(m):
    pick = np.zeros((2 * m, m))
    pick[2 * np.arange(m), np.arange(m)] = 1.0
    return pick


def lift_matrix(m):
    up = np.zeros((2 * m, m + 1))
    up[2 * np.arange(m), np.arange(m)] = 1.0
    up[2 * np.arange(m) + 1, np.arange(m)] = 0.5
    up[2 * np.arange(m) + 1, np.arange(m) + 1] = 0.5
    return up


def f32(values):
    return np.asarray(values, np.float32)


def combine_tables(sizes, tx, ty, tz, mz):
    gx, gy, gz = sizes
    count = gx * gy * gz
    sender = np.arange(count)
    qx, qy, qz = sender // (gy * gz), (sender // gz) % gy, sender % gz
    rows = 32
    wx, wy, wz = (np.zeros((parts, rows, count, 4)) for parts in sizes)

    def side(t, p, q, which):
        if which == 0:
            return (q == p) * 1.0
        return (t["weight_left"] if which == 1 else t["weight_right"])[p][q]

    for sx in range(3):
        for sy in range(3):
            if sx == 0 and sy == 0:
                continue
            for z in range(mz):
                row = (sx * 3 + sy) * mz + z
                for p in range(gx):
                    wx[p, row] = side(tx, p, qx, sx)[:, None]
                for p in range(gy):
                    wy[p, row] = side(ty, p, qy, sy)[:, None]
                for p in range(gz):
                    wz[p, row, :, z] += qz == p
                    wz[p, row, :, 0] += tz["weight_left"][p][qz] * tz["from_left"][p, z]
                    wz[p, row, :, 0] += tz["weight_right"][p][qz] * tz["from_right"][p, z]
    for case, (ox, oy) in enumerate(((1, 0), (0, 1), (1, 1))):
        for layer in range(mz + 1):
            row = 9 * mz + case * (mz + 1) + layer
            for p in range(gx):
                wx[p, row] = (qx == p + ox)[:, None]
            for p in range(gy):
                wy[p, row] = (qy == p + oy)[:, None]
            for p in range(gz):
                if layer < mz:
                    wz[p, row, :, mz + layer] = qz == p
                else:
                    wz[p, row, :, mz] = qz == p + 1
    return tuple(f32(w.reshape(w.shape[0], rows, count * 4)) for w in (wx, wy, wz))


def split(values):
    high = values.astype(jnp.bfloat16)
    return high, (values - high.astype(jnp.float32)).astype(jnp.bfloat16)


def one_pass(a, b, contract=((1,), (0,))):
    return lax.dot_general(a, b, (contract, ((), ())), preferred_element_type=jnp.float32)


def three_pass(a, b, contract=((1,), (0,))):
    return one_pass(a[0], b[0], contract) + one_pass(a[0], b[1], contract) + one_pass(a[1], b[0], contract)


def exact_left(a, b):
    high, low = split(b)
    return one_pass(a, high) + one_pass(a, low)


def split_exact(values):
    return values.astype(jnp.bfloat16)


def exact_right(a, b):
    high, low = split(a)
    return one_pass(high, b) + one_pass(low, b)


def start_all(copies):
    for copy in copies:
        copy.start()


def local_kernel(sizes, *refs):
    numbers, field, sum_x, sum_y, fold_z, row_y, row_x, line_y, line_x, block_x, pick = refs[:11]
    send, own, even, near, far, first = refs[11:17]
    f, ax, ay, az, vy, vx, ry, rx, bx, sel, kinds, scalars, sem = refs[17:]
    gx, gy, gz = sizes
    px, py, pz = lax.axis_index("gx"), lax.axis_index("gy"), lax.axis_index("gz")
    depth, height, _ = field.shape
    mz, mx, my = own.shape
    planes = []
    for z in range(depth):
        halves = [
            pltpu.make_async_copy(field.at[z, :, pl.ds(h * my, my)], f.at[h, z], sem.at[2 * z + h]) for h in range(2)
        ]
        planes.append(halves)
    sources = [(line_y.at[py], ry), (sum_y.at[py], ay), (fold_z.at[pz], az), (sum_x.at[px], ax), (numbers, scalars)]
    sources += [(row_y.at[py], vy), (row_x.at[px], vx), (block_x.at[px], bx), (pick, sel), (line_x.at[px], rx)]
    tables = [pltpu.make_async_copy(src, dst, sem.at[2 * depth + i]) for i, (src, dst) in enumerate(sources)]
    start_all(tables[:3] + planes[0] + planes[1] + tables[3:] + planes[2] + planes[3])
    for table in tables[:3]:
        table.wait()
    kinds[...] = jnp.zeros_like(kinds)
    solve_y = split(ry[...])
    by_y, along_x = [], None
    for z in range(depth):
        sum_z = split(ay[...] * az[z : z + 1, :])
        weights = tuple(jnp.concatenate([a, b], axis=1) for a, b in zip(solve_y, sum_z, strict=True))
        for half in planes[z]:
            half.wait()
        both = three_pass(split(jnp.concatenate([f[0, z], f[1, z]], axis=1)), weights)
        by_y.append(both[:, :my])
        along_x = both[:, my:] if along_x is None else along_x + both[:, my:]
    for table in tables[3:]:
        table.wait()

    by_x = three_pass(split(jnp.transpose(along_x)[:16, :]), split(rx[...]))
    sums = [[jnp.sum(by_y[z] * ax[ab], axis=0, keepdims=True) for ab in range(2)] for z in range(depth)]
    corners = [jnp.sum(along_x * ax[ab], axis=0, keepdims=True) for ab in range(2)]
    pick_y = split_exact(sel[...])
    evens = []
    for j in range(mz):
        rows = jnp.concatenate([f[h, 2 * j, pl.ds(0, mx, stride=2), :] for h in range(2)], axis=1)
        evens.append(exact_right(rows, pick_y))
        even[j] = evens[j]
    first_y, first_x = vy[8:9, :my], vx[8:9, :mx]
    kappa_x, kappa_y = scalars[gz, px], scalars[gz + 1, py]
    ends = 2 * (mz + 2)
    first_rows = [evens[j][0:1, :] for j in range(mz)]
    first_cols = [by_x[ends + j : ends + j + 1, mx:] for j in range(mz)]
    for out in range(mz + 2):
        base = (mz + 2) * depth + out * mz
        first_row = sum(scalars[pz, base + j] * first_rows[j] for j in range(mz))
        first_col = sum(scalars[pz, base + j] * first_cols[j] for j in range(mz))
        corner = first_row[:, 0:1]
        right_row, left_row = (sum(scalars[pz, out * depth + z] * sums[z][ab] for z in range(depth)) for ab in range(2))
        r, l = slice(2 * out, 2 * out + 1), slice(2 * out + 1, 2 * out + 2)
        spread = jnp.zeros((1, my), jnp.float32)
        chunks = {
            (1, 0): right_row - kappa_x * (first_row - first_y * corner),
            (2, 0): left_row,
            (0, 1): by_x[r, :mx] - kappa_y * (first_col - first_x * corner),
            (0, 2): by_x[l, :mx],
            (1, 1): spread + (corners[0][:, r] - kappa_x * kappa_y * corner),
            (1, 2): spread + corners[0][:, l],
            (2, 1): spread + corners[1][:, r],
            (2, 2): spread + corners[1][:, l],
        }
        for (sx, sy), row in chunks.items():
            kind = (sx * 3 + sy) * 3
            if out < mz:
                kinds[kind, out : out + 1, :] = row
            else:
                kinds[kind + out - mz + 1, 0:1, :] = row
    for sx in range(3):
        for sy in range(3):
            halo = jnp.concatenate(first_cols if sx == 0 else first_rows, axis=0)
            for sz in range(3):
                kinds[(sx * 3 + sy) * 3 + sz, mz : 2 * mz, :] = halo

    def side(there, here):
        return jnp.where(there == here, 0, jnp.where(there > here, 1, 2))

    def scatter(tx, ty, tz, at):
        send[pl.ds(at, 1)] = kinds[pl.ds((side(tx, px) * 3 + side(ty, py)) * 3 + side(tz, pz), 1)]

    if gx * gy * gz <= 32:
        for at in range(gx * gy * gz):
            scatter(at // (gy * gz), (at // gz) % gy, at % gz, at)
    else:

        @pl.loop(0, gx * gy * gz)
        def _(at):
            scatter(at // (gy * gz), (at // gz) % gy, at % gz, at)

    solve_x = split(bx[...])
    solved = [three_pass(solve_x, split(by_y[z])) for z in range(depth)]
    first_x = jnp.transpose(jnp.broadcast_to(first_x, (8, mx)))[:, 0:1]
    outs = []
    for out in range(mz + 2):
        value = sum(scalars[pz, out * depth + z] * solved[z] for z in range(depth))
        base = (mz + 2) * depth + out * mz
        part = sum(scalars[pz, base + j] * evens[j] for j in range(mz))
        part = part - first_x * part[0:1, :]
        part = part - part[:, 0:1] * first_y
        outs.append(value - part)
    for j in range(mz):
        own[j] = evens[j] + outs[j]
    near[...] = jnp.where(pz % 2 == 0, outs[mz], outs[mz + 1])
    far[...] = jnp.where(pz % 4 < 2, outs[mz], outs[mz + 1])
    first[...] = evens[0]


def inner_kernel(field, even, up_x, up_y, c, top):
    depth = field.shape[0]
    mz = even.shape[0]
    up_x, up_y = up_x[...].astype(jnp.bfloat16), up_y[...].astype(jnp.bfloat16)
    lifted = [exact_right(exact_left(up_x, even[j]), up_y) for j in range(mz)]
    for z in range(depth - 1):
        j = z // 2
        c[z] = field[z] - (lifted[j] if z % 2 == 0 else 0.5 * (lifted[j] + lifted[j + 1]))
    top[...] = field[depth - 1] - 0.5 * lifted[mz - 1]


def upper_kernel(scalars, top, own, up_x, up_y, one, two, three, first_one, first_three, last, coarse):
    gz = lax.axis_size("gz")
    pz = lax.axis_index("gz")
    mz = own.shape[0]
    base = (mz + 2) * (2 * mz + mz)
    left, right = jnp.zeros(own.shape[1:], jnp.float32), jnp.zeros(own.shape[1:], jnp.float32)
    for plane, hop in ((one, 1), (two, 2), (three, 3)):
        left = left + scalars[pz, base + (pz ^ hop)] * plane[...]
        right = right + scalars[pz, base + gz + (pz ^ hop)] * plane[...]
    ahead = jnp.where(pz ^ 1 == pz + 1, 1.0, 0.0) * first_one[...]
    ahead = ahead + jnp.where(pz ^ 3 == pz + 1, 1.0, 0.0) * first_three[...]
    up_x, up_y = up_x[...].astype(jnp.bfloat16), up_y[...].astype(jnp.bfloat16)
    last[...] = top[...] - 0.5 * exact_right(exact_left(up_x, ahead), up_y)
    base = base + 2 * gz
    for j in range(mz):
        coarse[j] = own[j] + scalars[pz, base + j] * left + scalars[pz, base + mz + j] * right


def finish_kernel(
    sizes,
    received,
    wx,
    wy,
    wz,
    row_x,
    row_y,
    up_x,
    up_y,
    inner,
    top,
    before,
    coefficients,
    coarse,
    rim,
    foot,
    values,
    sem,
):
    px, py, pz = lax.axis_index("gx"), lax.axis_index("gy"), lax.axis_index("gz")
    mz, mx, my = before.shape
    depth, height, breadth = 2 * mz, 2 * mx, 2 * my
    split_at = breadth - 128
    body = (pl.ds(0, height - 8), pl.ds(0, split_at))
    copies = [
        pltpu.make_async_copy(inner.at[:, *body], coefficients.at[pl.ds(0, depth - 1), *body], sem.at[0]),
        pltpu.make_async_copy(top.at[body], coefficients.at[depth - 1, *body], sem.at[1]),
    ]
    start_all(copies)
    weights = wx[px] * wy[py] * wz[pz]
    got = three_pass(split(weights), split(received[...]))

    base = 9 * mz
    layers = mz + 1
    halo_x, halo_y, halo_xy = (got[base + i * layers : base + (i + 1) * layers] for i in range(3))
    pad = jnp.zeros((8 - layers, halo_x.shape[1]), jnp.float32)
    row = exact_right(jnp.concatenate([halo_x, pad], axis=0), up_y[...].astype(jnp.bfloat16))
    tall = jnp.concatenate([halo_y, jnp.zeros((128 - layers, halo_y.shape[1]), jnp.float32)], axis=0)
    col = exact_left(up_x[...].astype(jnp.bfloat16), jnp.transpose(tall))
    lane = lax.broadcasted_iota(jnp.int32, (1, 128), 1)
    last = lane == 127
    for z in range(depth):
        j = z // 2
        if z % 2 == 0:
            r, s, k = row[j : j + 1], 0.5 * col[:, j : j + 1], halo_xy[j : j + 1, 0:1]
        else:
            r = 0.5 * (row[j : j + 1] + row[j + 1 : j + 2])
            s = 0.25 * (col[:, j : j + 1] + col[:, j + 1 : j + 2])
            k = 0.5 * (halo_xy[j : j + 1, 0:1] + halo_xy[j + 1 : j + 2, 0:1])
        old = inner[z] if z < depth - 1 else top[...]
        rim[z] = old[:, split_at:] - jnp.where(last, s, 0.0)
        end = 0.5 * r[:, split_at:] + jnp.where(last, 0.25 * k, 0.0)
        rim[z, height - 1 : height, :] = rim[z, height - 1 : height, :] - end
        foot[z] = old[height - 8 :, :split_at]
        foot[z, 7:8, :] = old[height - 1 :, :split_at] - 0.5 * r[:, :split_at]
    copies.append(pltpu.make_async_copy(rim, coefficients.at[:, :, pl.ds(split_at, 128)], sem.at[2]))
    copies.append(pltpu.make_async_copy(foot, coefficients.at[:, pl.ds(height - 8, 8), pl.ds(0, split_at)], sem.at[3]))
    start_all(copies[2:])

    ux, vx = row_x[px, 9:10, :mx], row_x[px, 10:11, :mx]
    uy, vy = row_y[py, 9:10, :my], row_y[py, 10:11, :my]

    def part(sx, sy, z):
        at = (sx * 3 + sy) * mz + z
        return got[at : at + 1]

    for z in range(mz):
        a, b = [], []
        for sy, end in ((1, uy), (2, vy)):
            a.append(part(0, sy, z) + ux * part(1, sy, z)[:, 0:1] + vx * part(2, sy, z)[:, 0:1])
            b.append(end)
        for sx, end in ((1, ux), (2, vx)):
            a.append(end)
            b.append(part(sx, 0, z))
        zero = [jnp.zeros((4, mx), jnp.float32)]
        a, b = split(jnp.concatenate(a + zero, axis=0)), split(jnp.concatenate(b + zero, axis=0))
        values[z] = before[z] + three_pass(a, b, ((0,), (0,)))
    copies.append(pltpu.make_async_copy(values, coarse, sem.at[4]))
    copies[4].start()
    for copy in copies:
        copy.wait()


def call(kernel, name, out_shape, in_specs, out_specs, scratch=(), aliases=None, flops=1, size=1):
    return pl.pallas_call(
        kernel,
        out_shape=out_shape,
        in_specs=in_specs,
        out_specs=out_specs,
        scratch_shapes=list(scratch),
        input_output_aliases=aliases or {},
        compiler_params=pltpu.CompilerParams(vmem_limit_bytes=VMEM_LIMIT),
        cost_estimate=pl.CostEstimate(flops=flops, bytes_accessed=size, transcendentals=0),
        name=name,
    )


ANY = pl.BlockSpec(memory_space=pl.ANY)
HBM = pl.BlockSpec(memory_space=pltpu.HBM)
SMEM = pl.BlockSpec(memory_space=pltpu.SMEM)
VMEM = pl.BlockSpec(memory_space=pltpu.VMEM)


def shape(*dims):
    return jax.ShapeDtypeStruct(dims, jnp.float32)


def on_device(sizes, field):
    gx, gy, gz = sizes
    depth, height, breadth = field.shape
    mz, mx, my = depth // 2, height // 2, breadth // 2
    count = gx * gy * gz
    axes = ("gx", "gy", "gz")
    tx, ty, tz = line_tables(gx, mx), line_tables(gy, my), line_tables(gz, mz)

    def rows(t, parts, m):
        table = np.zeros((parts, 16, 2 * m))
        table[:, 0], table[:, 1] = t["to_right"], t["to_left"]
        table[:, 8, :m], table[:, 9, :m], table[:, 10, :m] = t["first"], t["from_left"], t["from_right"]
        return f32(table)

    def right_side(t, parts, m):
        table = np.zeros((parts, 2 * m, 2 * m))
        table[:, :, :m] = t["block"].transpose(0, 2, 1)
        table[:, :, m:] = even_selector(m)
        return f32(table)

    row_x, row_y = rows(tx, gx, mx), rows(ty, gy, my)
    right_x, right_y = right_side(tx, gx, mx), f32(ty["block"].transpose(0, 2, 1))
    sum_x = f32(np.repeat(np.stack([tx["to_right"], tx["to_left"]], axis=1)[..., None], 128, axis=3))
    sum_y, fold_z = np.zeros((gy, breadth, 128)), np.zeros((gz, 8, 128))
    for out in range(mz + 2):
        sum_y[:, :, 2 * out], sum_y[:, :, 2 * out + 1] = ty["to_right"], ty["to_left"]
    sum_y[:, 0, 2 * (mz + 2) : 2 * (mz + 2) + mz] = 1.0

    width = max((mz + 2) * (depth + mz) + 2 * gz + 2 * mz, gx, gy)
    scalars = np.zeros((8 * ((gz + 2 + 7) // 8), 128 * ((width + 127) // 128)))
    for p in range(gz):
        full = np.concatenate([tz["block"][p], tz["to_right"][p : p + 1], tz["to_left"][p : p + 1]], axis=0)
        nodes = np.zeros((mz + 2, mz))
        nodes[:mz] = np.eye(mz)
        nodes[:mz, 0] -= tz["first"][p]
        nodes[mz, 0] = tz["first_right"][p]
        ends = [tz[key][p] for key in ("weight_left", "weight_right", "from_left", "from_right")]
        line = np.concatenate([full.reshape(-1), nodes.reshape(-1)] + ends)
        scalars[p, : line.size] = line
        fold_z[p, :depth, : 2 * (mz + 2)] = np.repeat(full.T, 2, axis=1)
        for j in range(mz):
            fold_z[p, 2 * j, 2 * (mz + 2) + j] = 1.0
    scalars[gz, :gx], scalars[gz + 1, :gy] = tx["first_right"], ty["first_right"]
    scalars = f32(scalars)

    vmem = pltpu.VMEM
    operands = (scalars, field, sum_x, f32(sum_y), f32(fold_z), row_y, row_x, right_y, right_x, f32(tx["block"]))
    operands += (f32(even_selector(my)),)
    send, own, even, near, far, first = call(
        functools.partial(local_kernel, sizes),
        "local",
        [shape(count, 4, my), shape(mz, mx, my), shape(mz, mx, my)] + [shape(mx, my)] * 3,
        [HBM] * 11,
        [VMEM] * 6,
        [
            vmem((2, depth, height, my), jnp.float32),
            vmem(sum_x.shape[1:], jnp.float32),
            vmem(sum_y.shape[1:], jnp.float32),
            vmem(fold_z.shape[1:], jnp.float32),
            vmem(row_y.shape[1:], jnp.float32),
            vmem(row_x.shape[1:], jnp.float32),
            vmem(right_y.shape[1:], jnp.float32),
            vmem(right_x.shape[1:], jnp.float32),
            vmem((mx, height), jnp.float32),
            vmem((breadth, my), jnp.float32),
            vmem((27, 4, my), jnp.float32),
            pltpu.SMEM(scalars.shape, jnp.float32),
            pltpu.SemaphoreType.DMA((2 * depth + 10,)),
        ],
    )(*(pltpu.with_memory_space_constraint(jnp.asarray(value), pltpu.HBM) for value in operands))
    received = lax.all_to_all(send, axes, 0, 0, tiled=True).reshape(count * 4, my)

    assert gz == 4
    plans = ((near, 1), (far, 2), (far, 3), (first, 1), (first, 3))
    gets = [lax.ppermute(plane, "gz", [(i, i ^ hop) for i in range(gz)]) for plane, hop in plans]

    up_x, up_y = f32(lift_matrix(mx)[:, :mx]), f32(lift_matrix(my)[:, :my].T)
    inner, top = call(
        inner_kernel,
        "inner",
        [shape(depth - 1, height, breadth), shape(height, breadth)],
        [VMEM] * 4,
        [VMEM] * 2,
    )(field, even, up_x, up_y)
    last, before = call(
        upper_kernel,
        "upper",
        [shape(height, breadth), shape(mz, mx, my)],
        [SMEM] + [VMEM] * 9,
        [VMEM] * 2,
    )(scalars, top, own, up_x, up_y, *gets)

    wx, wy, wz = combine_tables(sizes, tx, ty, tz, mz)
    return call(
        functools.partial(finish_kernel, sizes),
        "finish",
        [shape(*field.shape), shape(mz, mx, my)],
        [VMEM] * 11,
        [HBM, HBM],
        [
            vmem((depth, height, 128), jnp.float32),
            vmem((depth, 8, breadth - 128), jnp.float32),
            vmem((mz, mx, my), jnp.float32),
            pltpu.SemaphoreType.DMA((5,)),
        ],
    )(received, wx, wy, wz, row_x, row_y, up_x, up_y, inner, last, before)


def solution(mesh):
    sizes = tuple(mesh.shape[axis] for axis in ("gx", "gy", "gz"))
    return jax.shard_map(
        functools.partial(on_device, sizes),
        mesh=mesh,
        in_specs=(P("gz", "gx", "gy"),),
        out_specs=(P("gz", "gx", "gy"), P("gz", "gx", "gy")),
        check_vma=False,
    )
```

```python
import functools

import jax
import jax.numpy as jnp
import numpy as np
from jax import lax
from jax.experimental import pallas as pl
from jax.experimental.pallas import tpu as pltpu
from jax.sharding import PartitionSpec as P

RATIO = 2.0 - np.sqrt(3.0)
VMEM_LIMIT = 48 * 1024 * 1024


def inverse_mass(i, j, n):
    low, high = np.minimum(i, j), np.maximum(i, j)
    sign = np.where((high - low) % 2 == 0, 1.0, -1.0)
    value = RATIO ** (high - low + 1.0) * (1.0 - RATIO ** (2.0 * (low + 1))) * (1.0 - RATIO ** (2.0 * (n - high)))
    return 3.0 * sign * value / ((1.0 - RATIO**2) * (1.0 - RATIO ** (2.0 * (n + 1))))


def line_operator(i, k, n):
    a = k // 2
    odd = k % 2 == 1

    def at(j):
        inside = (j >= 0) & (j < n)
        return np.where(inside, inverse_mass(i, np.clip(j, 0, n - 1), n), 0.0)

    even_part = np.where(a == 0, 9.0, 10.0) * at(a) + at(a - 1) + at(a + 1)
    odd_part = 6.0 * at(a) + 6.0 * at(a + 1)
    return np.where(odd, odd_part, even_part) / 12.0


def line_tables(parts, m):
    n = parts * m
    node, fine = np.arange(m), np.arange(2 * m)
    block = np.zeros((parts, m, 2 * m))
    to_right, to_left = np.zeros((parts, 2 * m)), np.zeros((parts, 2 * m))
    from_left, from_right = np.zeros((parts, m)), np.zeros((parts, m))
    weight_left, weight_right = np.zeros((parts, parts)), np.zeros((parts, parts))
    first = np.zeros((parts, m))
    first_right = np.zeros((parts,))
    for p in range(parts):
        k = p * 2 * m + fine
        block[p] = line_operator((p * m + node)[:, None], k[None, :], n)
        if p + 1 < parts:
            to_right[p] = line_operator(np.full_like(k, (p + 1) * m), k, n)
        if p > 0:
            to_left[p] = line_operator(np.full_like(k, p * m - 1), k, n)
        from_left[p] = (-RATIO) ** node * (1 - RATIO ** (2.0 * (n - p * m - node))) / (1 - RATIO ** (2.0 * (n - p * m)))
        from_right[p] = (
            (-RATIO) ** (m - 1 - node) * (1 - RATIO ** (2.0 * (p * m + node + 1))) / (1 - RATIO ** (2.0 * (p + 1) * m))
        )
        for q in range(parts):
            if q < p:
                weight_left[p, q] = (
                    (-RATIO) ** ((p - q - 1) * m)
                    * (1 - RATIO ** (2.0 * (n - p * m)))
                    / (1 - RATIO ** (2.0 * (n - (q + 1) * m)))
                )
            if q > p:
                weight_right[p, q] = (
                    (-RATIO) ** ((q - p - 1) * m) * (1 - RATIO ** (2.0 * (p + 1) * m)) / (1 - RATIO ** (2.0 * q * m))
                )
    first[0] = inverse_mass(node, np.zeros_like(node), n) / 3.0
    if parts > 1:
        first_right[0] = -inverse_mass(np.array(m), np.array(0), n) / 3.0
    return {
        "block": block,
        "to_right": to_right,
        "to_left": to_left,
        "from_left": from_left,
        "from_right": from_right,
        "weight_left": weight_left,
        "weight_right": weight_right,
        "first": first,
        "first_right": first_right,
    }


def even_selector(m):
    pick = np.zeros((2 * m, m))
    pick[2 * np.arange(m), np.arange(m)] = 1.0
    return pick


def lift_matrix(m):
    up = np.zeros((2 * m, m + 1))
    up[2 * np.arange(m), np.arange(m)] = 1.0
    up[2 * np.arange(m) + 1, np.arange(m)] = 0.5
    up[2 * np.arange(m) + 1, np.arange(m) + 1] = 0.5
    return up


def f32(values):
    return np.asarray(values, np.float32)


def combine_tables(sizes, tx, ty, tz, mz):
    gx, gy, gz = sizes
    count = gx * gy * gz
    sender = np.arange(count)
    qx, qy, qz = sender // (gy * gz), (sender // gz) % gy, sender % gz
    rows = 32
    wx, wy, wz = (np.zeros((parts, rows, count, 4)) for parts in sizes)

    def side(t, p, q, which):
        if which == 0:
            return (q == p) * 1.0
        return (t["weight_left"] if which == 1 else t["weight_right"])[p][q]

    for sx in range(3):
        for sy in range(3):
            if sx == 0 and sy == 0:
                continue
            for z in range(mz):
                row = (sx * 3 + sy) * mz + z
                for p in range(gx):
                    wx[p, row] = side(tx, p, qx, sx)[:, None]
                for p in range(gy):
                    wy[p, row] = side(ty, p, qy, sy)[:, None]
                for p in range(gz):
                    wz[p, row, :, z] += qz == p
                    wz[p, row, :, 0] += tz["weight_left"][p][qz] * tz["from_left"][p, z]
                    wz[p, row, :, 0] += tz["weight_right"][p][qz] * tz["from_right"][p, z]
    for case, (ox, oy) in enumerate(((1, 0), (0, 1), (1, 1))):
        for layer in range(mz + 1):
            row = 9 * mz + case * (mz + 1) + layer
            for p in range(gx):
                wx[p, row] = (qx == p + ox)[:, None]
            for p in range(gy):
                wy[p, row] = (qy == p + oy)[:, None]
            for p in range(gz):
                if layer < mz:
                    wz[p, row, :, mz + layer] = qz == p
                else:
                    wz[p, row, :, mz] = qz == p + 1
    return tuple(f32(w.reshape(w.shape[0], rows, count * 4)) for w in (wx, wy, wz))


def split(values):
    high = values.astype(jnp.bfloat16)
    return high, (values - high.astype(jnp.float32)).astype(jnp.bfloat16)


def one_pass(a, b, contract=((1,), (0,))):
    return lax.dot_general(a, b, (contract, ((), ())), preferred_element_type=jnp.float32)


def three_pass(a, b, contract=((1,), (0,))):
    return one_pass(a[0], b[0], contract) + one_pass(a[0], b[1], contract) + one_pass(a[1], b[0], contract)


def exact_left(a, b):
    high, low = split(b)
    return one_pass(a, high) + one_pass(a, low)


def split_exact(values):
    return values.astype(jnp.bfloat16)


def exact_right(a, b):
    high, low = split(a)
    return one_pass(high, b) + one_pass(low, b)


def start_all(copies):
    for copy in copies:
        copy.start()


def local_kernel(sizes, *refs):
    numbers, field, sum_x, sum_y, fold_z, row_y, row_x, line_y, line_x, block_x, pick = refs[:11]
    send, own, even, near, far, first, both_far = refs[11:18]
    f, ax, ay, az, vy, vx, ry, rx, bx, sel, kinds, scalars, sem = refs[18:]
    gx, gy, gz = sizes
    px, py, pz = lax.axis_index("gx"), lax.axis_index("gy"), lax.axis_index("gz")
    depth, height, _ = field.shape
    mz, mx, my = own.shape
    planes = []
    for z in range(depth):
        halves = [
            pltpu.make_async_copy(field.at[z, :, pl.ds(h * my, my)], f.at[h, z], sem.at[2 * z + h]) for h in range(2)
        ]
        planes.append(halves)
    sources = [(line_y.at[py], ry), (sum_y.at[py], ay), (fold_z.at[pz], az), (sum_x.at[px], ax), (numbers, scalars)]
    sources += [(row_y.at[py], vy), (row_x.at[px], vx), (block_x.at[px], bx), (pick, sel), (line_x.at[px], rx)]
    tables = [pltpu.make_async_copy(src, dst, sem.at[2 * depth + i]) for i, (src, dst) in enumerate(sources)]
    start_all(tables[:3] + planes[0] + planes[1] + tables[3:] + planes[2] + planes[3])
    for table in tables[:3]:
        table.wait()
    kinds[...] = jnp.zeros_like(kinds)
    solve_y = split(ry[...])
    by_y, along_x = [], None
    for z in range(depth):
        sum_z = split(ay[...] * az[z : z + 1, :])
        weights = tuple(jnp.concatenate([a, b], axis=1) for a, b in zip(solve_y, sum_z, strict=True))
        for half in planes[z]:
            half.wait()
        both = three_pass(split(jnp.concatenate([f[0, z], f[1, z]], axis=1)), weights)
        by_y.append(both[:, :my])
        along_x = both[:, my:] if along_x is None else along_x + both[:, my:]
    for table in tables[3:]:
        table.wait()

    by_x = three_pass(split(jnp.transpose(along_x)[:16, :]), split(rx[...]))
    sums = [[jnp.sum(by_y[z] * ax[ab], axis=0, keepdims=True) for ab in range(2)] for z in range(depth)]
    corners = [jnp.sum(along_x * ax[ab], axis=0, keepdims=True) for ab in range(2)]
    pick_y = split_exact(sel[...])
    evens = []
    for j in range(mz):
        rows = jnp.concatenate([f[h, 2 * j, pl.ds(0, mx, stride=2), :] for h in range(2)], axis=1)
        evens.append(exact_right(rows, pick_y))
        even[j] = evens[j]
    first_y, first_x = vy[8:9, :my], vx[8:9, :mx]
    kappa_x, kappa_y = scalars[gz, px], scalars[gz + 1, py]
    ends = 2 * (mz + 2)
    first_rows = [evens[j][0:1, :] for j in range(mz)]
    first_cols = [by_x[ends + j : ends + j + 1, mx:] for j in range(mz)]
    for out in range(mz + 2):
        base = (mz + 2) * depth + out * mz
        first_row = sum(scalars[pz, base + j] * first_rows[j] for j in range(mz))
        first_col = sum(scalars[pz, base + j] * first_cols[j] for j in range(mz))
        corner = first_row[:, 0:1]
        right_row, left_row = (sum(scalars[pz, out * depth + z] * sums[z][ab] for z in range(depth)) for ab in range(2))
        r, l = slice(2 * out, 2 * out + 1), slice(2 * out + 1, 2 * out + 2)
        spread = jnp.zeros((1, my), jnp.float32)
        chunks = {
            (1, 0): right_row - kappa_x * (first_row - first_y * corner),
            (2, 0): left_row,
            (0, 1): by_x[r, :mx] - kappa_y * (first_col - first_x * corner),
            (0, 2): by_x[l, :mx],
            (1, 1): spread + (corners[0][:, r] - kappa_x * kappa_y * corner),
            (1, 2): spread + corners[0][:, l],
            (2, 1): spread + corners[1][:, r],
            (2, 2): spread + corners[1][:, l],
        }
        for (sx, sy), row in chunks.items():
            kind = (sx * 3 + sy) * 3
            if out < mz:
                kinds[kind, out : out + 1, :] = row
            else:
                kinds[kind + out - mz + 1, 0:1, :] = row
    for sx in range(3):
        for sy in range(3):
            halo = jnp.concatenate(first_cols if sx == 0 else first_rows, axis=0)
            for sz in range(3):
                kinds[(sx * 3 + sy) * 3 + sz, mz : 2 * mz, :] = halo

    def side(there, here):
        return jnp.where(there == here, 0, jnp.where(there > here, 1, 2))

    def scatter(tx, ty, tz, at):
        send[pl.ds(at, 1)] = kinds[pl.ds((side(tx, px) * 3 + side(ty, py)) * 3 + side(tz, pz), 1)]

    if gx * gy * gz <= 32:
        for at in range(gx * gy * gz):
            scatter(at // (gy * gz), (at // gz) % gy, at % gz, at)
    else:

        @pl.loop(0, gx * gy * gz)
        def _(at):
            scatter(at // (gy * gz), (at // gz) % gy, at % gz, at)

    solve_x = split(bx[...])
    solved = [three_pass(solve_x, split(by_y[z])) for z in range(depth)]
    first_x = jnp.transpose(jnp.broadcast_to(first_x, (8, mx)))[:, 0:1]
    outs = []
    for out in range(mz + 2):
        value = sum(scalars[pz, out * depth + z] * solved[z] for z in range(depth))
        base = (mz + 2) * depth + out * mz
        part = sum(scalars[pz, base + j] * evens[j] for j in range(mz))
        part = part - first_x * part[0:1, :]
        part = part - part[:, 0:1] * first_y
        outs.append(value - part)
    for j in range(mz):
        own[j] = evens[j] + outs[j]
    near[...] = jnp.where(pz % 2 == 0, outs[mz], outs[mz + 1])
    far[...] = jnp.where(pz % 4 < 2, outs[mz], outs[mz + 1])
    both_far[0] = jnp.where(pz % 4 < 2, outs[mz], outs[mz + 1])
    both_far[1] = evens[0]
    first[...] = evens[0]


def inner_kernel(field, even, up_x, up_y, c, top):
    depth = field.shape[0]
    mz = even.shape[0]
    up_x, up_y = up_x[...].astype(jnp.bfloat16), up_y[...].astype(jnp.bfloat16)
    lifted = [exact_right(exact_left(up_x, even[j]), up_y) for j in range(mz)]
    for z in range(depth - 1):
        j = z // 2
        c[z] = field[z] - (lifted[j] if z % 2 == 0 else 0.5 * (lifted[j] + lifted[j + 1]))
    top[...] = field[depth - 1] - 0.5 * lifted[mz - 1]


def upper_kernel(scalars, top, own, up_x, up_y, one, two, three, first, last, coarse):
    gz = lax.axis_size("gz")
    pz = lax.axis_index("gz")
    mz = own.shape[0]
    base = (mz + 2) * (2 * mz + mz)
    left, right = jnp.zeros(own.shape[1:], jnp.float32), jnp.zeros(own.shape[1:], jnp.float32)
    for plane, hop in ((one[...], 1), (two[...], 2), (three[0], 3)):
        left = left + scalars[pz, base + (pz ^ hop)] * plane
        right = right + scalars[pz, base + gz + (pz ^ hop)] * plane
    ahead = jnp.where(pz ^ 1 == pz + 1, 1.0, 0.0) * first[...]
    ahead = ahead + jnp.where(pz ^ 3 == pz + 1, 1.0, 0.0) * three[1]
    up_x, up_y = up_x[...].astype(jnp.bfloat16), up_y[...].astype(jnp.bfloat16)
    last[...] = top[...] - 0.5 * exact_right(exact_left(up_x, ahead), up_y)
    base = base + 2 * gz
    for j in range(mz):
        coarse[j] = own[j] + scalars[pz, base + j] * left + scalars[pz, base + mz + j] * right


def finish_kernel(
    sizes,
    received,
    wx,
    wy,
    wz,
    row_x,
    row_y,
    up_x,
    up_y,
    inner,
    top,
    before,
    coefficients,
    coarse,
    rim,
    foot,
    values,
    sem,
):
    px, py, pz = lax.axis_index("gx"), lax.axis_index("gy"), lax.axis_index("gz")
    mz, mx, my = before.shape
    depth, height, breadth = 2 * mz, 2 * mx, 2 * my
    split_at = breadth - 128
    body = (pl.ds(0, height - 8), pl.ds(0, split_at))
    copies = [
        pltpu.make_async_copy(inner.at[:, *body], coefficients.at[pl.ds(0, depth - 1), *body], sem.at[0]),
        pltpu.make_async_copy(top.at[body], coefficients.at[depth - 1, *body], sem.at[1]),
    ]
    start_all(copies)
    weights = wx[px] * wy[py] * wz[pz]
    got = three_pass(split(weights), split(received[...]))

    base = 9 * mz
    layers = mz + 1
    halo_x, halo_y, halo_xy = (got[base + i * layers : base + (i + 1) * layers] for i in range(3))
    pad = jnp.zeros((8 - layers, halo_x.shape[1]), jnp.float32)
    row = exact_right(jnp.concatenate([halo_x, pad], axis=0), up_y[...].astype(jnp.bfloat16))
    tall = jnp.concatenate([halo_y, jnp.zeros((128 - layers, halo_y.shape[1]), jnp.float32)], axis=0)
    col = exact_left(up_x[...].astype(jnp.bfloat16), jnp.transpose(tall))
    lane = lax.broadcasted_iota(jnp.int32, (1, 128), 1)
    last = lane == 127
    for z in range(depth):
        j = z // 2
        if z % 2 == 0:
            r, s, k = row[j : j + 1], 0.5 * col[:, j : j + 1], halo_xy[j : j + 1, 0:1]
        else:
            r = 0.5 * (row[j : j + 1] + row[j + 1 : j + 2])
            s = 0.25 * (col[:, j : j + 1] + col[:, j + 1 : j + 2])
            k = 0.5 * (halo_xy[j : j + 1, 0:1] + halo_xy[j + 1 : j + 2, 0:1])
        old = inner[z] if z < depth - 1 else top[...]
        rim[z] = old[:, split_at:] - jnp.where(last, s, 0.0)
        end = 0.5 * r[:, split_at:] + jnp.where(last, 0.25 * k, 0.0)
        rim[z, height - 1 : height, :] = rim[z, height - 1 : height, :] - end
        foot[z] = old[height - 8 :, :split_at]
        foot[z, 7:8, :] = old[height - 1 :, :split_at] - 0.5 * r[:, :split_at]
    copies.append(pltpu.make_async_copy(rim, coefficients.at[:, :, pl.ds(split_at, 128)], sem.at[2]))
    copies.append(pltpu.make_async_copy(foot, coefficients.at[:, pl.ds(height - 8, 8), pl.ds(0, split_at)], sem.at[3]))
    start_all(copies[2:])

    ux, vx = row_x[px, 9:10, :mx], row_x[px, 10:11, :mx]
    uy, vy = row_y[py, 9:10, :my], row_y[py, 10:11, :my]

    def part(sx, sy, z):
        at = (sx * 3 + sy) * mz + z
        return got[at : at + 1]

    for z in range(mz):
        a, b = [], []
        for sy, end in ((1, uy), (2, vy)):
            a.append(part(0, sy, z) + ux * part(1, sy, z)[:, 0:1] + vx * part(2, sy, z)[:, 0:1])
            b.append(end)
        for sx, end in ((1, ux), (2, vx)):
            a.append(end)
            b.append(part(sx, 0, z))
        zero = [jnp.zeros((4, mx), jnp.float32)]
        a, b = split(jnp.concatenate(a + zero, axis=0)), split(jnp.concatenate(b + zero, axis=0))
        values[z] = before[z] + three_pass(a, b, ((0,), (0,)))
    copies.append(pltpu.make_async_copy(values, coarse, sem.at[4]))
    copies[4].start()
    for copy in copies:
        copy.wait()


def call(kernel, name, out_shape, in_specs, out_specs, scratch=(), aliases=None, flops=1, size=1):
    return pl.pallas_call(
        kernel,
        out_shape=out_shape,
        in_specs=in_specs,
        out_specs=out_specs,
        scratch_shapes=list(scratch),
        input_output_aliases=aliases or {},
        compiler_params=pltpu.CompilerParams(vmem_limit_bytes=VMEM_LIMIT),
        cost_estimate=pl.CostEstimate(flops=flops, bytes_accessed=size, transcendentals=0),
        name=name,
    )


ANY = pl.BlockSpec(memory_space=pl.ANY)
HBM = pl.BlockSpec(memory_space=pltpu.HBM)
SMEM = pl.BlockSpec(memory_space=pltpu.SMEM)
VMEM = pl.BlockSpec(memory_space=pltpu.VMEM)


def shape(*dims):
    return jax.ShapeDtypeStruct(dims, jnp.float32)


def on_device(sizes, field):
    gx, gy, gz = sizes
    depth, height, breadth = field.shape
    mz, mx, my = depth // 2, height // 2, breadth // 2
    count = gx * gy * gz
    axes = ("gx", "gy", "gz")
    tx, ty, tz = line_tables(gx, mx), line_tables(gy, my), line_tables(gz, mz)

    def rows(t, parts, m):
        table = np.zeros((parts, 16, 2 * m))
        table[:, 0], table[:, 1] = t["to_right"], t["to_left"]
        table[:, 8, :m], table[:, 9, :m], table[:, 10, :m] = t["first"], t["from_left"], t["from_right"]
        return f32(table)

    def right_side(t, parts, m):
        table = np.zeros((parts, 2 * m, 2 * m))
        table[:, :, :m] = t["block"].transpose(0, 2, 1)
        table[:, :, m:] = even_selector(m)
        return f32(table)

    row_x, row_y = rows(tx, gx, mx), rows(ty, gy, my)
    right_x, right_y = right_side(tx, gx, mx), f32(ty["block"].transpose(0, 2, 1))
    sum_x = f32(np.repeat(np.stack([tx["to_right"], tx["to_left"]], axis=1)[..., None], 128, axis=3))
    sum_y, fold_z = np.zeros((gy, breadth, 128)), np.zeros((gz, 8, 128))
    for out in range(mz + 2):
        sum_y[:, :, 2 * out], sum_y[:, :, 2 * out + 1] = ty["to_right"], ty["to_left"]
    sum_y[:, 0, 2 * (mz + 2) : 2 * (mz + 2) + mz] = 1.0

    width = max((mz + 2) * (depth + mz) + 2 * gz + 2 * mz, gx, gy)
    scalars = np.zeros((8 * ((gz + 2 + 7) // 8), 128 * ((width + 127) // 128)))
    for p in range(gz):
        full = np.concatenate([tz["block"][p], tz["to_right"][p : p + 1], tz["to_left"][p : p + 1]], axis=0)
        nodes = np.zeros((mz + 2, mz))
        nodes[:mz] = np.eye(mz)
        nodes[:mz, 0] -= tz["first"][p]
        nodes[mz, 0] = tz["first_right"][p]
        ends = [tz[key][p] for key in ("weight_left", "weight_right", "from_left", "from_right")]
        line = np.concatenate([full.reshape(-1), nodes.reshape(-1)] + ends)
        scalars[p, : line.size] = line
        fold_z[p, :depth, : 2 * (mz + 2)] = np.repeat(full.T, 2, axis=1)
        for j in range(mz):
            fold_z[p, 2 * j, 2 * (mz + 2) + j] = 1.0
    scalars[gz, :gx], scalars[gz + 1, :gy] = tx["first_right"], ty["first_right"]
    scalars = f32(scalars)

    vmem = pltpu.VMEM
    operands = (scalars, field, sum_x, f32(sum_y), f32(fold_z), row_y, row_x, right_y, right_x, f32(tx["block"]))
    operands += (f32(even_selector(my)),)
    send, own, even, near, far, first, both_far = call(
        functools.partial(local_kernel, sizes),
        "local",
        [shape(count, 4, my), shape(mz, mx, my), shape(mz, mx, my)] + [shape(mx, my)] * 3 + [shape(2, mx, my)],
        [HBM] * 11,
        [VMEM] * 7,
        [
            vmem((2, depth, height, my), jnp.float32),
            vmem(sum_x.shape[1:], jnp.float32),
            vmem(sum_y.shape[1:], jnp.float32),
            vmem(fold_z.shape[1:], jnp.float32),
            vmem(row_y.shape[1:], jnp.float32),
            vmem(row_x.shape[1:], jnp.float32),
            vmem(right_y.shape[1:], jnp.float32),
            vmem(right_x.shape[1:], jnp.float32),
            vmem((mx, height), jnp.float32),
            vmem((breadth, my), jnp.float32),
            vmem((27, 4, my), jnp.float32),
            pltpu.SMEM(scalars.shape, jnp.float32),
            pltpu.SemaphoreType.DMA((2 * depth + 10,)),
        ],
    )(*(pltpu.with_memory_space_constraint(jnp.asarray(value), pltpu.HBM) for value in operands))
    received = lax.all_to_all(send, axes, 0, 0, tiled=True).reshape(count * 4, my)

    assert gz == 4
    plans = ((near, 1), (far, 2), (both_far, 3), (first, 1))
    gets = [lax.ppermute(plane, "gz", [(i, i ^ hop) for i in range(gz)]) for plane, hop in plans]

    up_x, up_y = f32(lift_matrix(mx)[:, :mx]), f32(lift_matrix(my)[:, :my].T)
    inner, top = call(
        inner_kernel,
        "inner",
        [shape(depth - 1, height, breadth), shape(height, breadth)],
        [VMEM] * 4,
        [VMEM] * 2,
    )(field, even, up_x, up_y)
    last, before = call(
        upper_kernel,
        "upper",
        [shape(height, breadth), shape(mz, mx, my)],
        [SMEM] + [VMEM] * 8,
        [VMEM] * 2,
    )(scalars, top, own, up_x, up_y, *gets)

    wx, wy, wz = combine_tables(sizes, tx, ty, tz, mz)
    return call(
        functools.partial(finish_kernel, sizes),
        "finish",
        [shape(*field.shape), shape(mz, mx, my)],
        [VMEM] * 11,
        [HBM, HBM],
        [
            vmem((depth, height, 128), jnp.float32),
            vmem((depth, 8, breadth - 128), jnp.float32),
            vmem((mz, mx, my), jnp.float32),
            pltpu.SemaphoreType.DMA((5,)),
        ],
    )(received, wx, wy, wz, row_x, row_y, up_x, up_y, inner, last, before)


def solution(mesh):
    sizes = tuple(mesh.shape[axis] for axis in ("gx", "gy", "gz"))
    return jax.shard_map(
        functools.partial(on_device, sizes),
        mesh=mesh,
        in_specs=(P("gz", "gx", "gy"),),
        out_specs=(P("gz", "gx", "gy"), P("gz", "gx", "gy")),
        check_vma=False,
    )
```

```python
import functools

import jax
import jax.numpy as jnp
import numpy as np
from jax import lax
from jax.experimental import pallas as pl
from jax.experimental.pallas import tpu as pltpu
from jax.sharding import PartitionSpec as P

RATIO = 2.0 - np.sqrt(3.0)
VMEM_LIMIT = 48 * 1024 * 1024


def inverse_mass(i, j, n):
    low, high = np.minimum(i, j), np.maximum(i, j)
    sign = np.where((high - low) % 2 == 0, 1.0, -1.0)
    value = RATIO ** (high - low + 1.0) * (1.0 - RATIO ** (2.0 * (low + 1))) * (1.0 - RATIO ** (2.0 * (n - high)))
    return 3.0 * sign * value / ((1.0 - RATIO**2) * (1.0 - RATIO ** (2.0 * (n + 1))))


def line_operator(i, k, n):
    a = k // 2
    odd = k % 2 == 1

    def at(j):
        inside = (j >= 0) & (j < n)
        return np.where(inside, inverse_mass(i, np.clip(j, 0, n - 1), n), 0.0)

    even_part = np.where(a == 0, 9.0, 10.0) * at(a) + at(a - 1) + at(a + 1)
    odd_part = 6.0 * at(a) + 6.0 * at(a + 1)
    return np.where(odd, odd_part, even_part) / 12.0


def line_tables(parts, m):
    n = parts * m
    node, fine = np.arange(m), np.arange(2 * m)
    block = np.zeros((parts, m, 2 * m))
    to_right, to_left = np.zeros((parts, 2 * m)), np.zeros((parts, 2 * m))
    from_left, from_right = np.zeros((parts, m)), np.zeros((parts, m))
    weight_left, weight_right = np.zeros((parts, parts)), np.zeros((parts, parts))
    first = np.zeros((parts, m))
    first_right = np.zeros((parts,))
    for p in range(parts):
        k = p * 2 * m + fine
        block[p] = line_operator((p * m + node)[:, None], k[None, :], n)
        if p + 1 < parts:
            to_right[p] = line_operator(np.full_like(k, (p + 1) * m), k, n)
        if p > 0:
            to_left[p] = line_operator(np.full_like(k, p * m - 1), k, n)
        from_left[p] = (-RATIO) ** node * (1 - RATIO ** (2.0 * (n - p * m - node))) / (1 - RATIO ** (2.0 * (n - p * m)))
        from_right[p] = (
            (-RATIO) ** (m - 1 - node) * (1 - RATIO ** (2.0 * (p * m + node + 1))) / (1 - RATIO ** (2.0 * (p + 1) * m))
        )
        for q in range(parts):
            if q < p:
                weight_left[p, q] = (
                    (-RATIO) ** ((p - q - 1) * m)
                    * (1 - RATIO ** (2.0 * (n - p * m)))
                    / (1 - RATIO ** (2.0 * (n - (q + 1) * m)))
                )
            if q > p:
                weight_right[p, q] = (
                    (-RATIO) ** ((q - p - 1) * m) * (1 - RATIO ** (2.0 * (p + 1) * m)) / (1 - RATIO ** (2.0 * q * m))
                )
    first[0] = inverse_mass(node, np.zeros_like(node), n) / 3.0
    if parts > 1:
        first_right[0] = -inverse_mass(np.array(m), np.array(0), n) / 3.0
    return {
        "block": block,
        "to_right": to_right,
        "to_left": to_left,
        "from_left": from_left,
        "from_right": from_right,
        "weight_left": weight_left,
        "weight_right": weight_right,
        "first": first,
        "first_right": first_right,
    }


def even_selector(m):
    pick = np.zeros((2 * m, m))
    pick[2 * np.arange(m), np.arange(m)] = 1.0
    return pick


def f32(values):
    return np.asarray(values, np.float32)


def combine_tables(sizes, tx, ty, tz, mz):
    gx, gy, gz = sizes
    count = gx * gy * gz
    sender = np.arange(count)
    qx, qy, qz = sender // (gy * gz), (sender // gz) % gy, sender % gz
    rows = 32
    wx, wy, wz = (np.zeros((parts, rows, count, 4)) for parts in sizes)

    def side(t, p, q, which):
        if which == 0:
            return (q == p) * 1.0
        return (t["weight_left"] if which == 1 else t["weight_right"])[p][q]

    for sx in range(3):
        for sy in range(3):
            if sx == 0 and sy == 0:
                continue
            for z in range(mz):
                row = (sx * 3 + sy) * mz + z
                for p in range(gx):
                    wx[p, row] = side(tx, p, qx, sx)[:, None]
                for p in range(gy):
                    wy[p, row] = side(ty, p, qy, sy)[:, None]
                for p in range(gz):
                    wz[p, row, :, z] += qz == p
                    wz[p, row, :, 0] += tz["weight_left"][p][qz] * tz["from_left"][p, z]
                    wz[p, row, :, 0] += tz["weight_right"][p][qz] * tz["from_right"][p, z]
    for case, (ox, oy) in enumerate(((1, 0), (0, 1), (1, 1))):
        for layer in range(mz + 1):
            row = 9 * mz + case * (mz + 1) + layer
            for p in range(gx):
                wx[p, row] = (qx == p + ox)[:, None]
            for p in range(gy):
                wy[p, row] = (qy == p + oy)[:, None]
            for p in range(gz):
                if layer < mz:
                    wz[p, row, :, mz + layer] = qz == p
                else:
                    wz[p, row, :, mz] = qz == p + 1
    return tuple(f32(w.reshape(w.shape[0], rows, count * 4)) for w in (wx, wy, wz))


def split(values):
    high = values.astype(jnp.bfloat16)
    return high, (values - high.astype(jnp.float32)).astype(jnp.bfloat16)


def one_pass(a, b, contract=((1,), (0,))):
    return lax.dot_general(a, b, (contract, ((), ())), preferred_element_type=jnp.float32)


def three_pass(a, b, contract=((1,), (0,))):
    return one_pass(a[0], b[0], contract) + one_pass(a[0], b[1], contract) + one_pass(a[1], b[0], contract)


def two_pass(a, b):
    return one_pass(a[0], b) + one_pass(a[1], b)


def exact_left(a, b):
    high, low = split(b)
    return one_pass(a, high) + one_pass(a, low)


def exact_right(a, b):
    high, low = split(a)
    return one_pass(high, b) + one_pass(low, b)


def start_all(copies):
    for copy in copies:
        copy.start()


def local_kernel(sizes, *refs):
    numbers, field, fold_z, line_y, line_x = refs[:5]
    send, own, even, near, far, first, both_far, f = refs[5:13]
    ry, bx, az, picked, column, kinds, scalars, sem = refs[13:]
    gx, gy, gz = sizes
    px, py, pz = lax.axis_index("gx"), lax.axis_index("gy"), lax.axis_index("gz")
    depth, height, breadth = field.shape
    mz, mx, my = own.shape
    planes = [pltpu.make_async_copy(field.at[z], f.at[z], sem.at[z]) for z in range(depth)]
    sources = [(fold_z.at[pz], az), (line_y.at[py], ry), (line_x.at[px], bx), (numbers, scalars)]
    tables = [pltpu.make_async_copy(src, dst, sem.at[depth + i]) for i, (src, dst) in enumerate(sources)]
    start_all(tables[:2] + planes + tables[2:])
    kinds[...] = jnp.zeros_like(kinds)
    fine = lax.broadcasted_iota(jnp.int32, (breadth, my), 0)
    node = lax.broadcasted_iota(jnp.int32, (breadth, my), 1)
    pick_y = jnp.where(fine == 2 * node, 1.0, 0.0).astype(jnp.bfloat16)
    tables[0].wait()
    tables[1].wait()
    weights = split(ry[:breadth])
    by_y, evens, along_x = [], [], None
    step = 2
    for start in range(0, depth, step):
        for z in range(start, start + step):
            planes[z].wait()
        part = split(f[start : start + step].reshape(step * height, breadth))
        result = three_pass(part, weights)
        for z in range(start, start + step):
            rows = slice((z - start) * height, (z - start + 1) * height)
            by_y.append(result[rows, :my])
            folded = result[rows, my:] * az[z : z + 1, :]
            along_x = folded if along_x is None else along_x + folded
            if z % 2 == 0:
                j = z // 2
                picked[j] = two_pass((part[0][rows], part[1][rows]), pick_y)
                evens.append(picked[j, pl.ds(0, mx, stride=2), :])
                even[j] = evens[j]
    column[...] = along_x
    edge = jnp.transpose(column[pl.ds(0, mx, stride=2), :])[:16, :]
    for table in tables[2:]:
        table.wait()
    solve_x = split(bx[: mx + 8])
    faces = three_pass(solve_x, split(along_x))
    by_x = jnp.transpose(faces[:mx])[:16, :]
    corners = [faces[mx + ab : mx + ab + 1] for ab in range(2)]
    by_split = split(jnp.concatenate(by_y, axis=1))
    ends_x = three_pass(tuple(half[mx:] for half in solve_x), by_split)
    sums = [[ends_x[ab : ab + 1, z * my : (z + 1) * my] for ab in range(2)] for z in range(depth)]

    first_y, first_x = ry[breadth : breadth + 1, :my], bx[mx + 8 : mx + 9, :mx]
    kappa_x, kappa_y = scalars[gz, px], scalars[gz + 1, py]
    ends = 2 * (mz + 2)
    first_rows = [evens[j][0:1, :] for j in range(mz)]
    first_cols = [edge[ends + j : ends + j + 1, :] for j in range(mz)]
    for out in range(mz + 2):
        base = (mz + 2) * depth + out * mz
        first_row = sum(scalars[pz, base + j] * first_rows[j] for j in range(mz))
        first_col = sum(scalars[pz, base + j] * first_cols[j] for j in range(mz))
        corner = first_row[:, 0:1]
        right_row, left_row = (sum(scalars[pz, out * depth + z] * sums[z][ab] for z in range(depth)) for ab in range(2))
        r, l = slice(2 * out, 2 * out + 1), slice(2 * out + 1, 2 * out + 2)
        spread = jnp.zeros((1, my), jnp.float32)
        chunks = {
            (1, 0): right_row - kappa_x * (first_row - first_y * corner),
            (2, 0): left_row,
            (0, 1): by_x[r] - kappa_y * (first_col - first_x * corner),
            (0, 2): by_x[l],
            (1, 1): spread + (corners[0][:, r] - kappa_x * kappa_y * corner),
            (1, 2): spread + corners[0][:, l],
            (2, 1): spread + corners[1][:, r],
            (2, 2): spread + corners[1][:, l],
        }
        for (sx, sy), row in chunks.items():
            kind = (sx * 3 + sy) * 3
            if out < mz:
                kinds[kind, out : out + 1, :] = row
            else:
                kinds[kind + out - mz + 1, 0:1, :] = row
    for sx in range(3):
        for sy in range(3):
            halo = jnp.concatenate(first_cols if sx == 0 else first_rows, axis=0)
            for sz in range(3):
                kinds[(sx * 3 + sy) * 3 + sz, mz : 2 * mz, :] = halo

    def side(there, here):
        return jnp.where(there == here, 0, jnp.where(there > here, 1, 2))

    def scatter(tx, ty, tz, at):
        send[pl.ds(at, 1)] = kinds[pl.ds((side(tx, px) * 3 + side(ty, py)) * 3 + side(tz, pz), 1)]

    if gx * gy * gz <= 32:
        for at in range(gx * gy * gz):
            scatter(at // (gy * gz), (at // gz) % gy, at % gz, at)
    else:

        @pl.loop(0, gx * gy * gz)
        def _(at):
            scatter(at // (gy * gz), (at // gz) % gy, at % gz, at)

    by_all = three_pass(tuple(half[:mx] for half in solve_x), by_split)
    solved = [by_all[:, z * my : (z + 1) * my] for z in range(depth)]
    first_x = jnp.transpose(jnp.broadcast_to(first_x, (8, mx)))[:, 0:1]
    outs = []
    for out in range(mz + 2):
        value = sum(scalars[pz, out * depth + z] * solved[z] for z in range(depth))
        base = (mz + 2) * depth + out * mz
        part = sum(scalars[pz, base + j] * evens[j] for j in range(mz))
        part = part - first_x * part[0:1, :]
        part = part - part[:, 0:1] * first_y
        outs.append(value - part)
    for j in range(mz):
        own[j] = evens[j] + outs[j]
    near[...] = jnp.where(pz % 2 == 0, outs[mz], outs[mz + 1])
    far[...] = jnp.where(pz % 4 < 2, outs[mz], outs[mz + 1])
    both_far[0] = jnp.where(pz % 4 < 2, outs[mz], outs[mz + 1])
    both_far[1] = evens[0]
    first[...] = evens[0]


def inner_kernel(field, even, *refs):
    tables, (coefficients, c, top, rows, weights, up_x, up_y), (parts, sem) = refs[:6], refs[6:13], refs[13:]
    px, py, pz = lax.axis_index("gx"), lax.axis_index("gy"), lax.axis_index("gz")
    depth, height, breadth = field.shape
    mz = even.shape[0]
    goals = (rows.at[0:8], rows.at[8:16], rows.at[16:32], parts.at[0], parts.at[1], parts.at[2])
    fetches = [
        pltpu.make_async_copy(table.at[at], goal, sem.at[depth + i])
        for i, (table, at, goal) in enumerate(zip(tables, (px, py, pz) * 2, goals, strict=True))
    ]
    start_all(fetches)
    for up, node_axis in ((up_x, 1), (up_y, 0)):
        node = lax.broadcasted_iota(jnp.int32, up.shape, node_axis)
        away = jnp.abs(lax.broadcasted_iota(jnp.int32, up.shape, 1 - node_axis) - 2 * node)
        up[...] = jnp.where(away == 0, 1.0, jnp.where(away == 1, 0.5, 0.0))
    body = (pl.ds(0, height - 8), pl.ds(0, breadth - 128))
    up_left, up_right = up_x[...].astype(jnp.bfloat16), up_y[...].astype(jnp.bfloat16)
    lifted = [exact_right(exact_left(up_left, even[j]), up_right) for j in range(mz)]
    copies = []
    for z in range(depth - 1):
        j = z // 2
        c[z] = field[z] - (lifted[j] if z % 2 == 0 else 0.5 * (lifted[j] + lifted[j + 1]))
        copies.append(pltpu.make_async_copy(c.at[z, *body], coefficients.at[z, *body], sem.at[z]))
        copies[z].start()
    top[...] = field[depth - 1] - 0.5 * lifted[mz - 1]
    for copy in fetches:
        copy.wait()
    weights[...] = parts[0] * parts[1] * parts[2]
    for copy in copies:
        copy.wait()


def gather_kernel(received, weights, got):
    got[...] = three_pass(split(weights[...]), split(received[...]))


def finish_kernel(*refs):
    got, rows, up_x, up_y, inner, top, own, one, two, three, first, partial = refs[:12]
    coefficients, coarse, last_plane, rim, foot, values, sem = refs[12:]
    del partial
    mz, mx, my = own.shape
    depth, height, breadth = 2 * mz, 2 * mx, 2 * my
    split_at = breadth - 128
    body = (pl.ds(0, height - 8), pl.ds(0, split_at))

    def row_at(i):
        return rows[16 + i : 17 + i, :]

    planes = (one[...], two[...], three[0])
    left = sum(row_at(i) * plane for i, plane in enumerate(planes))
    right = sum(row_at(3 + i) * plane for i, plane in enumerate(planes))
    ahead = row_at(6) * first[...] + row_at(7) * three[1]
    up_left, up_right = up_x[...].astype(jnp.bfloat16), up_y[...].astype(jnp.bfloat16)
    last_plane[...] = top[...] - 0.5 * exact_right(exact_left(up_left, ahead), up_right)
    copies = [pltpu.make_async_copy(last_plane.at[body], coefficients.at[depth - 1, *body], sem.at[0])]
    copies[0].start()
    before = [own[j] + row_at(8 + j) * left + row_at(8 + mz + j) * right for j in range(mz)]

    base = 9 * mz
    layers = mz + 1
    halo_x, halo_y, halo_xy = (got[base + i * layers : base + (i + 1) * layers] for i in range(3))
    pad = jnp.zeros((8 - layers, halo_x.shape[1]), jnp.float32)
    row = exact_right(jnp.concatenate([halo_x, pad], axis=0), up_right)
    tall = jnp.concatenate([halo_y, jnp.zeros((128 - layers, halo_y.shape[1]), jnp.float32)], axis=0)
    col = exact_left(up_left, jnp.transpose(tall))
    lane = lax.broadcasted_iota(jnp.int32, (1, 128), 1)
    last = lane == 127
    for z in range(depth):
        j = z // 2
        if z % 2 == 0:
            r, s, k = row[j : j + 1], 0.5 * col[:, j : j + 1], halo_xy[j : j + 1, 0:1]
        else:
            r = 0.5 * (row[j : j + 1] + row[j + 1 : j + 2])
            s = 0.25 * (col[:, j : j + 1] + col[:, j + 1 : j + 2])
            k = 0.5 * (halo_xy[j : j + 1, 0:1] + halo_xy[j + 1 : j + 2, 0:1])
        old = inner[z] if z < depth - 1 else last_plane[...]
        rim[z] = old[:, split_at:] - jnp.where(last, s, 0.0)
        end = 0.5 * r[:, split_at:] + jnp.where(last, 0.25 * k, 0.0)
        rim[z, height - 1 : height, :] = rim[z, height - 1 : height, :] - end
        foot[z] = old[height - 8 :, :split_at]
        foot[z, 7:8, :] = old[height - 1 :, :split_at] - 0.5 * r[:, :split_at]
        goal = coefficients.at[z, :, pl.ds(split_at, 128)]
        copies.append(pltpu.make_async_copy(rim.at[z], goal, sem.at[3 + 2 * z]))
        goal = coefficients.at[z, pl.ds(height - 8, 8), pl.ds(0, split_at)]
        copies.append(pltpu.make_async_copy(foot.at[z], goal, sem.at[4 + 2 * z]))
        start_all(copies[-2:])

    ux, vx, uy, vy = rows[0:1], rows[1:2], rows[8:9], rows[9:10]

    def part(sx, sy, z):
        at = (sx * 3 + sy) * mz + z
        return got[at : at + 1]

    for z in range(mz):
        a, b = [], []
        for sy, end in ((1, uy), (2, vy)):
            a.append(part(0, sy, z) + ux * part(1, sy, z)[:, 0:1] + vx * part(2, sy, z)[:, 0:1])
            b.append(end)
        for sx, end in ((1, ux), (2, vx)):
            a.append(end)
            b.append(part(sx, 0, z))
        zero = [jnp.zeros((4, mx), jnp.float32)]
        a, b = split(jnp.concatenate(a + zero, axis=0)), split(jnp.concatenate(b + zero, axis=0))
        values[z] = before[z] + three_pass(a, b, ((0,), (0,)))
    copies.append(pltpu.make_async_copy(values, coarse, sem.at[2]))
    copies[-1].start()
    for copy in copies:
        copy.wait()


def call(kernel, name, out_shape, in_specs, out_specs, scratch=(), aliases=None, flops=1, size=1):
    return pl.pallas_call(
        kernel,
        out_shape=out_shape,
        in_specs=in_specs,
        out_specs=out_specs,
        scratch_shapes=list(scratch),
        input_output_aliases=aliases or {},
        compiler_params=pltpu.CompilerParams(vmem_limit_bytes=VMEM_LIMIT),
        cost_estimate=pl.CostEstimate(flops=flops, bytes_accessed=size, transcendentals=0),
        name=name,
    )


ANY = pl.BlockSpec(memory_space=pl.ANY)
HBM = pl.BlockSpec(memory_space=pltpu.HBM)
SMEM = pl.BlockSpec(memory_space=pltpu.SMEM)
VMEM = pl.BlockSpec(memory_space=pltpu.VMEM)


def in_hbm(values):
    return pltpu.with_memory_space_constraint(jnp.asarray(values), pltpu.HBM)


def shape(*dims):
    return jax.ShapeDtypeStruct(dims, jnp.float32)


def on_device(sizes, field):
    gx, gy, gz = sizes
    depth, height, breadth = field.shape
    mz, mx, my = depth // 2, height // 2, breadth // 2
    count = gx * gy * gz
    axes = ("gx", "gy", "gz")
    tx, ty, tz = line_tables(gx, mx), line_tables(gy, my), line_tables(gz, mz)

    def vectors(t, parts, m):
        table = np.zeros((parts, 8, m))
        table[:, 0], table[:, 1] = t["from_left"], t["from_right"]
        return f32(table)

    row_x, row_y = vectors(tx, gx, mx), vectors(ty, gy, my)
    line_y, line_x = np.zeros((gy, breadth + 8, 2 * my)), np.zeros((gx, mx + 16, height))
    line_y[:, :breadth, :my] = ty["block"].transpose(0, 2, 1)
    for out in range(mz + 2):
        line_y[:, :breadth, my + 2 * out], line_y[:, :breadth, my + 2 * out + 1] = ty["to_right"], ty["to_left"]
    line_y[:, 0, my + 2 * (mz + 2) : my + 2 * (mz + 2) + mz] = 1.0
    line_y[:, breadth, :my] = ty["first"]
    line_x[:, :mx], line_x[:, mx], line_x[:, mx + 1] = tx["block"], tx["to_right"], tx["to_left"]
    line_x[:, mx + 8, :mx] = tx["first"]
    fold_z = np.zeros((gz, 8, 128))

    width = max((mz + 2) * (depth + mz) + 2 * gz + 2 * mz, gx, gy)
    scalars = np.zeros((8 * ((gz + 2 + 7) // 8), 128 * ((width + 127) // 128)))
    for p in range(gz):
        full = np.concatenate([tz["block"][p], tz["to_right"][p : p + 1], tz["to_left"][p : p + 1]], axis=0)
        nodes = np.zeros((mz + 2, mz))
        nodes[:mz] = np.eye(mz)
        nodes[:mz, 0] -= tz["first"][p]
        nodes[mz, 0] = tz["first_right"][p]
        ends = [tz[key][p] for key in ("weight_left", "weight_right", "from_left", "from_right")]
        line = np.concatenate([full.reshape(-1), nodes.reshape(-1)] + ends)
        scalars[p, : line.size] = line
        fold_z[p, :depth, : 2 * (mz + 2)] = np.repeat(full.T, 2, axis=1)
        for j in range(mz):
            fold_z[p, 2 * j, 2 * (mz + 2) + j] = 1.0
    scalars[gz, :gx], scalars[gz + 1, :gy] = tx["first_right"], ty["first_right"]
    scalars = f32(scalars)

    vmem = pltpu.VMEM
    operands = (scalars, field, f32(fold_z), f32(line_y), f32(line_x))
    send, own, even, near, far, first, both_far, kept = call(
        functools.partial(local_kernel, sizes),
        "local",
        [shape(count, 4, my), shape(mz, mx, my), shape(mz, mx, my)] + [shape(mx, my)] * 3 + [shape(2, mx, my), shape(*field.shape)],
        [HBM] * 5,
        [VMEM] * 8,
        [
            vmem(line_y.shape[1:], jnp.float32),
            vmem(line_x.shape[1:], jnp.float32),
            vmem(fold_z.shape[1:], jnp.float32),
            vmem((mz, height, my), jnp.float32),
            vmem((height, 128), jnp.float32),
            vmem((27, 4, my), jnp.float32),
            pltpu.SMEM(scalars.shape, jnp.float32),
            pltpu.SemaphoreType.DMA((depth + 4,)),
        ],
    )(*map(in_hbm, operands))
    received = lax.all_to_all(send, axes, 0, 0, tiled=True).reshape(count * 4, my)

    assert gz == 4
    plans = ((near, 1), (far, 2), (both_far, 3), (first, 1))
    gets = [lax.ppermute(plane, "gz", [(i, i ^ hop) for i in range(gz)]) for plane, hop in plans]

    row_z = np.zeros((gz, 16, my))
    for p in range(gz):
        for i, hop in enumerate((1, 2, 3)):
            row_z[p, i], row_z[p, 3 + i] = tz["weight_left"][p, p ^ hop], tz["weight_right"][p, p ^ hop]
        row_z[p, 6], row_z[p, 7] = p ^ 1 == p + 1, p ^ 3 == p + 1
        row_z[p, 8 : 8 + mz] = tz["from_left"][p][:, None]
        row_z[p, 8 + mz : 8 + 2 * mz] = tz["from_right"][p][:, None]
    wx, wy, wz = combine_tables(sizes, tx, ty, tz, mz)
    tables = (row_x, row_y, f32(row_z), wx, wy, wz)
    partial, inner, top, rows, weights, up_x, up_y = call(
        inner_kernel,
        "inner",
        [shape(*field.shape), shape(depth - 1, height, breadth), shape(height, breadth), shape(32, my)]
        + [shape(*wx.shape[1:]), shape(height, mx), shape(my, breadth)],
        [VMEM] * 2 + [HBM] * len(tables),
        [HBM] + [VMEM] * 6,
        [vmem((3, *wx.shape[1:]), jnp.float32), pltpu.SemaphoreType.DMA((depth + len(tables),))],
    )(kept, even, *map(in_hbm, tables))
    got = call(
        gather_kernel,
        "gather",
        shape(wx.shape[1], my),
        [VMEM] * 2,
        VMEM,
        flops=10**10,
        size=10**8,
    )(received, weights)
    return call(
        finish_kernel,
        "finish",
        [shape(*field.shape), shape(mz, mx, my)],
        [VMEM] * 11 + [HBM],
        [HBM, HBM],
        [
            vmem((height, breadth), jnp.float32),
            vmem((depth, height, 128), jnp.float32),
            vmem((depth, 8, breadth - 128), jnp.float32),
            vmem((mz, mx, my), jnp.float32),
            pltpu.SemaphoreType.DMA((3 + 2 * depth,)),
        ],
        {11: 0},
    )(got, rows, up_x, up_y, inner, top, own, *gets, partial)


def solution(mesh):
    sizes = tuple(mesh.shape[axis] for axis in ("gx", "gy", "gz"))
    return jax.shard_map(
        functools.partial(on_device, sizes),
        mesh=mesh,
        in_specs=(P("gz", "gx", "gy"),),
        out_specs=(P("gz", "gx", "gy"), P("gz", "gx", "gy")),
        check_vma=False,
    )
```

```python
import functools

import jax
import jax.numpy as jnp
import numpy as np
from jax import lax
from jax.experimental import pallas as pl
from jax.experimental.pallas import tpu as pltpu
from jax.sharding import PartitionSpec as P

RATIO = 2.0 - np.sqrt(3.0)
VMEM_LIMIT = 48 * 1024 * 1024


def inverse_mass(i, j, n):
    low, high = np.minimum(i, j), np.maximum(i, j)
    sign = np.where((high - low) % 2 == 0, 1.0, -1.0)
    value = RATIO ** (high - low + 1.0) * (1.0 - RATIO ** (2.0 * (low + 1))) * (1.0 - RATIO ** (2.0 * (n - high)))
    return 3.0 * sign * value / ((1.0 - RATIO**2) * (1.0 - RATIO ** (2.0 * (n + 1))))


def line_operator(i, k, n):
    a = k // 2
    odd = k % 2 == 1

    def at(j):
        inside = (j >= 0) & (j < n)
        return np.where(inside, inverse_mass(i, np.clip(j, 0, n - 1), n), 0.0)

    even_part = np.where(a == 0, 9.0, 10.0) * at(a) + at(a - 1) + at(a + 1)
    odd_part = 6.0 * at(a) + 6.0 * at(a + 1)
    return np.where(odd, odd_part, even_part) / 12.0


def line_tables(parts, m):
    n = parts * m
    node, fine = np.arange(m), np.arange(2 * m)
    block = np.zeros((parts, m, 2 * m))
    to_right, to_left = np.zeros((parts, 2 * m)), np.zeros((parts, 2 * m))
    from_left, from_right = np.zeros((parts, m)), np.zeros((parts, m))
    weight_left, weight_right = np.zeros((parts, parts)), np.zeros((parts, parts))
    first = np.zeros((parts, m))
    first_right = np.zeros((parts,))
    for p in range(parts):
        k = p * 2 * m + fine
        block[p] = line_operator((p * m + node)[:, None], k[None, :], n)
        if p + 1 < parts:
            to_right[p] = line_operator(np.full_like(k, (p + 1) * m), k, n)
        if p > 0:
            to_left[p] = line_operator(np.full_like(k, p * m - 1), k, n)
        from_left[p] = (-RATIO) ** node * (1 - RATIO ** (2.0 * (n - p * m - node))) / (1 - RATIO ** (2.0 * (n - p * m)))
        from_right[p] = (
            (-RATIO) ** (m - 1 - node) * (1 - RATIO ** (2.0 * (p * m + node + 1))) / (1 - RATIO ** (2.0 * (p + 1) * m))
        )
        for q in range(parts):
            if q < p:
                weight_left[p, q] = (
                    (-RATIO) ** ((p - q - 1) * m)
                    * (1 - RATIO ** (2.0 * (n - p * m)))
                    / (1 - RATIO ** (2.0 * (n - (q + 1) * m)))
                )
            if q > p:
                weight_right[p, q] = (
                    (-RATIO) ** ((q - p - 1) * m) * (1 - RATIO ** (2.0 * (p + 1) * m)) / (1 - RATIO ** (2.0 * q * m))
                )
    first[0] = inverse_mass(node, np.zeros_like(node), n) / 3.0
    if parts > 1:
        first_right[0] = -inverse_mass(np.array(m), np.array(0), n) / 3.0
    return {
        "block": block,
        "to_right": to_right,
        "to_left": to_left,
        "from_left": from_left,
        "from_right": from_right,
        "weight_left": weight_left,
        "weight_right": weight_right,
        "first": first,
        "first_right": first_right,
    }


def even_selector(m):
    pick = np.zeros((2 * m, m))
    pick[2 * np.arange(m), np.arange(m)] = 1.0
    return pick


def f32(values):
    return np.asarray(values, np.float32)


def combine_tables(sizes, tx, ty, tz, mz):
    gx, gy, gz = sizes
    count = gx * gy * gz
    sender = np.arange(count)
    qx, qy, qz = sender // (gy * gz), (sender // gz) % gy, sender % gz
    rows = 32
    wx, wy, wz = (np.zeros((parts, rows, count, 4)) for parts in sizes)

    def side(t, p, q, which):
        if which == 0:
            return (q == p) * 1.0
        return (t["weight_left"] if which == 1 else t["weight_right"])[p][q]

    for sx in range(3):
        for sy in range(3):
            if sx == 0 and sy == 0:
                continue
            for z in range(mz):
                row = (sx * 3 + sy) * mz + z
                for p in range(gx):
                    wx[p, row] = side(tx, p, qx, sx)[:, None]
                for p in range(gy):
                    wy[p, row] = side(ty, p, qy, sy)[:, None]
                for p in range(gz):
                    wz[p, row, :, z] += qz == p
                    wz[p, row, :, 0] += tz["weight_left"][p][qz] * tz["from_left"][p, z]
                    wz[p, row, :, 0] += tz["weight_right"][p][qz] * tz["from_right"][p, z]
    for case, (ox, oy) in enumerate(((1, 0), (0, 1), (1, 1))):
        for layer in range(mz + 1):
            row = 9 * mz + case * (mz + 1) + layer
            for p in range(gx):
                wx[p, row] = (qx == p + ox)[:, None]
            for p in range(gy):
                wy[p, row] = (qy == p + oy)[:, None]
            for p in range(gz):
                if layer < mz:
                    wz[p, row, :, mz + layer] = qz == p
                else:
                    wz[p, row, :, mz] = qz == p + 1
    return tuple(f32(w.reshape(w.shape[0], rows, count * 4)) for w in (wx, wy, wz))


def split(values):
    high = values.astype(jnp.bfloat16)
    return high, (values - high.astype(jnp.float32)).astype(jnp.bfloat16)


def one_pass(a, b, contract=((1,), (0,))):
    return lax.dot_general(a, b, (contract, ((), ())), preferred_element_type=jnp.float32)


def three_pass(a, b, contract=((1,), (0,))):
    return one_pass(a[0], b[0], contract) + one_pass(a[0], b[1], contract) + one_pass(a[1], b[0], contract)


def two_pass(a, b):
    return one_pass(a[0], b) + one_pass(a[1], b)


def exact_left(a, b):
    high, low = split(b)
    return one_pass(a, high) + one_pass(a, low)


def exact_right(a, b):
    high, low = split(a)
    return one_pass(high, b) + one_pass(low, b)


def start_all(copies):
    for copy in copies:
        copy.start()


def local_kernel(sizes, *refs):
    field, fold_z, line_y, line_x = refs[:4]
    send, own, even, near, far, first, both_far, f = refs[4:12]
    ry, bx, az, picked, column, kinds, sem = refs[12:]
    gx, gy, gz = sizes
    px, py, pz = lax.axis_index("gx"), lax.axis_index("gy"), lax.axis_index("gz")
    depth, height, breadth = field.shape
    mz, mx, my = own.shape
    planes = [pltpu.make_async_copy(field.at[z], f.at[z], sem.at[z]) for z in range(depth)]
    sources = [(fold_z.at[pz], az), (line_y.at[py], ry), (line_x.at[px], bx)]
    tables = [pltpu.make_async_copy(src, dst, sem.at[depth + i]) for i, (src, dst) in enumerate(sources)]
    start_all(tables[:2] + planes + tables[2:])
    kinds[...] = jnp.zeros_like(kinds)
    fine = lax.broadcasted_iota(jnp.int32, (breadth, my), 0)
    node = lax.broadcasted_iota(jnp.int32, (breadth, my), 1)
    pick_y = jnp.where(fine == 2 * node, 1.0, 0.0).astype(jnp.bfloat16)
    tables[0].wait()
    tables[1].wait()
    weights = split(ry[:breadth])
    by_y, evens, along_x = [], [], None
    step = 2
    for start in range(0, depth, step):
        for z in range(start, start + step):
            planes[z].wait()
        part = split(f[start : start + step].reshape(step * height, breadth))
        result = three_pass(part, weights)
        for z in range(start, start + step):
            rows = slice((z - start) * height, (z - start + 1) * height)
            by_y.append(result[rows, :my])
            folded = result[rows, my:] * az[z : z + 1, :]
            along_x = folded if along_x is None else along_x + folded
            if z % 2 == 0:
                j = z // 2
                picked[j] = two_pass((part[0][rows], part[1][rows]), pick_y)
                evens.append(picked[j, pl.ds(0, mx, stride=2), :])
                even[j] = evens[j]
    column[...] = along_x
    edge = jnp.transpose(column[pl.ds(0, mx, stride=2), :])[:16, :]
    for table in tables[2:]:
        table.wait()
    solve_x = split(bx[: mx + 8])
    faces = three_pass(solve_x, split(along_x))
    by_x = jnp.transpose(faces[:mx])[:16, :]
    corners = [faces[mx + ab : mx + ab + 1] for ab in range(2)]
    by_split = split(jnp.concatenate(by_y, axis=1))
    ends_x = three_pass(tuple(half[mx:] for half in solve_x), by_split)
    sums = [[ends_x[ab : ab + 1, z * my : (z + 1) * my] for ab in range(2)] for z in range(depth)]

    first_y, kappa_y = ry[breadth : breadth + 1, :my], ry[breadth + 1 : breadth + 2, :my]
    first_x, kappa_x = bx[mx + 8 : mx + 9, :mx], bx[mx + 9 : mx + 10, :mx]
    outs = mz + 2
    first_rows = jnp.concatenate([evens[j][0:1, :] for j in range(mz)], axis=0)
    first_cols = edge[2 * outs : 2 * outs + mz, :]

    def over_z(base, rows):
        return sum(az[base + 8 * j : base + 8 * j + 8, :] * rows[j] for j in range(len(rows)))

    first_row = over_z(8 + 8 * depth, [first_rows[j : j + 1] for j in range(mz)])
    first_col = over_z(8 + 8 * depth, [first_cols[j : j + 1] for j in range(mz)])
    corner = first_row[:, 0:1]
    lane = lax.broadcasted_iota(jnp.int32, (8, my), 1)
    here = lane == lax.broadcasted_iota(jnp.int32, (8, my), 0)
    ends = [jnp.sum(jnp.where(here, corners[ab], 0.0), axis=1, keepdims=True) for ab in range(2)]
    spread = jnp.zeros((outs, my), jnp.float32)
    chunks = {
        (1, 0): over_z(8, [sums[z][0] for z in range(depth)]) - kappa_x * (first_row - first_y * corner),
        (2, 0): over_z(8, [sums[z][1] for z in range(depth)]),
        (0, 1): by_x[:outs] - (kappa_y * (first_col - first_x * corner))[:outs],
        (0, 2): by_x[outs : 2 * outs],
        (1, 1): spread + ends[0][:outs] - kappa_x * kappa_y * corner[:outs],
        (1, 2): spread + ends[0][outs : 2 * outs],
        (2, 1): spread + ends[1][:outs],
        (2, 2): spread + ends[1][outs : 2 * outs],
    }
    for (sx, sy), rows in chunks.items():
        kind = (sx * 3 + sy) * 3
        kinds[kind, 0:mz, :] = rows[:mz]
        kinds[kind + 1, 0:1, :] = rows[mz : mz + 1]
        kinds[kind + 2, 0:1, :] = rows[mz + 1 : mz + 2]
    for sx in range(3):
        for sy in range(3):
            for sz in range(3):
                kinds[(sx * 3 + sy) * 3 + sz, mz : 2 * mz, :] = first_cols if sx == 0 else first_rows

    def side(there, here):
        return jnp.where(there == here, 0, jnp.where(there > here, 1, 2))

    def scatter(tx, ty, tz, at):
        send[pl.ds(at, 1)] = kinds[pl.ds((side(tx, px) * 3 + side(ty, py)) * 3 + side(tz, pz), 1)]

    if gx * gy * gz <= 32:
        for at in range(gx * gy * gz):
            scatter(at // (gy * gz), (at // gz) % gy, at % gz, at)
    else:

        @pl.loop(0, gx * gy * gz)
        def _(at):
            scatter(at // (gy * gz), (at // gz) % gy, at % gz, at)

    by_all = three_pass(tuple(half[:mx] for half in solve_x), by_split)
    solved = [by_all[:, z * my : (z + 1) * my] for z in range(depth)]
    first_x = jnp.transpose(jnp.broadcast_to(first_x, (8, mx)))[:, 0:1]
    outs = []
    for out in range(mz + 2):
        value = sum(az[8 + 8 * z + out : 9 + 8 * z + out, :] * solved[z] for z in range(depth))
        base = 8 + 8 * depth + out
        part = sum(az[base + 8 * j : base + 8 * j + 1, :] * evens[j] for j in range(mz))
        part = part - first_x * part[0:1, :]
        part = part - part[:, 0:1] * first_y
        outs.append(value - part)
    for j in range(mz):
        own[j] = evens[j] + outs[j]
    near[...] = jnp.where(pz % 2 == 0, outs[mz], outs[mz + 1])
    far[...] = jnp.where(pz % 4 < 2, outs[mz], outs[mz + 1])
    both_far[0] = jnp.where(pz % 4 < 2, outs[mz], outs[mz + 1])
    both_far[1] = evens[0]
    first[...] = evens[0]


def inner_kernel(field, even, *refs):
    tables, (parts, sem) = refs[:6], refs[14:]
    coefficients, c, top, rows, weights, columns, up_x, up_y = refs[6:14]
    px, py, pz = lax.axis_index("gx"), lax.axis_index("gy"), lax.axis_index("gz")
    depth, height, breadth = field.shape
    mz = even.shape[0]
    goals = (rows.at[0:8], rows.at[8:16], rows.at[16:32], parts.at[0], parts.at[1], parts.at[2])
    fetches = [
        pltpu.make_async_copy(table.at[at], goal, sem.at[depth + i])
        for i, (table, at, goal) in enumerate(zip(tables, (px, py, pz) * 2, goals, strict=True))
    ]
    start_all(fetches)
    for up, node_axis in ((up_x, 1), (up_y, 0)):
        node = lax.broadcasted_iota(jnp.int32, up.shape, node_axis)
        away = jnp.abs(lax.broadcasted_iota(jnp.int32, up.shape, 1 - node_axis) - 2 * node)
        up[...] = jnp.where(away == 0, 1.0, jnp.where(away == 1, 0.5, 0.0))
    body = (pl.ds(0, height - 8), pl.ds(0, breadth - 128))
    up_left, up_right = up_x[...].astype(jnp.bfloat16), up_y[...].astype(jnp.bfloat16)
    lifted = [exact_right(exact_left(up_left, even[j]), up_right) for j in range(mz)]
    copies = []
    for z in range(depth - 1):
        j = z // 2
        c[z] = field[z] - (lifted[j] if z % 2 == 0 else 0.5 * (lifted[j] + lifted[j + 1]))
        copies.append(pltpu.make_async_copy(c.at[z, *body], coefficients.at[z, *body], sem.at[z]))
        copies[z].start()
    top[...] = field[depth - 1] - 0.5 * lifted[mz - 1]
    for copy in fetches:
        copy.wait()
    weights[...] = parts[0] * parts[1] * parts[2]
    blank = jnp.zeros((columns.shape[1] - weights.shape[0], weights.shape[1]), jnp.float32)
    columns[...] = jnp.transpose(jnp.concatenate([weights[...], blank], axis=0))
    for copy in copies:
        copy.wait()


def gather_kernel(received, weights, columns, got, got_columns):
    chunks = split(received[...])
    got_columns[...] = three_pass(chunks, split(columns[...]), ((0,), (0,)))
    got[...] = three_pass(split(weights[...]), chunks)


def finish_kernel(*refs):
    got, got_columns, rows, up_x, up_y, inner, top, own, one, two, three, first, partial = refs[:13]
    coefficients, coarse, last_plane, rim, foot, values, sem = refs[13:]
    del partial
    mz, mx, my = own.shape
    depth, height, breadth = 2 * mz, 2 * mx, 2 * my
    split_at = breadth - 128
    body = (pl.ds(0, height - 8), pl.ds(0, split_at))

    def row_at(i):
        return rows[16 + i : 17 + i, :]

    planes = (one[...], two[...], three[0])
    left = sum(row_at(i) * plane for i, plane in enumerate(planes))
    right = sum(row_at(3 + i) * plane for i, plane in enumerate(planes))
    ahead = row_at(6) * first[...] + row_at(7) * three[1]
    up_left, up_right = up_x[...].astype(jnp.bfloat16), up_y[...].astype(jnp.bfloat16)
    last_plane[...] = top[...] - 0.5 * exact_right(exact_left(up_left, ahead), up_right)
    copies = [pltpu.make_async_copy(last_plane.at[body], coefficients.at[depth - 1, *body], sem.at[0])]
    copies[0].start()
    before = [own[j] + row_at(8 + j) * left + row_at(8 + mz + j) * right for j in range(mz)]

    base = 9 * mz
    layers = mz + 1
    halo_x, halo_xy = got[base : base + layers], got[base + 2 * layers : base + 3 * layers]
    pad = jnp.zeros((8 - layers, halo_x.shape[1]), jnp.float32)
    row = exact_right(jnp.concatenate([halo_x, pad], axis=0), up_right)
    col = exact_left(up_left, got_columns[...])[:, base + layers : base + 2 * layers]
    lane = lax.broadcasted_iota(jnp.int32, (1, 128), 1)
    last = lane == 127
    for z in range(depth):
        j = z // 2
        if z % 2 == 0:
            r, s, k = row[j : j + 1], 0.5 * col[:, j : j + 1], halo_xy[j : j + 1, 0:1]
        else:
            r = 0.5 * (row[j : j + 1] + row[j + 1 : j + 2])
            s = 0.25 * (col[:, j : j + 1] + col[:, j + 1 : j + 2])
            k = 0.5 * (halo_xy[j : j + 1, 0:1] + halo_xy[j + 1 : j + 2, 0:1])
        old = inner[z] if z < depth - 1 else last_plane[...]
        rim[z] = old[:, split_at:] - jnp.where(last, s, 0.0)
        end = 0.5 * r[:, split_at:] + jnp.where(last, 0.25 * k, 0.0)
        rim[z, height - 1 : height, :] = rim[z, height - 1 : height, :] - end
        foot[z] = old[height - 8 :, :split_at]
        foot[z, 7:8, :] = old[height - 1 :, :split_at] - 0.5 * r[:, :split_at]
        goal = coefficients.at[z, :, pl.ds(split_at, 128)]
        copies.append(pltpu.make_async_copy(rim.at[z], goal, sem.at[3 + 2 * z]))
        goal = coefficients.at[z, pl.ds(height - 8, 8), pl.ds(0, split_at)]
        copies.append(pltpu.make_async_copy(foot.at[z], goal, sem.at[4 + 2 * z]))
        start_all(copies[-2:])

    ux, vx, uy, vy = rows[0:1], rows[1:2], rows[8:9], rows[9:10]

    def part(sx, sy, z):
        at = (sx * 3 + sy) * mz + z
        return got[at : at + 1]

    for z in range(mz):
        a, b = [], []
        for sy, end in ((1, uy), (2, vy)):
            a.append(part(0, sy, z) + ux * part(1, sy, z)[:, 0:1] + vx * part(2, sy, z)[:, 0:1])
            b.append(end)
        for sx, end in ((1, ux), (2, vx)):
            a.append(end)
            b.append(part(sx, 0, z))
        zero = [jnp.zeros((4, mx), jnp.float32)]
        a, b = split(jnp.concatenate(a + zero, axis=0)), split(jnp.concatenate(b + zero, axis=0))
        values[z] = before[z] + three_pass(a, b, ((0,), (0,)))
    copies.append(pltpu.make_async_copy(values, coarse, sem.at[2]))
    copies[-1].start()
    for copy in copies:
        copy.wait()


def call(kernel, name, out_shape, in_specs, out_specs, scratch=(), aliases=None, flops=1, size=1):
    return pl.pallas_call(
        kernel,
        out_shape=out_shape,
        in_specs=in_specs,
        out_specs=out_specs,
        scratch_shapes=list(scratch),
        input_output_aliases=aliases or {},
        compiler_params=pltpu.CompilerParams(vmem_limit_bytes=VMEM_LIMIT),
        cost_estimate=pl.CostEstimate(flops=flops, bytes_accessed=size, transcendentals=0),
        name=name,
    )


ANY = pl.BlockSpec(memory_space=pl.ANY)
HBM = pl.BlockSpec(memory_space=pltpu.HBM)
SMEM = pl.BlockSpec(memory_space=pltpu.SMEM)
VMEM = pl.BlockSpec(memory_space=pltpu.VMEM)


def in_hbm(values):
    return pltpu.with_memory_space_constraint(jnp.asarray(values), pltpu.HBM)


def shape(*dims):
    return jax.ShapeDtypeStruct(dims, jnp.float32)


def on_device(sizes, field):
    gx, gy, gz = sizes
    depth, height, breadth = field.shape
    mz, mx, my = depth // 2, height // 2, breadth // 2
    count = gx * gy * gz
    axes = ("gx", "gy", "gz")
    tx, ty, tz = line_tables(gx, mx), line_tables(gy, my), line_tables(gz, mz)

    def vectors(t, parts, m):
        table = np.zeros((parts, 8, m))
        table[:, 0], table[:, 1] = t["from_left"], t["from_right"]
        return f32(table)

    row_x, row_y = vectors(tx, gx, mx), vectors(ty, gy, my)
    line_y, line_x = np.zeros((gy, breadth + 8, 2 * my)), np.zeros((gx, mx + 16, height))
    line_y[:, :breadth, :my] = ty["block"].transpose(0, 2, 1)
    outs = mz + 2
    line_y[:, :breadth, my : my + outs] = ty["to_right"][..., None]
    line_y[:, :breadth, my + outs : my + 2 * outs] = ty["to_left"][..., None]
    line_y[:, 0, my + 2 * (mz + 2) : my + 2 * (mz + 2) + mz] = 1.0
    line_y[:, breadth, :my], line_y[:, breadth + 1, :my] = ty["first"], ty["first_right"][:, None]
    line_x[:, :mx], line_x[:, mx], line_x[:, mx + 1] = tx["block"], tx["to_right"], tx["to_left"]
    line_x[:, mx + 8, :mx], line_x[:, mx + 9, :mx] = tx["first"], tx["first_right"][:, None]

    fold_z = np.zeros((gz, 8 + 8 * (depth + mz), my))
    for p in range(gz):
        full = np.concatenate([tz["block"][p], tz["to_right"][p : p + 1], tz["to_left"][p : p + 1]], axis=0)
        nodes = np.zeros((outs, mz))
        nodes[:mz] = np.eye(mz)
        nodes[:mz, 0] -= tz["first"][p]
        nodes[mz, 0] = tz["first_right"][p]
        fold_z[p, :depth, : 2 * outs] = np.tile(full.T, 2)
        for j in range(mz):
            fold_z[p, 2 * j, 2 * outs + j] = 1.0
        for z in range(depth):
            fold_z[p, 8 + 8 * z : 8 + 8 * z + outs] = full[:, z : z + 1]
        for j in range(mz):
            base = 8 + 8 * (depth + j)
            fold_z[p, base : base + outs] = nodes[:, j : j + 1]

    vmem = pltpu.VMEM
    operands = (field, f32(fold_z), f32(line_y), f32(line_x))
    send, own, even, near, far, first, both_far, kept = call(
        functools.partial(local_kernel, sizes),
        "local",
        [shape(count, 4, my), shape(mz, mx, my), shape(mz, mx, my)] + [shape(mx, my)] * 3 + [shape(2, mx, my), shape(*field.shape)],
        [HBM] * 4,
        [VMEM] * 8,
        [
            vmem(line_y.shape[1:], jnp.float32),
            vmem(line_x.shape[1:], jnp.float32),
            vmem(fold_z.shape[1:], jnp.float32),
            vmem((mz, height, my), jnp.float32),
            vmem((height, 128), jnp.float32),
            vmem((27, 4, my), jnp.float32),
            pltpu.SemaphoreType.DMA((depth + 3,)),
        ],
    )(*map(in_hbm, operands))
    received = lax.all_to_all(send, axes, 0, 0, tiled=True).reshape(count * 4, my)

    assert gz == 4
    plans = ((near, 1), (far, 2), (both_far, 3), (first, 1))
    gets = [lax.ppermute(plane, "gz", [(i, i ^ hop) for i in range(gz)]) for plane, hop in plans]

    row_z = np.zeros((gz, 16, my))
    for p in range(gz):
        for i, hop in enumerate((1, 2, 3)):
            row_z[p, i], row_z[p, 3 + i] = tz["weight_left"][p, p ^ hop], tz["weight_right"][p, p ^ hop]
        row_z[p, 6], row_z[p, 7] = p ^ 1 == p + 1, p ^ 3 == p + 1
        row_z[p, 8 : 8 + mz] = tz["from_left"][p][:, None]
        row_z[p, 8 + mz : 8 + 2 * mz] = tz["from_right"][p][:, None]
    wx, wy, wz = combine_tables(sizes, tx, ty, tz, mz)
    tables = (row_x, row_y, f32(row_z), wx, wy, wz)
    partial, inner, top, rows, weights, columns, up_x, up_y = call(
        inner_kernel,
        "inner",
        [shape(*field.shape), shape(depth - 1, height, breadth), shape(height, breadth), shape(32, my)]
        + [shape(*wx.shape[1:]), shape(count * 4, 128), shape(height, mx), shape(my, breadth)],
        [VMEM] * 2 + [HBM] * len(tables),
        [HBM] + [VMEM] * 7,
        [vmem((3, *wx.shape[1:]), jnp.float32), pltpu.SemaphoreType.DMA((depth + len(tables),))],
    )(kept, even, *map(in_hbm, tables))
    got, got_columns = call(
        gather_kernel,
        "gather",
        [shape(wx.shape[1], my), shape(mx, 128)],
        [VMEM] * 3,
        [VMEM] * 2,
        flops=10**10,
        size=10**8,
    )(received, weights, columns)
    return call(
        finish_kernel,
        "finish",
        [shape(*field.shape), shape(mz, mx, my)],
        [VMEM] * 12 + [HBM],
        [HBM, HBM],
        [
            vmem((height, breadth), jnp.float32),
            vmem((depth, height, 128), jnp.float32),
            vmem((depth, 8, breadth - 128), jnp.float32),
            vmem((mz, mx, my), jnp.float32),
            pltpu.SemaphoreType.DMA((3 + 2 * depth,)),
        ],
        {12: 0},
    )(got, got_columns, rows, up_x, up_y, inner, top, own, *gets, partial)


def solution(mesh):
    sizes = tuple(mesh.shape[axis] for axis in ("gx", "gy", "gz"))
    return jax.shard_map(
        functools.partial(on_device, sizes),
        mesh=mesh,
        in_specs=(P("gz", "gx", "gy"),),
        out_specs=(P("gz", "gx", "gy"), P("gz", "gx", "gy")),
        check_vma=False,
    )
```

```python
import functools

import jax
import jax.numpy as jnp
import numpy as np
from jax import lax
from jax.experimental import pallas as pl
from jax.experimental.pallas import tpu as pltpu
from jax.sharding import PartitionSpec as P

RATIO = 2.0 - np.sqrt(3.0)
VMEM_LIMIT = 48 * 1024 * 1024


def inverse_mass(i, j, n):
    low, high = np.minimum(i, j), np.maximum(i, j)
    sign = np.where((high - low) % 2 == 0, 1.0, -1.0)
    value = RATIO ** (high - low + 1.0) * (1.0 - RATIO ** (2.0 * (low + 1))) * (1.0 - RATIO ** (2.0 * (n - high)))
    return 3.0 * sign * value / ((1.0 - RATIO**2) * (1.0 - RATIO ** (2.0 * (n + 1))))


def line_operator(i, k, n):
    a = k // 2
    odd = k % 2 == 1

    def at(j):
        inside = (j >= 0) & (j < n)
        return np.where(inside, inverse_mass(i, np.clip(j, 0, n - 1), n), 0.0)

    even_part = np.where(a == 0, 9.0, 10.0) * at(a) + at(a - 1) + at(a + 1)
    odd_part = 6.0 * at(a) + 6.0 * at(a + 1)
    return np.where(odd, odd_part, even_part) / 12.0


def line_tables(parts, m):
    n = parts * m
    node, fine = np.arange(m), np.arange(2 * m)
    block = np.zeros((parts, m, 2 * m))
    to_right, to_left = np.zeros((parts, 2 * m)), np.zeros((parts, 2 * m))
    from_left, from_right = np.zeros((parts, m)), np.zeros((parts, m))
    weight_left, weight_right = np.zeros((parts, parts)), np.zeros((parts, parts))
    first = np.zeros((parts, m))
    first_right = np.zeros((parts,))
    for p in range(parts):
        k = p * 2 * m + fine
        block[p] = line_operator((p * m + node)[:, None], k[None, :], n)
        if p + 1 < parts:
            to_right[p] = line_operator(np.full_like(k, (p + 1) * m), k, n)
        if p > 0:
            to_left[p] = line_operator(np.full_like(k, p * m - 1), k, n)
        from_left[p] = (-RATIO) ** node * (1 - RATIO ** (2.0 * (n - p * m - node))) / (1 - RATIO ** (2.0 * (n - p * m)))
        from_right[p] = (
            (-RATIO) ** (m - 1 - node) * (1 - RATIO ** (2.0 * (p * m + node + 1))) / (1 - RATIO ** (2.0 * (p + 1) * m))
        )
        for q in range(parts):
            if q < p:
                weight_left[p, q] = (
                    (-RATIO) ** ((p - q - 1) * m)
                    * (1 - RATIO ** (2.0 * (n - p * m)))
                    / (1 - RATIO ** (2.0 * (n - (q + 1) * m)))
                )
            if q > p:
                weight_right[p, q] = (
                    (-RATIO) ** ((q - p - 1) * m) * (1 - RATIO ** (2.0 * (p + 1) * m)) / (1 - RATIO ** (2.0 * q * m))
                )
    first[0] = inverse_mass(node, np.zeros_like(node), n) / 3.0
    if parts > 1:
        first_right[0] = -inverse_mass(np.array(m), np.array(0), n) / 3.0
    return {
        "block": block,
        "to_right": to_right,
        "to_left": to_left,
        "from_left": from_left,
        "from_right": from_right,
        "weight_left": weight_left,
        "weight_right": weight_right,
        "first": first,
        "first_right": first_right,
    }


def even_selector(m):
    pick = np.zeros((2 * m, m))
    pick[2 * np.arange(m), np.arange(m)] = 1.0
    return pick


def f32(values):
    return np.asarray(values, np.float32)


def combine_tables(sizes, tx, ty, tz, mz):
    gx, gy, gz = sizes
    count = gx * gy * gz
    sender = np.arange(count)
    qx, qy, qz = sender // (gy * gz), (sender // gz) % gy, sender % gz
    rows = 32
    wx, wy, wz = (np.zeros((parts, rows, count, 4)) for parts in sizes)

    def side(t, p, q, which):
        if which == 0:
            return (q == p) * 1.0
        return (t["weight_left"] if which == 1 else t["weight_right"])[p][q]

    for sx in range(3):
        for sy in range(3):
            if sx == 0 and sy == 0:
                continue
            for z in range(mz):
                row = (sx * 3 + sy) * mz + z
                for p in range(gx):
                    wx[p, row] = side(tx, p, qx, sx)[:, None]
                for p in range(gy):
                    wy[p, row] = side(ty, p, qy, sy)[:, None]
                for p in range(gz):
                    wz[p, row, :, z] += qz == p
                    wz[p, row, :, 0] += tz["weight_left"][p][qz] * tz["from_left"][p, z]
                    wz[p, row, :, 0] += tz["weight_right"][p][qz] * tz["from_right"][p, z]
    for case, (ox, oy) in enumerate(((1, 0), (0, 1), (1, 1))):
        for layer in range(mz + 1):
            row = 9 * mz + case * (mz + 1) + layer
            for p in range(gx):
                wx[p, row] = (qx == p + ox)[:, None]
            for p in range(gy):
                wy[p, row] = (qy == p + oy)[:, None]
            for p in range(gz):
                if layer < mz:
                    wz[p, row, :, mz + layer] = qz == p
                else:
                    wz[p, row, :, mz] = qz == p + 1
    return tuple(f32(w.reshape(w.shape[0], rows, count * 4)) for w in (wx, wy, wz))


def split(values):
    high = values.astype(jnp.bfloat16)
    return high, (values - high.astype(jnp.float32)).astype(jnp.bfloat16)


def one_pass(a, b, contract=((1,), (0,))):
    return lax.dot_general(a, b, (contract, ((), ())), preferred_element_type=jnp.float32)


def three_pass(a, b, contract=((1,), (0,))):
    return one_pass(a[0], b[0], contract) + one_pass(a[0], b[1], contract) + one_pass(a[1], b[0], contract)


def two_pass(a, b):
    return one_pass(a[0], b) + one_pass(a[1], b)


def exact_left(a, b):
    high, low = split(b)
    return one_pass(a, high) + one_pass(a, low)


def exact_right(a, b):
    high, low = split(a)
    return one_pass(high, b) + one_pass(low, b)


def start_all(copies):
    for copy in copies:
        copy.start()


def local_kernel(sizes, *refs):
    field, fold_z, line_y, line_x = refs[:4]
    send, own, even, near, far, first, f = refs[4:11]
    ry, bx, az, picked, column, kinds, sem = refs[11:]
    gx, gy, gz = sizes
    px, py, pz = lax.axis_index("gx"), lax.axis_index("gy"), lax.axis_index("gz")
    depth, height, breadth = field.shape
    mz, mx, my = own.shape
    planes = [pltpu.make_async_copy(field.at[z], f.at[z], sem.at[z]) for z in range(depth)]
    sources = [(fold_z.at[pz], az), (line_y.at[py], ry), (line_x.at[px], bx)]
    tables = [pltpu.make_async_copy(src, dst, sem.at[depth + i]) for i, (src, dst) in enumerate(sources)]
    start_all(tables[:2] + planes + tables[2:])
    kinds[...] = jnp.zeros_like(kinds)
    fine = lax.broadcasted_iota(jnp.int32, (breadth, my), 0)
    node = lax.broadcasted_iota(jnp.int32, (breadth, my), 1)
    pick_y = jnp.where(fine == 2 * node, 1.0, 0.0).astype(jnp.bfloat16)
    tables[0].wait()
    tables[1].wait()
    weights = split(ry[:breadth])
    by_y, evens, along_x = [], [], None
    step = 2
    for start in range(0, depth, step):
        for z in range(start, start + step):
            planes[z].wait()
        part = split(f[start : start + step].reshape(step * height, breadth))
        result = three_pass(part, weights)
        for z in range(start, start + step):
            rows = slice((z - start) * height, (z - start + 1) * height)
            by_y.append(result[rows, :my])
            folded = result[rows, my:] * az[z : z + 1, :]
            along_x = folded if along_x is None else along_x + folded
            if z % 2 == 0:
                j = z // 2
                picked[j] = two_pass((part[0][rows], part[1][rows]), pick_y)
                evens.append(picked[j, pl.ds(0, mx, stride=2), :])
                even[j] = evens[j]
    column[...] = along_x
    edge = jnp.transpose(column[pl.ds(0, mx, stride=2), :])[:16, :]
    for table in tables[2:]:
        table.wait()
    solve_x = split(bx[: mx + 8])
    faces = three_pass(solve_x, split(along_x))
    by_x = jnp.transpose(faces[:mx])[:16, :]
    corners = [faces[mx + ab : mx + ab + 1] for ab in range(2)]
    by_split = split(jnp.concatenate(by_y, axis=1))
    ends_x = three_pass(tuple(half[mx:] for half in solve_x), by_split)
    sums = [[ends_x[ab : ab + 1, z * my : (z + 1) * my] for ab in range(2)] for z in range(depth)]

    first_y, kappa_y = ry[breadth : breadth + 1, :my], ry[breadth + 1 : breadth + 2, :my]
    first_x, kappa_x = bx[mx + 8 : mx + 9, :mx], bx[mx + 9 : mx + 10, :mx]
    outs = mz + 2
    first_rows = jnp.concatenate([evens[j][0:1, :] for j in range(mz)], axis=0)
    first_cols = edge[2 * outs : 2 * outs + mz, :]

    def over_z(base, rows):
        return sum(az[base + 8 * j : base + 8 * j + 8, :] * rows[j] for j in range(len(rows)))

    first_row = over_z(8 + 8 * depth, [first_rows[j : j + 1] for j in range(mz)])
    first_col = over_z(8 + 8 * depth, [first_cols[j : j + 1] for j in range(mz)])
    corner = first_row[:, 0:1]
    lane = lax.broadcasted_iota(jnp.int32, (8, my), 1)
    here = lane == lax.broadcasted_iota(jnp.int32, (8, my), 0)
    ends = [jnp.sum(jnp.where(here, corners[ab], 0.0), axis=1, keepdims=True) for ab in range(2)]
    spread = jnp.zeros((outs, my), jnp.float32)
    chunks = {
        (1, 0): over_z(8, [sums[z][0] for z in range(depth)]) - kappa_x * (first_row - first_y * corner),
        (2, 0): over_z(8, [sums[z][1] for z in range(depth)]),
        (0, 1): by_x[:outs] - (kappa_y * (first_col - first_x * corner))[:outs],
        (0, 2): by_x[outs : 2 * outs],
        (1, 1): spread + ends[0][:outs] - kappa_x * kappa_y * corner[:outs],
        (1, 2): spread + ends[0][outs : 2 * outs],
        (2, 1): spread + ends[1][:outs],
        (2, 2): spread + ends[1][outs : 2 * outs],
    }
    for (sx, sy), rows in chunks.items():
        kind = (sx * 3 + sy) * 3
        kinds[kind, 0:mz, :] = rows[:mz]
        kinds[kind + 1, 0:1, :] = rows[mz : mz + 1]
        kinds[kind + 2, 0:1, :] = rows[mz + 1 : mz + 2]
    for sx in range(3):
        for sy in range(3):
            for sz in range(3):
                kinds[(sx * 3 + sy) * 3 + sz, mz : 2 * mz, :] = first_cols if sx == 0 else first_rows

    def side(there, here):
        return jnp.where(there == here, 0, jnp.where(there > here, 1, 2))

    def scatter(tx, ty, tz, at):
        send[pl.ds(at, 1)] = kinds[pl.ds((side(tx, px) * 3 + side(ty, py)) * 3 + side(tz, pz), 1)]

    if gx * gy * gz <= 32:
        for at in range(gx * gy * gz):
            scatter(at // (gy * gz), (at // gz) % gy, at % gz, at)
    else:

        @pl.loop(0, gx * gy * gz)
        def _(at):
            scatter(at // (gy * gz), (at // gz) % gy, at % gz, at)

    by_all = three_pass(tuple(half[:mx] for half in solve_x), by_split)
    solved = [by_all[:, z * my : (z + 1) * my] for z in range(depth)]
    first_x = jnp.transpose(jnp.broadcast_to(first_x, (8, mx)))[:, 0:1]
    outs = []
    for out in range(mz + 2):
        value = sum(az[8 + 8 * z + out : 9 + 8 * z + out, :] * solved[z] for z in range(depth))
        base = 8 + 8 * depth + out
        part = sum(az[base + 8 * j : base + 8 * j + 1, :] * evens[j] for j in range(mz))
        part = part - first_x * part[0:1, :]
        part = part - part[:, 0:1] * first_y
        outs.append(value - part)
    for j in range(mz):
        own[j] = evens[j] + outs[j]
    near[...] = jnp.where(pz % 2 == 0, outs[mz], outs[mz + 1])
    far[...] = jnp.where(pz % 4 < 2, outs[mz], outs[mz + 1])
    first[...] = evens[0]


def inner_kernel(field, even, *refs):
    tables, (parts, sem) = refs[:6], refs[14:]
    coefficients, c, top, rows, weights, columns, up_x, up_y = refs[6:14]
    px, py, pz = lax.axis_index("gx"), lax.axis_index("gy"), lax.axis_index("gz")
    depth, height, breadth = field.shape
    mz = even.shape[0]
    goals = (rows.at[0:8], rows.at[8:16], rows.at[16:32], parts.at[0], parts.at[1], parts.at[2])
    fetches = [
        pltpu.make_async_copy(table.at[at], goal, sem.at[depth + i])
        for i, (table, at, goal) in enumerate(zip(tables, (px, py, pz) * 2, goals, strict=True))
    ]
    start_all(fetches)
    for up, node_axis in ((up_x, 1), (up_y, 0)):
        node = lax.broadcasted_iota(jnp.int32, up.shape, node_axis)
        away = jnp.abs(lax.broadcasted_iota(jnp.int32, up.shape, 1 - node_axis) - 2 * node)
        up[...] = jnp.where(away == 0, 1.0, jnp.where(away == 1, 0.5, 0.0))
    body = (pl.ds(0, height - 8), pl.ds(0, breadth - 128))
    up_left, up_right = up_x[...].astype(jnp.bfloat16), up_y[...].astype(jnp.bfloat16)
    lifted = [exact_right(exact_left(up_left, even[j]), up_right) for j in range(mz)]
    copies = []
    for z in range(depth - 1):
        j = z // 2
        c[z] = field[z] - (lifted[j] if z % 2 == 0 else 0.5 * (lifted[j] + lifted[j + 1]))
        copies.append(pltpu.make_async_copy(c.at[z, *body], coefficients.at[z, *body], sem.at[z]))
        copies[z].start()
    top[...] = field[depth - 1] - 0.5 * lifted[mz - 1]
    for copy in fetches:
        copy.wait()
    weights[...] = parts[0] * parts[1] * parts[2]
    blank = jnp.zeros((columns.shape[1] - weights.shape[0], weights.shape[1]), jnp.float32)
    columns[...] = jnp.transpose(jnp.concatenate([weights[...], blank], axis=0))
    for copy in copies:
        copy.wait()


def gather_kernel(received, weights, columns, got, got_columns):
    chunks = split(received[...])
    got_columns[...] = three_pass(chunks, split(columns[...]), ((0,), (0,)))
    got[...] = three_pass(split(weights[...]), chunks)


def finish_kernel(*refs):
    got, got_columns, rows, up_x, up_y, inner, top, own, one, two, three, first, first_far, partial = refs[:14]
    coefficients, coarse, last_plane, rim, foot, values, sem = refs[14:]
    del partial
    mz, mx, my = own.shape
    depth, height, breadth = 2 * mz, 2 * mx, 2 * my
    split_at = breadth - 128
    body = (pl.ds(0, height - 8), pl.ds(0, split_at))

    def row_at(i):
        return rows[16 + i : 17 + i, :]

    planes = (one[...], two[...], three[...])
    left = sum(row_at(i) * plane for i, plane in enumerate(planes))
    right = sum(row_at(3 + i) * plane for i, plane in enumerate(planes))
    ahead = row_at(6) * first[...] + row_at(7) * first_far[...]
    up_left, up_right = up_x[...].astype(jnp.bfloat16), up_y[...].astype(jnp.bfloat16)
    last_plane[...] = top[...] - 0.5 * exact_right(exact_left(up_left, ahead), up_right)
    copies = [pltpu.make_async_copy(last_plane.at[body], coefficients.at[depth - 1, *body], sem.at[0])]
    copies[0].start()
    before = [own[j] + row_at(8 + j) * left + row_at(8 + mz + j) * right for j in range(mz)]

    base = 9 * mz
    layers = mz + 1
    halo_x, halo_xy = got[base : base + layers], got[base + 2 * layers : base + 3 * layers]
    pad = jnp.zeros((8 - layers, halo_x.shape[1]), jnp.float32)
    row = exact_right(jnp.concatenate([halo_x, pad], axis=0), up_right)
    col = exact_left(up_left, got_columns[...])[:, base + layers : base + 2 * layers]
    lane = lax.broadcasted_iota(jnp.int32, (1, 128), 1)
    last = lane == 127
    for z in range(depth):
        j = z // 2
        if z % 2 == 0:
            r, s, k = row[j : j + 1], 0.5 * col[:, j : j + 1], halo_xy[j : j + 1, 0:1]
        else:
            r = 0.5 * (row[j : j + 1] + row[j + 1 : j + 2])
            s = 0.25 * (col[:, j : j + 1] + col[:, j + 1 : j + 2])
            k = 0.5 * (halo_xy[j : j + 1, 0:1] + halo_xy[j + 1 : j + 2, 0:1])
        old = inner[z] if z < depth - 1 else last_plane[...]
        rim[z] = old[:, split_at:] - jnp.where(last, s, 0.0)
        end = 0.5 * r[:, split_at:] + jnp.where(last, 0.25 * k, 0.0)
        rim[z, height - 1 : height, :] = rim[z, height - 1 : height, :] - end
        foot[z] = old[height - 8 :, :split_at]
        foot[z, 7:8, :] = old[height - 1 :, :split_at] - 0.5 * r[:, :split_at]
        goal = coefficients.at[z, :, pl.ds(split_at, 128)]
        copies.append(pltpu.make_async_copy(rim.at[z], goal, sem.at[3 + 2 * z]))
        goal = coefficients.at[z, pl.ds(height - 8, 8), pl.ds(0, split_at)]
        copies.append(pltpu.make_async_copy(foot.at[z], goal, sem.at[4 + 2 * z]))
        start_all(copies[-2:])

    ux, vx, uy, vy = rows[0:1], rows[1:2], rows[8:9], rows[9:10]

    def part(sx, sy, z):
        at = (sx * 3 + sy) * mz + z
        return got[at : at + 1]

    for z in range(mz):
        a, b = [], []
        for sy, end in ((1, uy), (2, vy)):
            a.append(part(0, sy, z) + ux * part(1, sy, z)[:, 0:1] + vx * part(2, sy, z)[:, 0:1])
            b.append(end)
        for sx, end in ((1, ux), (2, vx)):
            a.append(end)
            b.append(part(sx, 0, z))
        zero = [jnp.zeros((4, mx), jnp.float32)]
        a, b = split(jnp.concatenate(a + zero, axis=0)), split(jnp.concatenate(b + zero, axis=0))
        values[z] = before[z] + three_pass(a, b, ((0,), (0,)))
    copies.append(pltpu.make_async_copy(values, coarse, sem.at[2]))
    copies[-1].start()
    for copy in copies:
        copy.wait()


def call(kernel, name, out_shape, in_specs, out_specs, scratch=(), aliases=None, flops=1, size=1):
    return pl.pallas_call(
        kernel,
        out_shape=out_shape,
        in_specs=in_specs,
        out_specs=out_specs,
        scratch_shapes=list(scratch),
        input_output_aliases=aliases or {},
        compiler_params=pltpu.CompilerParams(vmem_limit_bytes=VMEM_LIMIT),
        cost_estimate=pl.CostEstimate(flops=flops, bytes_accessed=size, transcendentals=0),
        name=name,
    )


ANY = pl.BlockSpec(memory_space=pl.ANY)
HBM = pl.BlockSpec(memory_space=pltpu.HBM)
SMEM = pl.BlockSpec(memory_space=pltpu.SMEM)
VMEM = pl.BlockSpec(memory_space=pltpu.VMEM)


def in_hbm(values):
    return pltpu.with_memory_space_constraint(jnp.asarray(values), pltpu.HBM)


def shape(*dims):
    return jax.ShapeDtypeStruct(dims, jnp.float32)


def on_device(sizes, field):
    gx, gy, gz = sizes
    depth, height, breadth = field.shape
    mz, mx, my = depth // 2, height // 2, breadth // 2
    count = gx * gy * gz
    axes = ("gx", "gy", "gz")
    tx, ty, tz = line_tables(gx, mx), line_tables(gy, my), line_tables(gz, mz)

    def vectors(t, parts, m):
        table = np.zeros((parts, 8, m))
        table[:, 0], table[:, 1] = t["from_left"], t["from_right"]
        return f32(table)

    row_x, row_y = vectors(tx, gx, mx), vectors(ty, gy, my)
    line_y, line_x = np.zeros((gy, breadth + 8, 2 * my)), np.zeros((gx, mx + 16, height))
    line_y[:, :breadth, :my] = ty["block"].transpose(0, 2, 1)
    outs = mz + 2
    line_y[:, :breadth, my : my + outs] = ty["to_right"][..., None]
    line_y[:, :breadth, my + outs : my + 2 * outs] = ty["to_left"][..., None]
    line_y[:, 0, my + 2 * (mz + 2) : my + 2 * (mz + 2) + mz] = 1.0
    line_y[:, breadth, :my], line_y[:, breadth + 1, :my] = ty["first"], ty["first_right"][:, None]
    line_x[:, :mx], line_x[:, mx], line_x[:, mx + 1] = tx["block"], tx["to_right"], tx["to_left"]
    line_x[:, mx + 8, :mx], line_x[:, mx + 9, :mx] = tx["first"], tx["first_right"][:, None]

    fold_z = np.zeros((gz, 8 + 8 * (depth + mz), my))
    for p in range(gz):
        full = np.concatenate([tz["block"][p], tz["to_right"][p : p + 1], tz["to_left"][p : p + 1]], axis=0)
        nodes = np.zeros((outs, mz))
        nodes[:mz] = np.eye(mz)
        nodes[:mz, 0] -= tz["first"][p]
        nodes[mz, 0] = tz["first_right"][p]
        fold_z[p, :depth, : 2 * outs] = np.tile(full.T, 2)
        for j in range(mz):
            fold_z[p, 2 * j, 2 * outs + j] = 1.0
        for z in range(depth):
            fold_z[p, 8 + 8 * z : 8 + 8 * z + outs] = full[:, z : z + 1]
        for j in range(mz):
            base = 8 + 8 * (depth + j)
            fold_z[p, base : base + outs] = nodes[:, j : j + 1]

    vmem = pltpu.VMEM
    operands = (field, f32(fold_z), f32(line_y), f32(line_x))
    send, own, even, near, far, first, kept = call(
        functools.partial(local_kernel, sizes),
        "local",
        [shape(count, 4, my), shape(mz, mx, my), shape(mz, mx, my)] + [shape(mx, my)] * 3 + [shape(*field.shape)],
        [HBM] * 4,
        [VMEM] * 7,
        [
            vmem(line_y.shape[1:], jnp.float32),
            vmem(line_x.shape[1:], jnp.float32),
            vmem(fold_z.shape[1:], jnp.float32),
            vmem((mz, height, my), jnp.float32),
            vmem((height, 128), jnp.float32),
            vmem((27, 4, my), jnp.float32),
            pltpu.SemaphoreType.DMA((depth + 3,)),
        ],
    )(*map(in_hbm, operands))
    received = lax.all_to_all(send, axes, 0, 0, tiled=True).reshape(count * 4, my)

    assert gz == 4

    def exchange(plane, hop):
        return lax.ppermute(plane, "gz", [(i, i ^ hop) for i in range(gz)])

    from_far = exchange(far, 3)
    gets = (exchange(near, 1), exchange(from_far, 1), from_far, exchange(first, 1), exchange(first, 3))

    row_z = np.zeros((gz, 16, my))
    for p in range(gz):
        for i, hop in enumerate((1, 2, 3)):
            row_z[p, i], row_z[p, 3 + i] = tz["weight_left"][p, p ^ hop], tz["weight_right"][p, p ^ hop]
        row_z[p, 6], row_z[p, 7] = p ^ 1 == p + 1, p ^ 3 == p + 1
        row_z[p, 8 : 8 + mz] = tz["from_left"][p][:, None]
        row_z[p, 8 + mz : 8 + 2 * mz] = tz["from_right"][p][:, None]
    wx, wy, wz = combine_tables(sizes, tx, ty, tz, mz)
    tables = (row_x, row_y, f32(row_z), wx, wy, wz)
    partial, inner, top, rows, weights, columns, up_x, up_y = call(
        inner_kernel,
        "inner",
        [shape(*field.shape), shape(depth - 1, height, breadth), shape(height, breadth), shape(32, my)]
        + [shape(*wx.shape[1:]), shape(count * 4, 128), shape(height, mx), shape(my, breadth)],
        [VMEM] * 2 + [HBM] * len(tables),
        [HBM] + [VMEM] * 7,
        [vmem((3, *wx.shape[1:]), jnp.float32), pltpu.SemaphoreType.DMA((depth + len(tables),))],
    )(kept, even, *map(in_hbm, tables))
    got, got_columns = call(
        gather_kernel,
        "gather",
        [shape(wx.shape[1], my), shape(mx, 128)],
        [VMEM] * 3,
        [VMEM] * 2,
        flops=10**10,
        size=10**8,
    )(received, weights, columns)
    return call(
        finish_kernel,
        "finish",
        [shape(*field.shape), shape(mz, mx, my)],
        [VMEM] * 13 + [HBM],
        [HBM, HBM],
        [
            vmem((height, breadth), jnp.float32),
            vmem((depth, height, 128), jnp.float32),
            vmem((depth, 8, breadth - 128), jnp.float32),
            vmem((mz, mx, my), jnp.float32),
            pltpu.SemaphoreType.DMA((3 + 2 * depth,)),
        ],
        {13: 0},
    )(got, got_columns, rows, up_x, up_y, inner, top, own, *gets, partial)


def solution(mesh):
    sizes = tuple(mesh.shape[axis] for axis in ("gx", "gy", "gz"))
    return jax.shard_map(
        functools.partial(on_device, sizes),
        mesh=mesh,
        in_specs=(P("gz", "gx", "gy"),),
        out_specs=(P("gz", "gx", "gy"), P("gz", "gx", "gy")),
        check_vma=False,
    )
```

```python
import functools

import jax
import jax.numpy as jnp
import numpy as np
from jax import lax
from jax.experimental import pallas as pl
from jax.experimental.pallas import tpu as pltpu
from jax.sharding import PartitionSpec as P

RATIO = 2.0 - np.sqrt(3.0)
VMEM_LIMIT = 48 * 1024 * 1024


def inverse_mass(i, j, n):
    low, high = np.minimum(i, j), np.maximum(i, j)
    sign = np.where((high - low) % 2 == 0, 1.0, -1.0)
    value = RATIO ** (high - low + 1.0) * (1.0 - RATIO ** (2.0 * (low + 1))) * (1.0 - RATIO ** (2.0 * (n - high)))
    return 3.0 * sign * value / ((1.0 - RATIO**2) * (1.0 - RATIO ** (2.0 * (n + 1))))


def line_operator(i, k, n):
    a = k // 2
    odd = k % 2 == 1

    def at(j):
        inside = (j >= 0) & (j < n)
        return np.where(inside, inverse_mass(i, np.clip(j, 0, n - 1), n), 0.0)

    even_part = np.where(a == 0, 9.0, 10.0) * at(a) + at(a - 1) + at(a + 1)
    odd_part = 6.0 * at(a) + 6.0 * at(a + 1)
    return np.where(odd, odd_part, even_part) / 12.0


def line_tables(parts, m):
    n = parts * m
    node, fine = np.arange(m), np.arange(2 * m)
    block = np.zeros((parts, m, 2 * m))
    to_right, to_left = np.zeros((parts, 2 * m)), np.zeros((parts, 2 * m))
    from_left, from_right = np.zeros((parts, m)), np.zeros((parts, m))
    weight_left, weight_right = np.zeros((parts, parts)), np.zeros((parts, parts))
    first = np.zeros((parts, m))
    first_right = np.zeros((parts,))
    for p in range(parts):
        k = p * 2 * m + fine
        block[p] = line_operator((p * m + node)[:, None], k[None, :], n)
        if p + 1 < parts:
            to_right[p] = line_operator(np.full_like(k, (p + 1) * m), k, n)
        if p > 0:
            to_left[p] = line_operator(np.full_like(k, p * m - 1), k, n)
        from_left[p] = (-RATIO) ** node * (1 - RATIO ** (2.0 * (n - p * m - node))) / (1 - RATIO ** (2.0 * (n - p * m)))
        from_right[p] = (
            (-RATIO) ** (m - 1 - node) * (1 - RATIO ** (2.0 * (p * m + node + 1))) / (1 - RATIO ** (2.0 * (p + 1) * m))
        )
        for q in range(parts):
            if q < p:
                weight_left[p, q] = (
                    (-RATIO) ** ((p - q - 1) * m)
                    * (1 - RATIO ** (2.0 * (n - p * m)))
                    / (1 - RATIO ** (2.0 * (n - (q + 1) * m)))
                )
            if q > p:
                weight_right[p, q] = (
                    (-RATIO) ** ((q - p - 1) * m) * (1 - RATIO ** (2.0 * (p + 1) * m)) / (1 - RATIO ** (2.0 * q * m))
                )
    first[0] = inverse_mass(node, np.zeros_like(node), n) / 3.0
    if parts > 1:
        first_right[0] = -inverse_mass(np.array(m), np.array(0), n) / 3.0
    return {
        "block": block,
        "to_right": to_right,
        "to_left": to_left,
        "from_left": from_left,
        "from_right": from_right,
        "weight_left": weight_left,
        "weight_right": weight_right,
        "first": first,
        "first_right": first_right,
    }


def even_selector(m):
    pick = np.zeros((2 * m, m))
    pick[2 * np.arange(m), np.arange(m)] = 1.0
    return pick


def f32(values):
    return np.asarray(values, np.float32)


def combine_tables(sizes, tx, ty, tz, mz):
    gx, gy, gz = sizes
    count = gx * gy * gz
    sender = np.arange(count)
    qx, qy, qz = sender % gx, (sender // gx) % gy, sender // (gy * gx)
    rows = 32
    wx, wy, wz = (np.zeros((parts, rows, count, 4)) for parts in sizes)

    def side(t, p, q, which):
        if which == 0:
            return (q == p) * 1.0
        return (t["weight_left"] if which == 1 else t["weight_right"])[p][q]

    for sx in range(3):
        for sy in range(3):
            if sx == 0 and sy == 0:
                continue
            for z in range(mz):
                row = (sx * 3 + sy) * mz + z
                for p in range(gx):
                    wx[p, row] = side(tx, p, qx, sx)[:, None]
                for p in range(gy):
                    wy[p, row] = side(ty, p, qy, sy)[:, None]
                for p in range(gz):
                    wz[p, row, :, z] += qz == p
                    wz[p, row, :, 0] += tz["weight_left"][p][qz] * tz["from_left"][p, z]
                    wz[p, row, :, 0] += tz["weight_right"][p][qz] * tz["from_right"][p, z]
    for case, (ox, oy) in enumerate(((1, 0), (0, 1), (1, 1))):
        for layer in range(mz + 1):
            row = 9 * mz + case * (mz + 1) + layer
            for p in range(gx):
                wx[p, row] = (qx == p + ox)[:, None]
            for p in range(gy):
                wy[p, row] = (qy == p + oy)[:, None]
            for p in range(gz):
                if layer < mz:
                    wz[p, row, :, mz + layer] = qz == p
                else:
                    wz[p, row, :, mz] = qz == p + 1
    return tuple(f32(w.reshape(w.shape[0], rows, count * 4)) for w in (wx, wy, wz))


def split(values):
    high = values.astype(jnp.bfloat16)
    return high, (values - high.astype(jnp.float32)).astype(jnp.bfloat16)


def one_pass(a, b, contract=((1,), (0,))):
    return lax.dot_general(a, b, (contract, ((), ())), preferred_element_type=jnp.float32)


def three_pass(a, b, contract=((1,), (0,))):
    return one_pass(a[0], b[0], contract) + one_pass(a[0], b[1], contract) + one_pass(a[1], b[0], contract)


def two_pass(a, b):
    return one_pass(a[0], b) + one_pass(a[1], b)


def exact_left(a, b):
    high, low = split(b)
    return one_pass(a, high) + one_pass(a, low)


def exact_right(a, b):
    high, low = split(a)
    return one_pass(high, b) + one_pass(low, b)


def start_all(copies):
    for copy in copies:
        copy.start()


def local_kernel(sizes, *refs):
    field, fold_z, line_y, line_x = refs[:4]
    send, own, even, near, far, first, f = refs[4:11]
    ry, bx, az, picked, column, kinds, sem = refs[11:]
    gx, gy, gz = sizes
    px, py, pz = lax.axis_index("gx"), lax.axis_index("gy"), lax.axis_index("gz")
    depth, height, breadth = field.shape
    mz, mx, my = own.shape
    planes = [pltpu.make_async_copy(field.at[z], f.at[z], sem.at[z]) for z in range(depth)]
    sources = [(fold_z.at[pz], az), (line_y.at[py], ry), (line_x.at[px], bx)]
    tables = [pltpu.make_async_copy(src, dst, sem.at[depth + i]) for i, (src, dst) in enumerate(sources)]
    start_all(tables[:2] + planes + tables[2:])
    kinds[...] = jnp.zeros_like(kinds)
    fine = lax.broadcasted_iota(jnp.int32, (breadth, my), 0)
    node = lax.broadcasted_iota(jnp.int32, (breadth, my), 1)
    pick_y = jnp.where(fine == 2 * node, 1.0, 0.0).astype(jnp.bfloat16)
    tables[0].wait()
    tables[1].wait()
    weights = split(ry[:breadth])
    by_y, evens, along_x = [], [], None
    step = 2
    for start in range(0, depth, step):
        for z in range(start, start + step):
            planes[z].wait()
        part = split(f[start : start + step].reshape(step * height, breadth))
        result = three_pass(part, weights)
        for z in range(start, start + step):
            rows = slice((z - start) * height, (z - start + 1) * height)
            by_y.append(result[rows, :my])
            folded = result[rows, my:] * az[z : z + 1, :]
            along_x = folded if along_x is None else along_x + folded
            if z % 2 == 0:
                j = z // 2
                picked[j] = two_pass((part[0][rows], part[1][rows]), pick_y)
                evens.append(picked[j, pl.ds(0, mx, stride=2), :])
                even[j] = evens[j]
    column[...] = along_x
    edge = jnp.transpose(column[pl.ds(0, mx, stride=2), :])[:16, :]
    for table in tables[2:]:
        table.wait()
    solve_x = split(bx[: mx + 8])
    faces = three_pass(solve_x, split(along_x))
    by_x = jnp.transpose(faces[:mx])[:16, :]
    corners = [faces[mx + ab : mx + ab + 1] for ab in range(2)]
    by_split = split(jnp.concatenate(by_y, axis=1))
    ends_x = three_pass(tuple(half[mx:] for half in solve_x), by_split)
    sums = [[ends_x[ab : ab + 1, z * my : (z + 1) * my] for ab in range(2)] for z in range(depth)]

    first_y, kappa_y = ry[breadth : breadth + 1, :my], ry[breadth + 1 : breadth + 2, :my]
    first_x, kappa_x = bx[mx + 8 : mx + 9, :mx], bx[mx + 9 : mx + 10, :mx]
    outs = mz + 2
    first_rows = jnp.concatenate([evens[j][0:1, :] for j in range(mz)], axis=0)
    first_cols = edge[2 * outs : 2 * outs + mz, :]

    def over_z(base, rows):
        return sum(az[base + 8 * j : base + 8 * j + 8, :] * rows[j] for j in range(len(rows)))

    first_row = over_z(8 + 8 * depth, [first_rows[j : j + 1] for j in range(mz)])
    first_col = over_z(8 + 8 * depth, [first_cols[j : j + 1] for j in range(mz)])
    corner = first_row[:, 0:1]
    lane = lax.broadcasted_iota(jnp.int32, (8, my), 1)
    here = lane == lax.broadcasted_iota(jnp.int32, (8, my), 0)
    ends = [jnp.sum(jnp.where(here, corners[ab], 0.0), axis=1, keepdims=True) for ab in range(2)]
    spread = jnp.zeros((outs, my), jnp.float32)
    chunks = {
        (1, 0): over_z(8, [sums[z][0] for z in range(depth)]) - kappa_x * (first_row - first_y * corner),
        (2, 0): over_z(8, [sums[z][1] for z in range(depth)]),
        (0, 1): by_x[:outs] - (kappa_y * (first_col - first_x * corner))[:outs],
        (0, 2): by_x[outs : 2 * outs],
        (1, 1): spread + ends[0][:outs] - kappa_x * kappa_y * corner[:outs],
        (1, 2): spread + ends[0][outs : 2 * outs],
        (2, 1): spread + ends[1][:outs],
        (2, 2): spread + ends[1][outs : 2 * outs],
    }
    for (sx, sy), rows in chunks.items():
        kind = (sx * 3 + sy) * 3
        kinds[kind, 0:mz, :] = rows[:mz]
        kinds[kind + 1, 0:1, :] = rows[mz : mz + 1]
        kinds[kind + 2, 0:1, :] = rows[mz + 1 : mz + 2]
    for sx in range(3):
        for sy in range(3):
            for sz in range(3):
                kinds[(sx * 3 + sy) * 3 + sz, mz : 2 * mz, :] = first_cols if sx == 0 else first_rows

    def side(there, here):
        return jnp.where(there == here, 0, jnp.where(there > here, 1, 2))

    def scatter(tx, ty, tz, at):
        send[pl.ds(at, 1)] = kinds[pl.ds((side(tx, px) * 3 + side(ty, py)) * 3 + side(tz, pz), 1)]

    if gx * gy * gz <= 32:
        for at in range(gx * gy * gz):
            scatter(at % gx, (at // gx) % gy, at // (gy * gx), at)
    else:

        @pl.loop(0, gx * gy * gz)
        def _(at):
            scatter(at % gx, (at // gx) % gy, at // (gy * gx), at)

    by_all = three_pass(tuple(half[:mx] for half in solve_x), by_split)
    solved = [by_all[:, z * my : (z + 1) * my] for z in range(depth)]
    first_x = jnp.transpose(jnp.broadcast_to(first_x, (8, mx)))[:, 0:1]
    outs = []
    for out in range(mz + 2):
        value = sum(az[8 + 8 * z + out : 9 + 8 * z + out, :] * solved[z] for z in range(depth))
        base = 8 + 8 * depth + out
        part = sum(az[base + 8 * j : base + 8 * j + 1, :] * evens[j] for j in range(mz))
        part = part - first_x * part[0:1, :]
        part = part - part[:, 0:1] * first_y
        outs.append(value - part)
    for j in range(mz):
        own[j] = evens[j] + outs[j]
    near[...] = jnp.where(pz % 2 == 0, outs[mz], outs[mz + 1])
    far[...] = jnp.where(pz % 4 < 2, outs[mz], outs[mz + 1])
    first[...] = evens[0]


def inner_kernel(field, even, *refs):
    tables, (parts, sem) = refs[:6], refs[14:]
    coefficients, c, top, rows, weights, columns, up_x, up_y = refs[6:14]
    px, py, pz = lax.axis_index("gx"), lax.axis_index("gy"), lax.axis_index("gz")
    depth, height, breadth = field.shape
    mz = even.shape[0]
    goals = (rows.at[0:8], rows.at[8:16], rows.at[16:32], parts.at[0], parts.at[1], parts.at[2])
    fetches = [
        pltpu.make_async_copy(table.at[at], goal, sem.at[depth + i])
        for i, (table, at, goal) in enumerate(zip(tables, (px, py, pz) * 2, goals, strict=True))
    ]
    start_all(fetches)
    for up, node_axis in ((up_x, 1), (up_y, 0)):
        node = lax.broadcasted_iota(jnp.int32, up.shape, node_axis)
        away = jnp.abs(lax.broadcasted_iota(jnp.int32, up.shape, 1 - node_axis) - 2 * node)
        up[...] = jnp.where(away == 0, 1.0, jnp.where(away == 1, 0.5, 0.0))
    body = (pl.ds(0, height - 8), pl.ds(0, breadth - 128))
    up_left, up_right = up_x[...].astype(jnp.bfloat16), up_y[...].astype(jnp.bfloat16)
    lifted = [exact_right(exact_left(up_left, even[j]), up_right) for j in range(mz)]
    copies = []
    for z in range(depth - 1):
        j = z // 2
        c[z] = field[z] - (lifted[j] if z % 2 == 0 else 0.5 * (lifted[j] + lifted[j + 1]))
        copies.append(pltpu.make_async_copy(c.at[z, *body], coefficients.at[z, *body], sem.at[z]))
        copies[z].start()
    top[...] = field[depth - 1] - 0.5 * lifted[mz - 1]
    for copy in fetches:
        copy.wait()
    weights[...] = parts[0] * parts[1] * parts[2]
    blank = jnp.zeros((columns.shape[1] - weights.shape[0], weights.shape[1]), jnp.float32)
    columns[...] = jnp.transpose(jnp.concatenate([weights[...], blank], axis=0))
    for copy in copies:
        copy.wait()


def gather_kernel(received, weights, columns, got, got_columns):
    chunks = split(received[...])
    got_columns[...] = three_pass(chunks, split(columns[...]), ((0,), (0,)))
    got[...] = three_pass(split(weights[...]), chunks)


def finish_kernel(*refs):
    got, got_columns, rows, up_x, up_y, inner, top, own, one, two, three, first, first_far, partial = refs[:14]
    coefficients, coarse, last_plane, rim, foot, values, sem = refs[14:]
    del partial
    mz, mx, my = own.shape
    depth, height, breadth = 2 * mz, 2 * mx, 2 * my
    split_at = breadth - 128
    body = (pl.ds(0, height - 8), pl.ds(0, split_at))

    def row_at(i):
        return rows[16 + i : 17 + i, :]

    planes = (one[...], two[...], three[...])
    left = sum(row_at(i) * plane for i, plane in enumerate(planes))
    right = sum(row_at(3 + i) * plane for i, plane in enumerate(planes))
    ahead = row_at(6) * first[...] + row_at(7) * first_far[...]
    up_left, up_right = up_x[...].astype(jnp.bfloat16), up_y[...].astype(jnp.bfloat16)
    last_plane[...] = top[...] - 0.5 * exact_right(exact_left(up_left, ahead), up_right)
    copies = [pltpu.make_async_copy(last_plane.at[body], coefficients.at[depth - 1, *body], sem.at[0])]
    copies[0].start()
    before = [own[j] + row_at(8 + j) * left + row_at(8 + mz + j) * right for j in range(mz)]

    base = 9 * mz
    layers = mz + 1
    halo_x, halo_xy = got[base : base + layers], got[base + 2 * layers : base + 3 * layers]
    pad = jnp.zeros((8 - layers, halo_x.shape[1]), jnp.float32)
    row = exact_right(jnp.concatenate([halo_x, pad], axis=0), up_right)
    col = exact_left(up_left, got_columns[...])[:, base + layers : base + 2 * layers]
    lane = lax.broadcasted_iota(jnp.int32, (1, 128), 1)
    last = lane == 127
    for z in range(depth):
        j = z // 2
        if z % 2 == 0:
            r, s, k = row[j : j + 1], 0.5 * col[:, j : j + 1], halo_xy[j : j + 1, 0:1]
        else:
            r = 0.5 * (row[j : j + 1] + row[j + 1 : j + 2])
            s = 0.25 * (col[:, j : j + 1] + col[:, j + 1 : j + 2])
            k = 0.5 * (halo_xy[j : j + 1, 0:1] + halo_xy[j + 1 : j + 2, 0:1])
        old = inner[z] if z < depth - 1 else last_plane[...]
        rim[z] = old[:, split_at:] - jnp.where(last, s, 0.0)
        end = 0.5 * r[:, split_at:] + jnp.where(last, 0.25 * k, 0.0)
        rim[z, height - 1 : height, :] = rim[z, height - 1 : height, :] - end
        foot[z] = old[height - 8 :, :split_at]
        foot[z, 7:8, :] = old[height - 1 :, :split_at] - 0.5 * r[:, :split_at]
        goal = coefficients.at[z, :, pl.ds(split_at, 128)]
        copies.append(pltpu.make_async_copy(rim.at[z], goal, sem.at[3 + 2 * z]))
        goal = coefficients.at[z, pl.ds(height - 8, 8), pl.ds(0, split_at)]
        copies.append(pltpu.make_async_copy(foot.at[z], goal, sem.at[4 + 2 * z]))
        start_all(copies[-2:])

    ux, vx, uy, vy = rows[0:1], rows[1:2], rows[8:9], rows[9:10]

    def part(sx, sy, z):
        at = (sx * 3 + sy) * mz + z
        return got[at : at + 1]

    for z in range(mz):
        a, b = [], []
        for sy, end in ((1, uy), (2, vy)):
            a.append(part(0, sy, z) + ux * part(1, sy, z)[:, 0:1] + vx * part(2, sy, z)[:, 0:1])
            b.append(end)
        for sx, end in ((1, ux), (2, vx)):
            a.append(end)
            b.append(part(sx, 0, z))
        zero = [jnp.zeros((4, mx), jnp.float32)]
        a, b = split(jnp.concatenate(a + zero, axis=0)), split(jnp.concatenate(b + zero, axis=0))
        values[z] = before[z] + three_pass(a, b, ((0,), (0,)))
    copies.append(pltpu.make_async_copy(values, coarse, sem.at[2]))
    copies[-1].start()
    for copy in copies:
        copy.wait()


def call(kernel, name, out_shape, in_specs, out_specs, scratch=(), aliases=None, flops=1, size=1):
    return pl.pallas_call(
        kernel,
        out_shape=out_shape,
        in_specs=in_specs,
        out_specs=out_specs,
        scratch_shapes=list(scratch),
        input_output_aliases=aliases or {},
        compiler_params=pltpu.CompilerParams(vmem_limit_bytes=VMEM_LIMIT),
        cost_estimate=pl.CostEstimate(flops=flops, bytes_accessed=size, transcendentals=0),
        name=name,
    )


ANY = pl.BlockSpec(memory_space=pl.ANY)
HBM = pl.BlockSpec(memory_space=pltpu.HBM)
SMEM = pl.BlockSpec(memory_space=pltpu.SMEM)
VMEM = pl.BlockSpec(memory_space=pltpu.VMEM)


def in_hbm(values):
    return pltpu.with_memory_space_constraint(jnp.asarray(values), pltpu.HBM)


def shape(*dims):
    return jax.ShapeDtypeStruct(dims, jnp.float32)


def on_device(sizes, field):
    gx, gy, gz = sizes
    depth, height, breadth = field.shape
    mz, mx, my = depth // 2, height // 2, breadth // 2
    count = gx * gy * gz
    axes = ("gz", "gy", "gx")
    tx, ty, tz = line_tables(gx, mx), line_tables(gy, my), line_tables(gz, mz)

    def vectors(t, parts, m):
        table = np.zeros((parts, 8, m))
        table[:, 0], table[:, 1] = t["from_left"], t["from_right"]
        return f32(table)

    row_x, row_y = vectors(tx, gx, mx), vectors(ty, gy, my)
    line_y, line_x = np.zeros((gy, breadth + 8, 2 * my)), np.zeros((gx, mx + 16, height))
    line_y[:, :breadth, :my] = ty["block"].transpose(0, 2, 1)
    outs = mz + 2
    line_y[:, :breadth, my : my + outs] = ty["to_right"][..., None]
    line_y[:, :breadth, my + outs : my + 2 * outs] = ty["to_left"][..., None]
    line_y[:, 0, my + 2 * (mz + 2) : my + 2 * (mz + 2) + mz] = 1.0
    line_y[:, breadth, :my], line_y[:, breadth + 1, :my] = ty["first"], ty["first_right"][:, None]
    line_x[:, :mx], line_x[:, mx], line_x[:, mx + 1] = tx["block"], tx["to_right"], tx["to_left"]
    line_x[:, mx + 8, :mx], line_x[:, mx + 9, :mx] = tx["first"], tx["first_right"][:, None]

    fold_z = np.zeros((gz, 8 + 8 * (depth + mz), my))
    for p in range(gz):
        full = np.concatenate([tz["block"][p], tz["to_right"][p : p + 1], tz["to_left"][p : p + 1]], axis=0)
        nodes = np.zeros((outs, mz))
        nodes[:mz] = np.eye(mz)
        nodes[:mz, 0] -= tz["first"][p]
        nodes[mz, 0] = tz["first_right"][p]
        fold_z[p, :depth, : 2 * outs] = np.tile(full.T, 2)
        for j in range(mz):
            fold_z[p, 2 * j, 2 * outs + j] = 1.0
        for z in range(depth):
            fold_z[p, 8 + 8 * z : 8 + 8 * z + outs] = full[:, z : z + 1]
        for j in range(mz):
            base = 8 + 8 * (depth + j)
            fold_z[p, base : base + outs] = nodes[:, j : j + 1]

    vmem = pltpu.VMEM
    operands = (field, f32(fold_z), f32(line_y), f32(line_x))
    send, own, even, near, far, first, kept = call(
        functools.partial(local_kernel, sizes),
        "local",
        [shape(count, 4, my), shape(mz, mx, my), shape(mz, mx, my)] + [shape(mx, my)] * 3 + [shape(*field.shape)],
        [HBM] * 4,
        [VMEM] * 7,
        [
            vmem(line_y.shape[1:], jnp.float32),
            vmem(line_x.shape[1:], jnp.float32),
            vmem(fold_z.shape[1:], jnp.float32),
            vmem((mz, height, my), jnp.float32),
            vmem((height, 128), jnp.float32),
            vmem((27, 4, my), jnp.float32),
            pltpu.SemaphoreType.DMA((depth + 3,)),
        ],
    )(*map(in_hbm, operands))
    received = lax.all_to_all(send, axes, 0, 0, tiled=True).reshape(count * 4, my)

    assert gz == 4

    def exchange(plane, hop):
        return lax.ppermute(plane, "gz", [(i, i ^ hop) for i in range(gz)])

    from_far = exchange(far, 3)
    gets = (exchange(near, 1), exchange(from_far, 1), from_far, exchange(first, 1), exchange(first, 3))

    row_z = np.zeros((gz, 16, my))
    for p in range(gz):
        for i, hop in enumerate((1, 2, 3)):
            row_z[p, i], row_z[p, 3 + i] = tz["weight_left"][p, p ^ hop], tz["weight_right"][p, p ^ hop]
        row_z[p, 6], row_z[p, 7] = p ^ 1 == p + 1, p ^ 3 == p + 1
        row_z[p, 8 : 8 + mz] = tz["from_left"][p][:, None]
        row_z[p, 8 + mz : 8 + 2 * mz] = tz["from_right"][p][:, None]
    wx, wy, wz = combine_tables(sizes, tx, ty, tz, mz)
    tables = (row_x, row_y, f32(row_z), wx, wy, wz)
    partial, inner, top, rows, weights, columns, up_x, up_y = call(
        inner_kernel,
        "inner",
        [shape(*field.shape), shape(depth - 1, height, breadth), shape(height, breadth), shape(32, my)]
        + [shape(*wx.shape[1:]), shape(count * 4, 128), shape(height, mx), shape(my, breadth)],
        [VMEM] * 2 + [HBM] * len(tables),
        [HBM] + [VMEM] * 7,
        [vmem((3, *wx.shape[1:]), jnp.float32), pltpu.SemaphoreType.DMA((depth + len(tables),))],
    )(kept, even, *map(in_hbm, tables))
    got, got_columns = call(
        gather_kernel,
        "gather",
        [shape(wx.shape[1], my), shape(mx, 128)],
        [VMEM] * 3,
        [VMEM] * 2,
        flops=10**10,
        size=10**8,
    )(received, weights, columns)
    return call(
        finish_kernel,
        "finish",
        [shape(*field.shape), shape(mz, mx, my)],
        [VMEM] * 13 + [HBM],
        [HBM, HBM],
        [
            vmem((height, breadth), jnp.float32),
            vmem((depth, height, 128), jnp.float32),
            vmem((depth, 8, breadth - 128), jnp.float32),
            vmem((mz, mx, my), jnp.float32),
            pltpu.SemaphoreType.DMA((3 + 2 * depth,)),
        ],
        {13: 0},
    )(got, got_columns, rows, up_x, up_y, inner, top, own, *gets, partial)


def solution(mesh):
    sizes = tuple(mesh.shape[axis] for axis in ("gx", "gy", "gz"))
    return jax.shard_map(
        functools.partial(on_device, sizes),
        mesh=mesh,
        in_specs=(P("gz", "gx", "gy"),),
        out_specs=(P("gz", "gx", "gy"), P("gz", "gx", "gy")),
        check_vma=False,
    )
```

```python
import functools

import jax
import jax.numpy as jnp
import numpy as np
from jax import lax
from jax.experimental import pallas as pl
from jax.experimental.pallas import tpu as pltpu
from jax.sharding import PartitionSpec as P

RATIO = 2.0 - np.sqrt(3.0)
VMEM_LIMIT = 48 * 1024 * 1024


def inverse_mass(i, j, n):
    low, high = np.minimum(i, j), np.maximum(i, j)
    sign = np.where((high - low) % 2 == 0, 1.0, -1.0)
    value = RATIO ** (high - low + 1.0) * (1.0 - RATIO ** (2.0 * (low + 1))) * (1.0 - RATIO ** (2.0 * (n - high)))
    return 3.0 * sign * value / ((1.0 - RATIO**2) * (1.0 - RATIO ** (2.0 * (n + 1))))


def line_operator(i, k, n):
    a = k // 2
    odd = k % 2 == 1

    def at(j):
        inside = (j >= 0) & (j < n)
        return np.where(inside, inverse_mass(i, np.clip(j, 0, n - 1), n), 0.0)

    even_part = np.where(a == 0, 9.0, 10.0) * at(a) + at(a - 1) + at(a + 1)
    odd_part = 6.0 * at(a) + 6.0 * at(a + 1)
    return np.where(odd, odd_part, even_part) / 12.0


def line_tables(parts, m):
    n = parts * m
    node, fine = np.arange(m), np.arange(2 * m)
    block = np.zeros((parts, m, 2 * m))
    to_right, to_left = np.zeros((parts, 2 * m)), np.zeros((parts, 2 * m))
    from_left, from_right = np.zeros((parts, m)), np.zeros((parts, m))
    weight_left, weight_right = np.zeros((parts, parts)), np.zeros((parts, parts))
    first = np.zeros((parts, m))
    first_right = np.zeros((parts,))
    for p in range(parts):
        k = p * 2 * m + fine
        block[p] = line_operator((p * m + node)[:, None], k[None, :], n)
        if p + 1 < parts:
            to_right[p] = line_operator(np.full_like(k, (p + 1) * m), k, n)
        if p > 0:
            to_left[p] = line_operator(np.full_like(k, p * m - 1), k, n)
        from_left[p] = (-RATIO) ** node * (1 - RATIO ** (2.0 * (n - p * m - node))) / (1 - RATIO ** (2.0 * (n - p * m)))
        from_right[p] = (
            (-RATIO) ** (m - 1 - node) * (1 - RATIO ** (2.0 * (p * m + node + 1))) / (1 - RATIO ** (2.0 * (p + 1) * m))
        )
        for q in range(parts):
            if q < p:
                weight_left[p, q] = (
                    (-RATIO) ** ((p - q - 1) * m)
                    * (1 - RATIO ** (2.0 * (n - p * m)))
                    / (1 - RATIO ** (2.0 * (n - (q + 1) * m)))
                )
            if q > p:
                weight_right[p, q] = (
                    (-RATIO) ** ((q - p - 1) * m) * (1 - RATIO ** (2.0 * (p + 1) * m)) / (1 - RATIO ** (2.0 * q * m))
                )
    first[0] = inverse_mass(node, np.zeros_like(node), n) / 3.0
    if parts > 1:
        first_right[0] = -inverse_mass(np.array(m), np.array(0), n) / 3.0
    return {
        "block": block,
        "to_right": to_right,
        "to_left": to_left,
        "from_left": from_left,
        "from_right": from_right,
        "weight_left": weight_left,
        "weight_right": weight_right,
        "first": first,
        "first_right": first_right,
    }


def f32(values):
    return np.asarray(values, np.float32)


def combine_tables(sizes, tx, ty, tz, mz):
    gx, gy, gz = sizes
    count = gx * gy * gz
    sender = np.arange(count)
    qx, qy, qz = sender % gx, (sender // gx) % gy, sender // (gy * gx)
    rows = 32
    wx, wy, wz = (np.zeros((parts, rows, count, 4)) for parts in sizes)

    def side(t, p, q, which):
        if which == 0:
            return (q == p) * 1.0
        return (t["weight_left"] if which == 1 else t["weight_right"])[p][q]

    for sx in range(3):
        for sy in range(3):
            if sx == 0 and sy == 0:
                continue
            for z in range(mz):
                row = (sx * 3 + sy) * mz + z
                for p in range(gx):
                    wx[p, row] = side(tx, p, qx, sx)[:, None]
                for p in range(gy):
                    wy[p, row] = side(ty, p, qy, sy)[:, None]
                for p in range(gz):
                    wz[p, row, :, z] += qz == p
                    wz[p, row, :, 0] += tz["weight_left"][p][qz] * tz["from_left"][p, z]
                    wz[p, row, :, 0] += tz["weight_right"][p][qz] * tz["from_right"][p, z]
    for case, (ox, oy) in enumerate(((1, 0), (0, 1), (1, 1))):
        for layer in range(mz + 1):
            row = 9 * mz + case * (mz + 1) + layer
            for p in range(gx):
                wx[p, row] = (qx == p + ox)[:, None]
            for p in range(gy):
                wy[p, row] = (qy == p + oy)[:, None]
            for p in range(gz):
                if layer < mz:
                    wz[p, row, :, mz + layer] = qz == p
                else:
                    wz[p, row, :, mz] = qz == p + 1
    return tuple(f32(w.reshape(w.shape[0], rows, count * 4)) for w in (wx, wy, wz))


def split(values):
    high = values.astype(jnp.bfloat16)
    return high, (values - high.astype(jnp.float32)).astype(jnp.bfloat16)


def one_pass(a, b, contract=((1,), (0,))):
    return lax.dot_general(a, b, (contract, ((), ())), preferred_element_type=jnp.float32)


def three_pass(a, b, contract=((1,), (0,))):
    return one_pass(a[0], b[0], contract) + one_pass(a[0], b[1], contract) + one_pass(a[1], b[0], contract)


def two_pass(a, b):
    return one_pass(a[0], b) + one_pass(a[1], b)


def exact_left(a, b):
    high, low = split(b)
    return one_pass(a, high) + one_pass(a, low)


def exact_right(a, b):
    high, low = split(a)
    return one_pass(high, b) + one_pass(low, b)


def start_all(copies):
    for copy in copies:
        copy.start()


def faces_kernel(sizes, *refs):
    field, fold_z, line_y, line_x = refs[:4]
    send, f, bx, az, by, head = refs[4:10]
    ry, column, kinds, sem = refs[10:]
    gx, gy, gz = sizes
    px, py, pz = lax.axis_index("gx"), lax.axis_index("gy"), lax.axis_index("gz")
    depth, height, breadth = field.shape
    mz, mx, my = depth // 2, height // 2, breadth // 2
    planes = [pltpu.make_async_copy(field.at[z], f.at[z], sem.at[z]) for z in range(depth)]
    sources = [(fold_z.at[pz], az), (line_y.at[py], ry), (line_x.at[px], bx)]
    tables = [pltpu.make_async_copy(src, dst, sem.at[depth + i]) for i, (src, dst) in enumerate(sources)]
    start_all(tables[:2] + planes + tables[2:])
    kinds[...] = jnp.zeros_like(kinds)
    fine = lax.broadcasted_iota(jnp.int32, (breadth, my), 0)
    node = lax.broadcasted_iota(jnp.int32, (breadth, my), 1)
    pick_y = jnp.where(fine == 2 * node, 1.0, 0.0).astype(jnp.bfloat16)
    tables[0].wait()
    tables[1].wait()
    weights = split(ry[:breadth])
    by_y, tops, along_x = [], [], None
    step = 2
    for start in range(0, depth, step):
        for z in range(start, start + step):
            planes[z].wait()
        part = split(f[start : start + step].reshape(step * height, breadth))
        result = three_pass(part, weights)
        for z in range(start, start + step):
            rows = slice((z - start) * height, (z - start + 1) * height)
            by_y.append(result[rows, :my])
            folded = result[rows, my:] * az[z : z + 1, :]
            along_x = folded if along_x is None else along_x + folded
            if z % 2 == 0:
                tops.append(tuple(half[rows][:16] for half in part))
    column[...] = along_x
    edge = jnp.transpose(column[pl.ds(0, mx, stride=2), :])[:16, :]
    for table in tables[2:]:
        table.wait()
    solve_x = split(bx[: mx + 8])
    faces = three_pass(solve_x, split(along_x))
    by_x = jnp.transpose(faces[:mx])[:16, :]
    corners = [faces[mx + ab : mx + ab + 1] for ab in range(2)]
    by[...] = jnp.concatenate(by_y, axis=1)
    head[...] = ry[breadth : breadth + 8, :my]
    by_split = split(by[...])
    ends_x = three_pass(tuple(half[mx:] for half in solve_x), by_split)
    sums = [[ends_x[ab : ab + 1, z * my : (z + 1) * my] for ab in range(2)] for z in range(depth)]

    first_y, kappa_y = ry[breadth : breadth + 1, :my], ry[breadth + 1 : breadth + 2, :my]
    first_x, kappa_x = bx[mx + 8 : mx + 9, :mx], bx[mx + 9 : mx + 10, :mx]
    outs = mz + 2
    heads = two_pass(tuple(jnp.concatenate(halves, axis=0) for halves in zip(*tops, strict=True)), pick_y)
    first_rows = jnp.concatenate([heads[16 * j : 16 * j + 1, :] for j in range(mz)], axis=0)
    first_cols = edge[2 * outs : 2 * outs + mz, :]

    def over_z(base, rows):
        return sum(az[base + 8 * j : base + 8 * j + 8, :] * rows[j] for j in range(len(rows)))

    first_row = over_z(8 + 8 * depth, [first_rows[j : j + 1] for j in range(mz)])
    first_col = over_z(8 + 8 * depth, [first_cols[j : j + 1] for j in range(mz)])
    corner = first_row[:, 0:1]
    lane = lax.broadcasted_iota(jnp.int32, (8, my), 1)
    here = lane == lax.broadcasted_iota(jnp.int32, (8, my), 0)
    ends = [jnp.sum(jnp.where(here, corners[ab], 0.0), axis=1, keepdims=True) for ab in range(2)]
    spread = jnp.zeros((outs, my), jnp.float32)
    chunks = {
        (1, 0): over_z(8, [sums[z][0] for z in range(depth)]) - kappa_x * (first_row - first_y * corner),
        (2, 0): over_z(8, [sums[z][1] for z in range(depth)]),
        (0, 1): by_x[:outs] - (kappa_y * (first_col - first_x * corner))[:outs],
        (0, 2): by_x[outs : 2 * outs],
        (1, 1): spread + ends[0][:outs] - kappa_x * kappa_y * corner[:outs],
        (1, 2): spread + ends[0][outs : 2 * outs],
        (2, 1): spread + ends[1][:outs],
        (2, 2): spread + ends[1][outs : 2 * outs],
    }
    for (sx, sy), rows in chunks.items():
        kind = (sx * 3 + sy) * 3
        kinds[kind, 0:mz, :] = rows[:mz]
        kinds[kind + 1, 0:1, :] = rows[mz : mz + 1]
        kinds[kind + 2, 0:1, :] = rows[mz + 1 : mz + 2]
    for sx in range(3):
        for sy in range(3):
            for sz in range(3):
                kinds[(sx * 3 + sy) * 3 + sz, mz : 2 * mz, :] = first_cols if sx == 0 else first_rows

    def side(there, here):
        return jnp.where(there == here, 0, jnp.where(there > here, 1, 2))

    def scatter(tx, ty, tz, at):
        send[pl.ds(at, 1)] = kinds[pl.ds((side(tx, px) * 3 + side(ty, py)) * 3 + side(tz, pz), 1)]

    if gx * gy * gz <= 32:
        for at in range(gx * gy * gz):
            scatter(at % gx, (at // gx) % gy, at // (gy * gx), at)
    else:

        @pl.loop(0, gx * gy * gz)
        def _(at):
            scatter(at % gx, (at // gx) % gy, at // (gy * gx), at)


def planes_kernel(f, bx, az, by, head, own, even, near, far, first, picked):
    pz = lax.axis_index("gz")
    depth, _, breadth = f.shape
    mz, mx, my = own.shape
    fine = lax.broadcasted_iota(jnp.int32, (breadth, my), 0)
    node = lax.broadcasted_iota(jnp.int32, (breadth, my), 1)
    pick_y = jnp.where(fine == 2 * node, 1.0, 0.0).astype(jnp.bfloat16)
    evens = []
    for j in range(mz):
        picked[j] = two_pass(split(f[2 * j]), pick_y)
        evens.append(picked[j, pl.ds(0, mx, stride=2), :])
        even[j] = evens[j]
    first_y, first_x = head[0:1], bx[mx + 8 : mx + 9, :mx]
    by_all = three_pass(split(bx[:mx]), split(by[...]))
    solved = [by_all[:, z * my : (z + 1) * my] for z in range(depth)]
    first_x = jnp.transpose(jnp.broadcast_to(first_x, (8, mx)))[:, 0:1]
    outs = []
    for out in range(mz + 2):
        value = sum(az[8 + 8 * z + out : 9 + 8 * z + out, :] * solved[z] for z in range(depth))
        base = 8 + 8 * depth + out
        part = sum(az[base + 8 * j : base + 8 * j + 1, :] * evens[j] for j in range(mz))
        part = part - first_x * part[0:1, :]
        part = part - part[:, 0:1] * first_y
        outs.append(value - part)
    for j in range(mz):
        own[j] = evens[j] + outs[j]
    near[...] = jnp.where(pz % 2 == 0, outs[mz], outs[mz + 1])
    far[...] = jnp.where(pz % 4 < 2, outs[mz], outs[mz + 1])
    first[...] = evens[0]


def inner_kernel(field, even, *refs):
    tables, (parts, sem) = refs[:6], refs[14:]
    coefficients, c, top, rows, weights, columns, up_x, up_y = refs[6:14]
    px, py, pz = lax.axis_index("gx"), lax.axis_index("gy"), lax.axis_index("gz")
    depth, height, breadth = field.shape
    mz = even.shape[0]
    goals = (rows.at[0:8], rows.at[8:16], rows.at[16:32], parts.at[0], parts.at[1], parts.at[2])
    fetches = [
        pltpu.make_async_copy(table.at[at], goal, sem.at[depth + i])
        for i, (table, at, goal) in enumerate(zip(tables, (px, py, pz) * 2, goals, strict=True))
    ]
    start_all(fetches)
    for up, node_axis in ((up_x, 1), (up_y, 0)):
        node = lax.broadcasted_iota(jnp.int32, up.shape, node_axis)
        away = jnp.abs(lax.broadcasted_iota(jnp.int32, up.shape, 1 - node_axis) - 2 * node)
        up[...] = jnp.where(away == 0, 1.0, jnp.where(away == 1, 0.5, 0.0))
    body = (pl.ds(0, height - 8), pl.ds(0, breadth - 128))
    up_left, up_right = up_x[...].astype(jnp.bfloat16), up_y[...].astype(jnp.bfloat16)
    lifted = [exact_right(exact_left(up_left, even[j]), up_right) for j in range(mz)]
    copies = []
    for z in range(depth - 1):
        j = z // 2
        c[z] = field[z] - (lifted[j] if z % 2 == 0 else 0.5 * (lifted[j] + lifted[j + 1]))
        copies.append(pltpu.make_async_copy(c.at[z, *body], coefficients.at[z, *body], sem.at[z]))
        copies[z].start()
    top[...] = field[depth - 1] - 0.5 * lifted[mz - 1]
    for copy in fetches:
        copy.wait()
    weights[...] = parts[0] * parts[1] * parts[2]
    blank = jnp.zeros((columns.shape[1] - weights.shape[0], weights.shape[1]), jnp.float32)
    columns[...] = jnp.transpose(jnp.concatenate([weights[...], blank], axis=0))
    for copy in copies:
        copy.wait()


def gather_kernel(received, weights, columns, got, got_columns):
    chunks = split(received[...])
    got_columns[...] = three_pass(chunks, split(columns[...]), ((0,), (0,)))
    got[...] = three_pass(split(weights[...]), chunks)


def finish_kernel(*refs):
    got, got_columns, rows, up_x, up_y, inner, top, own, one, two, three, first, first_far, partial = refs[:14]
    coefficients, coarse, last_plane, rim, foot, values, sem = refs[14:]
    del partial
    mz, mx, my = own.shape
    depth, height, breadth = 2 * mz, 2 * mx, 2 * my
    split_at = breadth - 128
    body = (pl.ds(0, height - 8), pl.ds(0, split_at))

    def row_at(i):
        return rows[16 + i : 17 + i, :]

    planes = (one[...], two[...], three[...])
    left = sum(row_at(i) * plane for i, plane in enumerate(planes))
    right = sum(row_at(3 + i) * plane for i, plane in enumerate(planes))
    ahead = row_at(6) * first[...] + row_at(7) * first_far[...]
    up_left, up_right = up_x[...].astype(jnp.bfloat16), up_y[...].astype(jnp.bfloat16)
    last_plane[...] = top[...] - 0.5 * exact_right(exact_left(up_left, ahead), up_right)
    copies = [pltpu.make_async_copy(last_plane.at[body], coefficients.at[depth - 1, *body], sem.at[0])]
    copies[0].start()
    before = [own[j] + row_at(8 + j) * left + row_at(8 + mz + j) * right for j in range(mz)]

    base = 9 * mz
    layers = mz + 1
    halo_x, halo_xy = got[base : base + layers], got[base + 2 * layers : base + 3 * layers]
    pad = jnp.zeros((8 - layers, halo_x.shape[1]), jnp.float32)
    row = exact_right(jnp.concatenate([halo_x, pad], axis=0), up_right)
    col = exact_left(up_left, got_columns[...])[:, base + layers : base + 2 * layers]
    lane = lax.broadcasted_iota(jnp.int32, (1, 128), 1)
    last = lane == 127
    for z in range(depth):
        j = z // 2
        if z % 2 == 0:
            r, s, k = row[j : j + 1], 0.5 * col[:, j : j + 1], halo_xy[j : j + 1, 0:1]
        else:
            r = 0.5 * (row[j : j + 1] + row[j + 1 : j + 2])
            s = 0.25 * (col[:, j : j + 1] + col[:, j + 1 : j + 2])
            k = 0.5 * (halo_xy[j : j + 1, 0:1] + halo_xy[j + 1 : j + 2, 0:1])
        old = inner[z] if z < depth - 1 else last_plane[...]
        rim[z] = old[:, split_at:] - jnp.where(last, s, 0.0)
        end = 0.5 * r[:, split_at:] + jnp.where(last, 0.25 * k, 0.0)
        rim[z, height - 1 : height, :] = rim[z, height - 1 : height, :] - end
        foot[z] = old[height - 8 :, :split_at]
        foot[z, 7:8, :] = old[height - 1 :, :split_at] - 0.5 * r[:, :split_at]
        goal = coefficients.at[z, :, pl.ds(split_at, 128)]
        copies.append(pltpu.make_async_copy(rim.at[z], goal, sem.at[3 + 2 * z]))
        goal = coefficients.at[z, pl.ds(height - 8, 8), pl.ds(0, split_at)]
        copies.append(pltpu.make_async_copy(foot.at[z], goal, sem.at[4 + 2 * z]))
        start_all(copies[-2:])

    ux, vx, uy, vy = rows[0:1], rows[1:2], rows[8:9], rows[9:10]

    def part(sx, sy, z):
        at = (sx * 3 + sy) * mz + z
        return got[at : at + 1]

    for z in range(mz):
        a, b = [], []
        for sy, end in ((1, uy), (2, vy)):
            a.append(part(0, sy, z) + ux * part(1, sy, z)[:, 0:1] + vx * part(2, sy, z)[:, 0:1])
            b.append(end)
        for sx, end in ((1, ux), (2, vx)):
            a.append(end)
            b.append(part(sx, 0, z))
        zero = [jnp.zeros((4, mx), jnp.float32)]
        a, b = split(jnp.concatenate(a + zero, axis=0)), split(jnp.concatenate(b + zero, axis=0))
        values[z] = before[z] + three_pass(a, b, ((0,), (0,)))
    copies.append(pltpu.make_async_copy(values, coarse, sem.at[2]))
    copies[-1].start()
    for copy in copies:
        copy.wait()


def call(kernel, name, out_shape, in_specs, out_specs, scratch=(), aliases=None, flops=1, size=1):
    return pl.pallas_call(
        kernel,
        out_shape=out_shape,
        in_specs=in_specs,
        out_specs=out_specs,
        scratch_shapes=list(scratch),
        input_output_aliases=aliases or {},
        compiler_params=pltpu.CompilerParams(vmem_limit_bytes=VMEM_LIMIT),
        cost_estimate=pl.CostEstimate(flops=flops, bytes_accessed=size, transcendentals=0),
        name=name,
    )


ANY = pl.BlockSpec(memory_space=pl.ANY)
HBM = pl.BlockSpec(memory_space=pltpu.HBM)
SMEM = pl.BlockSpec(memory_space=pltpu.SMEM)
VMEM = pl.BlockSpec(memory_space=pltpu.VMEM)


def in_hbm(values):
    return pltpu.with_memory_space_constraint(jnp.asarray(values), pltpu.HBM)


def shape(*dims):
    return jax.ShapeDtypeStruct(dims, jnp.float32)


def on_device(sizes, field):
    gx, gy, gz = sizes
    depth, height, breadth = field.shape
    mz, mx, my = depth // 2, height // 2, breadth // 2
    count = gx * gy * gz
    axes = ("gz", "gy", "gx")
    tx, ty, tz = line_tables(gx, mx), line_tables(gy, my), line_tables(gz, mz)

    def vectors(t, parts, m):
        table = np.zeros((parts, 8, m))
        table[:, 0], table[:, 1] = t["from_left"], t["from_right"]
        return f32(table)

    row_x, row_y = vectors(tx, gx, mx), vectors(ty, gy, my)
    line_y, line_x = np.zeros((gy, breadth + 8, 2 * my)), np.zeros((gx, mx + 16, height))
    line_y[:, :breadth, :my] = ty["block"].transpose(0, 2, 1)
    outs = mz + 2
    line_y[:, :breadth, my : my + outs] = ty["to_right"][..., None]
    line_y[:, :breadth, my + outs : my + 2 * outs] = ty["to_left"][..., None]
    line_y[:, 0, my + 2 * (mz + 2) : my + 2 * (mz + 2) + mz] = 1.0
    line_y[:, breadth, :my], line_y[:, breadth + 1, :my] = ty["first"], ty["first_right"][:, None]
    line_x[:, :mx], line_x[:, mx], line_x[:, mx + 1] = tx["block"], tx["to_right"], tx["to_left"]
    line_x[:, mx + 8, :mx], line_x[:, mx + 9, :mx] = tx["first"], tx["first_right"][:, None]

    fold_z = np.zeros((gz, 8 + 8 * (depth + mz), my))
    for p in range(gz):
        full = np.concatenate([tz["block"][p], tz["to_right"][p : p + 1], tz["to_left"][p : p + 1]], axis=0)
        nodes = np.zeros((outs, mz))
        nodes[:mz] = np.eye(mz)
        nodes[:mz, 0] -= tz["first"][p]
        nodes[mz, 0] = tz["first_right"][p]
        fold_z[p, :depth, : 2 * outs] = np.tile(full.T, 2)
        for j in range(mz):
            fold_z[p, 2 * j, 2 * outs + j] = 1.0
        for z in range(depth):
            fold_z[p, 8 + 8 * z : 8 + 8 * z + outs] = full[:, z : z + 1]
        for j in range(mz):
            base = 8 + 8 * (depth + j)
            fold_z[p, base : base + outs] = nodes[:, j : j + 1]

    vmem = pltpu.VMEM
    operands = (field, f32(fold_z), f32(line_y), f32(line_x))
    bx, az = shape(*line_x.shape[1:]), shape(*fold_z.shape[1:])
    send, kept, *saved = call(
        functools.partial(faces_kernel, sizes),
        "faces",
        [shape(count, 4, my), shape(*field.shape), bx, az, shape(height, depth * my), shape(8, my)],
        [HBM] * 4,
        [VMEM] * 6,
        [
            vmem(line_y.shape[1:], jnp.float32),
            vmem((height, 128), jnp.float32),
            vmem((27, 4, my), jnp.float32),
            pltpu.SemaphoreType.DMA((depth + 3,)),
        ],
    )(*map(in_hbm, operands))
    own, even, near, far, first = call(
        planes_kernel,
        "planes",
        [shape(mz, mx, my)] * 2 + [shape(mx, my)] * 3,
        [VMEM] * 5,
        [VMEM] * 5,
        [vmem((mz, height, my), jnp.float32)],
    )(kept, *saved)
    received = lax.all_to_all(send, axes, 0, 0, tiled=True).reshape(count * 4, my)

    assert gz == 4

    def exchange(plane, hop):
        return lax.ppermute(plane, "gz", [(i, i ^ hop) for i in range(gz)])

    from_far = exchange(far, 3)
    gets = (exchange(near, 1), exchange(from_far, 1), from_far, exchange(first, 1), exchange(first, 3))

    row_z = np.zeros((gz, 16, my))
    for p in range(gz):
        for i, hop in enumerate((1, 2, 3)):
            row_z[p, i], row_z[p, 3 + i] = tz["weight_left"][p, p ^ hop], tz["weight_right"][p, p ^ hop]
        row_z[p, 6], row_z[p, 7] = p ^ 1 == p + 1, p ^ 3 == p + 1
        row_z[p, 8 : 8 + mz] = tz["from_left"][p][:, None]
        row_z[p, 8 + mz : 8 + 2 * mz] = tz["from_right"][p][:, None]
    wx, wy, wz = combine_tables(sizes, tx, ty, tz, mz)
    tables = (row_x, row_y, f32(row_z), wx, wy, wz)
    partial, inner, top, rows, weights, columns, up_x, up_y = call(
        inner_kernel,
        "inner",
        [shape(*field.shape), shape(depth - 1, height, breadth), shape(height, breadth), shape(32, my)]
        + [shape(*wx.shape[1:]), shape(count * 4, 128), shape(height, mx), shape(my, breadth)],
        [VMEM] * 2 + [HBM] * len(tables),
        [HBM] + [VMEM] * 7,
        [vmem((3, *wx.shape[1:]), jnp.float32), pltpu.SemaphoreType.DMA((depth + len(tables),))],
    )(kept, even, *map(in_hbm, tables))
    got, got_columns = call(
        gather_kernel,
        "gather",
        [shape(wx.shape[1], my), shape(mx, 128)],
        [VMEM] * 3,
        [VMEM] * 2,
        flops=10**10,
        size=10**8,
    )(received, weights, columns)
    return call(
        finish_kernel,
        "finish",
        [shape(*field.shape), shape(mz, mx, my)],
        [VMEM] * 13 + [HBM],
        [HBM, HBM],
        [
            vmem((height, breadth), jnp.float32),
            vmem((depth, height, 128), jnp.float32),
            vmem((depth, 8, breadth - 128), jnp.float32),
            vmem((mz, mx, my), jnp.float32),
            pltpu.SemaphoreType.DMA((3 + 2 * depth,)),
        ],
        {13: 0},
    )(got, got_columns, rows, up_x, up_y, inner, top, own, *gets, partial)


def solution(mesh):
    sizes = tuple(mesh.shape[axis] for axis in ("gx", "gy", "gz"))
    return jax.shard_map(
        functools.partial(on_device, sizes),
        mesh=mesh,
        in_specs=(P("gz", "gx", "gy"),),
        out_specs=(P("gz", "gx", "gy"), P("gz", "gx", "gy")),
        check_vma=False,
    )
```

```python
import functools

import jax
import jax.numpy as jnp
import numpy as np
from jax import lax
from jax.experimental import pallas as pl
from jax.experimental.pallas import tpu as pltpu
from jax.sharding import PartitionSpec as P

RATIO = 2.0 - np.sqrt(3.0)
VMEM_LIMIT = 48 * 1024 * 1024


def inverse_mass(i, j, n):
    low, high = np.minimum(i, j), np.maximum(i, j)
    sign = np.where((high - low) % 2 == 0, 1.0, -1.0)
    value = RATIO ** (high - low + 1.0) * (1.0 - RATIO ** (2.0 * (low + 1))) * (1.0 - RATIO ** (2.0 * (n - high)))
    return 3.0 * sign * value / ((1.0 - RATIO**2) * (1.0 - RATIO ** (2.0 * (n + 1))))


def line_operator(i, k, n):
    a = k // 2
    odd = k % 2 == 1

    def at(j):
        inside = (j >= 0) & (j < n)
        return np.where(inside, inverse_mass(i, np.clip(j, 0, n - 1), n), 0.0)

    even_part = np.where(a == 0, 9.0, 10.0) * at(a) + at(a - 1) + at(a + 1)
    odd_part = 6.0 * at(a) + 6.0 * at(a + 1)
    return np.where(odd, odd_part, even_part) / 12.0


def line_tables(parts, m):
    n = parts * m
    node, fine = np.arange(m), np.arange(2 * m)
    block = np.zeros((parts, m, 2 * m))
    to_right, to_left = np.zeros((parts, 2 * m)), np.zeros((parts, 2 * m))
    from_left, from_right = np.zeros((parts, m)), np.zeros((parts, m))
    weight_left, weight_right = np.zeros((parts, parts)), np.zeros((parts, parts))
    first = np.zeros((parts, m))
    first_right = np.zeros((parts,))
    for p in range(parts):
        k = p * 2 * m + fine
        block[p] = line_operator((p * m + node)[:, None], k[None, :], n)
        if p + 1 < parts:
            to_right[p] = line_operator(np.full_like(k, (p + 1) * m), k, n)
        if p > 0:
            to_left[p] = line_operator(np.full_like(k, p * m - 1), k, n)
        from_left[p] = (-RATIO) ** node * (1 - RATIO ** (2.0 * (n - p * m - node))) / (1 - RATIO ** (2.0 * (n - p * m)))
        from_right[p] = (
            (-RATIO) ** (m - 1 - node) * (1 - RATIO ** (2.0 * (p * m + node + 1))) / (1 - RATIO ** (2.0 * (p + 1) * m))
        )
        for q in range(parts):
            if q < p:
                weight_left[p, q] = (
                    (-RATIO) ** ((p - q - 1) * m)
                    * (1 - RATIO ** (2.0 * (n - p * m)))
                    / (1 - RATIO ** (2.0 * (n - (q + 1) * m)))
                )
            if q > p:
                weight_right[p, q] = (
                    (-RATIO) ** ((q - p - 1) * m) * (1 - RATIO ** (2.0 * (p + 1) * m)) / (1 - RATIO ** (2.0 * q * m))
                )
    first[0] = inverse_mass(node, np.zeros_like(node), n) / 3.0
    if parts > 1:
        first_right[0] = -inverse_mass(np.array(m), np.array(0), n) / 3.0
    return {
        "block": block,
        "to_right": to_right,
        "to_left": to_left,
        "from_left": from_left,
        "from_right": from_right,
        "weight_left": weight_left,
        "weight_right": weight_right,
        "first": first,
        "first_right": first_right,
    }


def even_selector(m):
    pick = np.zeros((2 * m, m))
    pick[2 * np.arange(m), np.arange(m)] = 1.0
    return pick


def f32(values):
    return np.asarray(values, np.float32)


def combine_tables(sizes, tx, ty, tz, mz):
    gx, gy, gz = sizes
    count = gx * gy * gz
    sender = np.arange(count)
    qx, qy, qz = (sender // gy) % gx, sender % gy, sender // (gx * gy)
    rows = 32
    wx, wy, wz = (np.zeros((parts, rows, count, 4)) for parts in sizes)

    def side(t, p, q, which):
        if which == 0:
            return (q == p) * 1.0
        return (t["weight_left"] if which == 1 else t["weight_right"])[p][q]

    for sx in range(3):
        for sy in range(3):
            if sx == 0 and sy == 0:
                continue
            for z in range(mz):
                row = (sx * 3 + sy) * mz + z
                for p in range(gx):
                    wx[p, row] = side(tx, p, qx, sx)[:, None]
                for p in range(gy):
                    wy[p, row] = side(ty, p, qy, sy)[:, None]
                for p in range(gz):
                    wz[p, row, :, z] += qz == p
                    wz[p, row, :, 0] += tz["weight_left"][p][qz] * tz["from_left"][p, z]
                    wz[p, row, :, 0] += tz["weight_right"][p][qz] * tz["from_right"][p, z]
    for case, (ox, oy) in enumerate(((1, 0), (0, 1), (1, 1))):
        for layer in range(mz + 1):
            row = 9 * mz + case * (mz + 1) + layer
            for p in range(gx):
                wx[p, row] = (qx == p + ox)[:, None]
            for p in range(gy):
                wy[p, row] = (qy == p + oy)[:, None]
            for p in range(gz):
                if layer < mz:
                    wz[p, row, :, mz + layer] = qz == p
                else:
                    wz[p, row, :, mz] = qz == p + 1
    return tuple(f32(w.reshape(w.shape[0], rows, count * 4)) for w in (wx, wy, wz))


def split(values):
    high = values.astype(jnp.bfloat16)
    return high, (values - high.astype(jnp.float32)).astype(jnp.bfloat16)


def one_pass(a, b, contract=((1,), (0,))):
    return lax.dot_general(a, b, (contract, ((), ())), preferred_element_type=jnp.float32)


def three_pass(a, b, contract=((1,), (0,))):
    return one_pass(a[0], b[0], contract) + one_pass(a[0], b[1], contract) + one_pass(a[1], b[0], contract)


def two_pass(a, b):
    return one_pass(a[0], b) + one_pass(a[1], b)


def exact_left(a, b):
    high, low = split(b)
    return one_pass(a, high) + one_pass(a, low)


def exact_right(a, b):
    high, low = split(a)
    return one_pass(high, b) + one_pass(low, b)


def start_all(copies):
    for copy in copies:
        copy.start()


def local_kernel(sizes, *refs):
    field, fold_z, line_y, line_x = refs[:4]
    send, own, even, near, far, first, f = refs[4:11]
    ry, bx, az, picked, column, kinds, sem = refs[11:]
    gx, gy, gz = sizes
    px, py, pz = lax.axis_index("gx"), lax.axis_index("gy"), lax.axis_index("gz")
    depth, height, breadth = field.shape
    mz, mx, my = own.shape
    planes = [pltpu.make_async_copy(field.at[z], f.at[z], sem.at[z]) for z in range(depth)]
    sources = [(fold_z.at[pz], az), (line_y.at[py], ry), (line_x.at[px], bx)]
    tables = [pltpu.make_async_copy(src, dst, sem.at[depth + i]) for i, (src, dst) in enumerate(sources)]
    start_all(tables[:2] + planes + tables[2:])
    kinds[...] = jnp.zeros_like(kinds)
    fine = lax.broadcasted_iota(jnp.int32, (breadth, my), 0)
    node = lax.broadcasted_iota(jnp.int32, (breadth, my), 1)
    pick_y = jnp.where(fine == 2 * node, 1.0, 0.0).astype(jnp.bfloat16)
    tables[0].wait()
    tables[1].wait()
    weights = split(ry[:breadth])
    by_y, evens, along_x = [], [], None
    step = 2
    for start in range(0, depth, step):
        for z in range(start, start + step):
            planes[z].wait()
        part = split(f[start : start + step].reshape(step * height, breadth))
        result = three_pass(part, weights)
        for z in range(start, start + step):
            rows = slice((z - start) * height, (z - start + 1) * height)
            by_y.append(result[rows, :my])
            folded = result[rows, my:] * az[z : z + 1, :]
            along_x = folded if along_x is None else along_x + folded
            if z % 2 == 0:
                j = z // 2
                picked[j] = two_pass((part[0][rows], part[1][rows]), pick_y)
                evens.append(picked[j, pl.ds(0, mx, stride=2), :])
                even[j] = evens[j]
    column[...] = along_x
    edge = jnp.transpose(column[pl.ds(0, mx, stride=2), :])[:16, :]
    for table in tables[2:]:
        table.wait()
    solve_x = split(bx[: mx + 8])
    faces = three_pass(solve_x, split(along_x))
    by_x = jnp.transpose(faces[:mx])[:16, :]
    corners = [faces[mx + ab : mx + ab + 1] for ab in range(2)]
    by_split = split(jnp.concatenate(by_y, axis=1))
    ends_x = three_pass(tuple(half[mx:] for half in solve_x), by_split)
    sums = [[ends_x[ab : ab + 1, z * my : (z + 1) * my] for ab in range(2)] for z in range(depth)]

    first_y, kappa_y = ry[breadth : breadth + 1, :my], ry[breadth + 1 : breadth + 2, :my]
    first_x, kappa_x = bx[mx + 8 : mx + 9, :mx], bx[mx + 9 : mx + 10, :mx]
    outs = mz + 2
    first_rows = jnp.concatenate([evens[j][0:1, :] for j in range(mz)], axis=0)
    first_cols = edge[2 * outs : 2 * outs + mz, :]

    def over_z(base, rows):
        return sum(az[base + 8 * j : base + 8 * j + 8, :] * rows[j] for j in range(len(rows)))

    first_row = over_z(8 + 8 * depth, [first_rows[j : j + 1] for j in range(mz)])
    first_col = over_z(8 + 8 * depth, [first_cols[j : j + 1] for j in range(mz)])
    corner = first_row[:, 0:1]
    lane = lax.broadcasted_iota(jnp.int32, (8, my), 1)
    here = lane == lax.broadcasted_iota(jnp.int32, (8, my), 0)
    ends = [jnp.sum(jnp.where(here, corners[ab], 0.0), axis=1, keepdims=True) for ab in range(2)]
    spread = jnp.zeros((outs, my), jnp.float32)
    chunks = {
        (1, 0): over_z(8, [sums[z][0] for z in range(depth)]) - kappa_x * (first_row - first_y * corner),
        (2, 0): over_z(8, [sums[z][1] for z in range(depth)]),
        (0, 1): by_x[:outs] - (kappa_y * (first_col - first_x * corner))[:outs],
        (0, 2): by_x[outs : 2 * outs],
        (1, 1): spread + ends[0][:outs] - kappa_x * kappa_y * corner[:outs],
        (1, 2): spread + ends[0][outs : 2 * outs],
        (2, 1): spread + ends[1][:outs],
        (2, 2): spread + ends[1][outs : 2 * outs],
    }
    for (sx, sy), rows in chunks.items():
        kind = (sx * 3 + sy) * 3
        kinds[kind, 0:mz, :] = rows[:mz]
        kinds[kind + 1, 0:1, :] = rows[mz : mz + 1]
        kinds[kind + 2, 0:1, :] = rows[mz + 1 : mz + 2]
    for sx in range(3):
        for sy in range(3):
            for sz in range(3):
                kinds[(sx * 3 + sy) * 3 + sz, mz : 2 * mz, :] = first_cols if sx == 0 else first_rows

    def side(there, here):
        return jnp.where(there == here, 0, jnp.where(there > here, 1, 2))

    def scatter(tx, ty, tz, at):
        send[pl.ds(at, 1)] = kinds[pl.ds((side(tx, px) * 3 + side(ty, py)) * 3 + side(tz, pz), 1)]

    if gx * gy * gz <= 32:
        for at in range(gx * gy * gz):
            scatter((at // gy) % gx, at % gy, at // (gx * gy), at)
    else:

        @pl.loop(0, gx * gy * gz)
        def _(at):
            scatter((at // gy) % gx, at % gy, at // (gx * gy), at)

    by_all = three_pass(tuple(half[:mx] for half in solve_x), by_split)
    solved = [by_all[:, z * my : (z + 1) * my] for z in range(depth)]
    first_x = jnp.transpose(jnp.broadcast_to(first_x, (8, mx)))[:, 0:1]
    outs = []
    for out in range(mz + 2):
        value = sum(az[8 + 8 * z + out : 9 + 8 * z + out, :] * solved[z] for z in range(depth))
        base = 8 + 8 * depth + out
        part = sum(az[base + 8 * j : base + 8 * j + 1, :] * evens[j] for j in range(mz))
        part = part - first_x * part[0:1, :]
        part = part - part[:, 0:1] * first_y
        outs.append(value - part)
    for j in range(mz):
        own[j] = evens[j] + outs[j]
    near[...] = jnp.where(pz % 2 == 0, outs[mz], outs[mz + 1])
    far[...] = jnp.where(pz % 4 < 2, outs[mz], outs[mz + 1])
    first[...] = evens[0]


def inner_kernel(field, even, *refs):
    tables, (parts, sem) = refs[:6], refs[14:]
    coefficients, c, top, rows, weights, columns, up_x, up_y = refs[6:14]
    px, py, pz = lax.axis_index("gx"), lax.axis_index("gy"), lax.axis_index("gz")
    depth, height, breadth = field.shape
    mz = even.shape[0]
    goals = (rows.at[0:8], rows.at[8:16], rows.at[16:32], parts.at[0], parts.at[1], parts.at[2])
    fetches = [
        pltpu.make_async_copy(table.at[at], goal, sem.at[depth + i])
        for i, (table, at, goal) in enumerate(zip(tables, (px, py, pz) * 2, goals, strict=True))
    ]
    start_all(fetches)
    for up, node_axis in ((up_x, 1), (up_y, 0)):
        node = lax.broadcasted_iota(jnp.int32, up.shape, node_axis)
        away = jnp.abs(lax.broadcasted_iota(jnp.int32, up.shape, 1 - node_axis) - 2 * node)
        up[...] = jnp.where(away == 0, 1.0, jnp.where(away == 1, 0.5, 0.0))
    body = (pl.ds(0, height - 8), pl.ds(0, breadth - 128))
    up_left, up_right = up_x[...].astype(jnp.bfloat16), up_y[...].astype(jnp.bfloat16)
    lifted = [exact_right(exact_left(up_left, even[j]), up_right) for j in range(mz)]
    copies = []
    for z in range(depth - 1):
        j = z // 2
        c[z] = field[z] - (lifted[j] if z % 2 == 0 else 0.5 * (lifted[j] + lifted[j + 1]))
        copies.append(pltpu.make_async_copy(c.at[z, *body], coefficients.at[z, *body], sem.at[z]))
        copies[z].start()
    top[...] = field[depth - 1] - 0.5 * lifted[mz - 1]
    for copy in fetches:
        copy.wait()
    weights[...] = parts[0] * parts[1] * parts[2]
    blank = jnp.zeros((columns.shape[1] - weights.shape[0], weights.shape[1]), jnp.float32)
    columns[...] = jnp.transpose(jnp.concatenate([weights[...], blank], axis=0))
    for copy in copies:
        copy.wait()


def gather_kernel(received, weights, columns, got, got_columns):
    chunks = split(received[...])
    got_columns[...] = three_pass(chunks, split(columns[...]), ((0,), (0,)))
    got[...] = three_pass(split(weights[...]), chunks)


def finish_kernel(*refs):
    got, got_columns, rows, up_x, up_y, inner, top, own, one, two, three, first, first_far, partial = refs[:14]
    coefficients, coarse, last_plane, rim, foot, values, sem = refs[14:]
    del partial
    mz, mx, my = own.shape
    depth, height, breadth = 2 * mz, 2 * mx, 2 * my
    split_at = breadth - 128
    body = (pl.ds(0, height - 8), pl.ds(0, split_at))

    def row_at(i):
        return rows[16 + i : 17 + i, :]

    planes = (one[...], two[...], three[...])
    left = sum(row_at(i) * plane for i, plane in enumerate(planes))
    right = sum(row_at(3 + i) * plane for i, plane in enumerate(planes))
    ahead = row_at(6) * first[...] + row_at(7) * first_far[...]
    up_left, up_right = up_x[...].astype(jnp.bfloat16), up_y[...].astype(jnp.bfloat16)
    last_plane[...] = top[...] - 0.5 * exact_right(exact_left(up_left, ahead), up_right)
    copies = [pltpu.make_async_copy(last_plane.at[body], coefficients.at[depth - 1, *body], sem.at[0])]
    copies[0].start()
    before = [own[j] + row_at(8 + j) * left + row_at(8 + mz + j) * right for j in range(mz)]

    base = 9 * mz
    layers = mz + 1
    halo_x, halo_xy = got[base : base + layers], got[base + 2 * layers : base + 3 * layers]
    pad = jnp.zeros((8 - layers, halo_x.shape[1]), jnp.float32)
    row = exact_right(jnp.concatenate([halo_x, pad], axis=0), up_right)
    col = exact_left(up_left, got_columns[...])[:, base + layers : base + 2 * layers]
    lane = lax.broadcasted_iota(jnp.int32, (1, 128), 1)
    last = lane == 127
    for z in range(depth):
        j = z // 2
        if z % 2 == 0:
            r, s, k = row[j : j + 1], 0.5 * col[:, j : j + 1], halo_xy[j : j + 1, 0:1]
        else:
            r = 0.5 * (row[j : j + 1] + row[j + 1 : j + 2])
            s = 0.25 * (col[:, j : j + 1] + col[:, j + 1 : j + 2])
            k = 0.5 * (halo_xy[j : j + 1, 0:1] + halo_xy[j + 1 : j + 2, 0:1])
        old = inner[z] if z < depth - 1 else last_plane[...]
        rim[z] = old[:, split_at:] - jnp.where(last, s, 0.0)
        end = 0.5 * r[:, split_at:] + jnp.where(last, 0.25 * k, 0.0)
        rim[z, height - 1 : height, :] = rim[z, height - 1 : height, :] - end
        foot[z] = old[height - 8 :, :split_at]
        foot[z, 7:8, :] = old[height - 1 :, :split_at] - 0.5 * r[:, :split_at]
        goal = coefficients.at[z, :, pl.ds(split_at, 128)]
        copies.append(pltpu.make_async_copy(rim.at[z], goal, sem.at[3 + 2 * z]))
        goal = coefficients.at[z, pl.ds(height - 8, 8), pl.ds(0, split_at)]
        copies.append(pltpu.make_async_copy(foot.at[z], goal, sem.at[4 + 2 * z]))
        start_all(copies[-2:])

    ux, vx, uy, vy = rows[0:1], rows[1:2], rows[8:9], rows[9:10]

    def part(sx, sy, z):
        at = (sx * 3 + sy) * mz + z
        return got[at : at + 1]

    for z in range(mz):
        a, b = [], []
        for sy, end in ((1, uy), (2, vy)):
            a.append(part(0, sy, z) + ux * part(1, sy, z)[:, 0:1] + vx * part(2, sy, z)[:, 0:1])
            b.append(end)
        for sx, end in ((1, ux), (2, vx)):
            a.append(end)
            b.append(part(sx, 0, z))
        zero = [jnp.zeros((4, mx), jnp.float32)]
        a, b = split(jnp.concatenate(a + zero, axis=0)), split(jnp.concatenate(b + zero, axis=0))
        values[z] = before[z] + three_pass(a, b, ((0,), (0,)))
    copies.append(pltpu.make_async_copy(values, coarse, sem.at[2]))
    copies[-1].start()
    for copy in copies:
        copy.wait()


def call(kernel, name, out_shape, in_specs, out_specs, scratch=(), aliases=None, flops=1, size=1):
    return pl.pallas_call(
        kernel,
        out_shape=out_shape,
        in_specs=in_specs,
        out_specs=out_specs,
        scratch_shapes=list(scratch),
        input_output_aliases=aliases or {},
        compiler_params=pltpu.CompilerParams(vmem_limit_bytes=VMEM_LIMIT),
        cost_estimate=pl.CostEstimate(flops=flops, bytes_accessed=size, transcendentals=0),
        name=name,
    )


ANY = pl.BlockSpec(memory_space=pl.ANY)
HBM = pl.BlockSpec(memory_space=pltpu.HBM)
SMEM = pl.BlockSpec(memory_space=pltpu.SMEM)
VMEM = pl.BlockSpec(memory_space=pltpu.VMEM)


def in_hbm(values):
    return pltpu.with_memory_space_constraint(jnp.asarray(values), pltpu.HBM)


def shape(*dims):
    return jax.ShapeDtypeStruct(dims, jnp.float32)


def on_device(sizes, field):
    gx, gy, gz = sizes
    depth, height, breadth = field.shape
    mz, mx, my = depth // 2, height // 2, breadth // 2
    count = gx * gy * gz
    axes = ("gz", "gx", "gy")
    tx, ty, tz = line_tables(gx, mx), line_tables(gy, my), line_tables(gz, mz)

    def vectors(t, parts, m):
        table = np.zeros((parts, 8, m))
        table[:, 0], table[:, 1] = t["from_left"], t["from_right"]
        return f32(table)

    row_x, row_y = vectors(tx, gx, mx), vectors(ty, gy, my)
    line_y, line_x = np.zeros((gy, breadth + 8, 2 * my)), np.zeros((gx, mx + 16, height))
    line_y[:, :breadth, :my] = ty["block"].transpose(0, 2, 1)
    outs = mz + 2
    line_y[:, :breadth, my : my + outs] = ty["to_right"][..., None]
    line_y[:, :breadth, my + outs : my + 2 * outs] = ty["to_left"][..., None]
    line_y[:, 0, my + 2 * (mz + 2) : my + 2 * (mz + 2) + mz] = 1.0
    line_y[:, breadth, :my], line_y[:, breadth + 1, :my] = ty["first"], ty["first_right"][:, None]
    line_x[:, :mx], line_x[:, mx], line_x[:, mx + 1] = tx["block"], tx["to_right"], tx["to_left"]
    line_x[:, mx + 8, :mx], line_x[:, mx + 9, :mx] = tx["first"], tx["first_right"][:, None]

    fold_z = np.zeros((gz, 8 + 8 * (depth + mz), my))
    for p in range(gz):
        full = np.concatenate([tz["block"][p], tz["to_right"][p : p + 1], tz["to_left"][p : p + 1]], axis=0)
        nodes = np.zeros((outs, mz))
        nodes[:mz] = np.eye(mz)
        nodes[:mz, 0] -= tz["first"][p]
        nodes[mz, 0] = tz["first_right"][p]
        fold_z[p, :depth, : 2 * outs] = np.tile(full.T, 2)
        for j in range(mz):
            fold_z[p, 2 * j, 2 * outs + j] = 1.0
        for z in range(depth):
            fold_z[p, 8 + 8 * z : 8 + 8 * z + outs] = full[:, z : z + 1]
        for j in range(mz):
            base = 8 + 8 * (depth + j)
            fold_z[p, base : base + outs] = nodes[:, j : j + 1]

    vmem = pltpu.VMEM
    operands = (field, f32(fold_z), f32(line_y), f32(line_x))
    send, own, even, near, far, first, kept = call(
        functools.partial(local_kernel, sizes),
        "local",
        [shape(count, 4, my), shape(mz, mx, my), shape(mz, mx, my)] + [shape(mx, my)] * 3 + [shape(*field.shape)],
        [HBM] * 4,
        [VMEM] * 7,
        [
            vmem(line_y.shape[1:], jnp.float32),
            vmem(line_x.shape[1:], jnp.float32),
            vmem(fold_z.shape[1:], jnp.float32),
            vmem((mz, height, my), jnp.float32),
            vmem((height, 128), jnp.float32),
            vmem((27, 4, my), jnp.float32),
            pltpu.SemaphoreType.DMA((depth + 3,)),
        ],
    )(*map(in_hbm, operands))
    received = lax.all_to_all(send, axes, 0, 0, tiled=True).reshape(count * 4, my)

    assert gz == 4

    def exchange(plane, hop):
        return lax.ppermute(plane, "gz", [(i, i ^ hop) for i in range(gz)])

    from_far = exchange(far, 3)
    gets = (exchange(near, 1), exchange(from_far, 1), from_far, exchange(first, 1), exchange(first, 3))

    row_z = np.zeros((gz, 16, my))
    for p in range(gz):
        for i, hop in enumerate((1, 2, 3)):
            row_z[p, i], row_z[p, 3 + i] = tz["weight_left"][p, p ^ hop], tz["weight_right"][p, p ^ hop]
        row_z[p, 6], row_z[p, 7] = p ^ 1 == p + 1, p ^ 3 == p + 1
        row_z[p, 8 : 8 + mz] = tz["from_left"][p][:, None]
        row_z[p, 8 + mz : 8 + 2 * mz] = tz["from_right"][p][:, None]
    wx, wy, wz = combine_tables(sizes, tx, ty, tz, mz)
    tables = (row_x, row_y, f32(row_z), wx, wy, wz)
    partial, inner, top, rows, weights, columns, up_x, up_y = call(
        inner_kernel,
        "inner",
        [shape(*field.shape), shape(depth - 1, height, breadth), shape(height, breadth), shape(32, my)]
        + [shape(*wx.shape[1:]), shape(count * 4, 128), shape(height, mx), shape(my, breadth)],
        [VMEM] * 2 + [HBM] * len(tables),
        [HBM] + [VMEM] * 7,
        [vmem((3, *wx.shape[1:]), jnp.float32), pltpu.SemaphoreType.DMA((depth + len(tables),))],
    )(kept, even, *map(in_hbm, tables))
    got, got_columns = call(
        gather_kernel,
        "gather",
        [shape(wx.shape[1], my), shape(mx, 128)],
        [VMEM] * 3,
        [VMEM] * 2,
        flops=10**10,
        size=10**8,
    )(received, weights, columns)
    return call(
        finish_kernel,
        "finish",
        [shape(*field.shape), shape(mz, mx, my)],
        [VMEM] * 13 + [HBM],
        [HBM, HBM],
        [
            vmem((height, breadth), jnp.float32),
            vmem((depth, height, 128), jnp.float32),
            vmem((depth, 8, breadth - 128), jnp.float32),
            vmem((mz, mx, my), jnp.float32),
            pltpu.SemaphoreType.DMA((3 + 2 * depth,)),
        ],
        {13: 0},
    )(got, got_columns, rows, up_x, up_y, inner, top, own, *gets, partial)


def solution(mesh):
    sizes = tuple(mesh.shape[axis] for axis in ("gx", "gy", "gz"))
    return jax.shard_map(
        functools.partial(on_device, sizes),
        mesh=mesh,
        in_specs=(P("gz", "gx", "gy"),),
        out_specs=(P("gz", "gx", "gy"), P("gz", "gx", "gy")),
        check_vma=False,
    )
```
